128 devices in a mesh: dp: 8 (over z, core), seq: 16 (over y, x).
Axes of the slice: x: 4, y: 4, z: 4, core: 2. Of those that a mesh axis runs over, the one named last changes fastest.
Arguments:
- tokens: bfloat16 [8192, 3584], P(('dp', 'seq')), may hold values from -6 to 6
- gain: float32 [3584], replicated, may hold values from 0.25 to 1.75
- q_weight: bfloat16 [3584, 2048], P(('dp', 'seq')), may hold values from -0.09375 to 0.09375
- key_value_weight: bfloat16 [3584, 768], P(('dp', 'seq')), may hold values from -0.09375 to 0.09375
- q_bias: float32 [2048], replicated, may hold values from -8 to 8
- kv_bias: float32 [768], replicated, may hold values from -8 to 8
- plan: int32 [8, 16], replicated, may hold values from 0 to 7, as said below
- home_offsets: int32 [8, 16], replicated, may hold values from 0 to 15, as said below
Outputs:
- attended: bfloat16 [8192, 2048], P(('dp', 'seq'))
- kv_cache: bfloat16 [8, 16, 512, 768], P('dp', 'seq')
The draws below stay inside these ranges and needn't reach their ends.
Inputs may be any that keep to these rules, and one draw needn't show every extreme that they name: `plan`: all stretches of a home row have one group; no group gets more than two home rows, and some group gets two. `home_offsets`: each home row holds one or two sequences of consecutive stretches; the value is the column where the stretch's sequence begins.
All inputs are finite; a program needn't handle non-finite values.
Results may differ from the reference program's by a relative error of at most 0.0096.
Values may be sent and summed in bfloat16 or wider, within the bound.
No kernel may reach another device: no remote copies, remote signals or barrier semaphores. Data moves between devices by JAX's collectives and lax.ppermute only.
A program may use at most 128 MiB of HBM per device.

```python
import jax
import jax.numpy as jnp
from jax import lax

MODEL_WIDTH = 3584
HEAD_SIZE = 128
HQ = 16
GROUP = 7
TOK_DEV = 64
HOME_STRETCHES = 16
KEY_VALUE_HEADS = 3
TOKENS = 8192
N_DP = 8
N_SEQ = 16


def layout(key):
    cut_key, use_key, long_key, perm_key, pick_key = jax.random.split(jax.random.fold_in(key, 5), 5)
    column = jnp.arange(N_SEQ, dtype=jnp.int32)
    row_ids = jnp.arange(N_DP, dtype=jnp.int32)
    cut_at = jax.random.randint(cut_key, (N_DP,), 1, N_SEQ).astype(jnp.int32)
    use_cut = jax.random.randint(use_key, (N_DP,), 0, 2) == 1
    long_row = jax.random.randint(long_key, (), 0, N_DP)
    cut_at = jnp.where(row_ids == long_row, N_SEQ - 1, cut_at)
    use_cut = use_cut | (row_ids == long_row)
    first = jnp.where(use_cut[:, None] & (column[None, :] >= cut_at[:, None]), cut_at[:, None], 0)
    orders = jax.random.permutation(perm_key, N_DP).astype(jnp.int32)
    picks = jax.random.randint(pick_key, (2,), 0, 1 << 20)
    loser = 1 + picks[0] % (N_DP - 2)
    gainer = (loser + 1 + picks[1] % (N_DP - 1)) % N_DP
    row_lost = jnp.argmax((orders == loser).astype(jnp.int32))
    groups = jnp.where(row_ids == row_lost, gainer, orders)
    plan = jnp.broadcast_to(groups[:, None], (N_DP, N_SEQ))
    return (plan.astype(jnp.int32), first.astype(jnp.int32))


def draw_plan(key, part):
    shared = layout(key)
    return shared[0]


def draw_home_offsets(key, part):
    shared = layout(key)
    return shared[1]


def draw_q_bias(key, part):
    key = jax.random.fold_in(key, 21)
    return jnp.clip(0.5 * jax.random.normal(key, (HQ * HEAD_SIZE,), jnp.float32), -8.0, 8.0)


def draw_kv_bias(key, part):
    key = jax.random.fold_in(key, 22)
    return jnp.clip(0.5 * jax.random.normal(key, (2 * KEY_VALUE_HEADS * HEAD_SIZE,), jnp.float32), -8.0, 8.0)


def steps_of(stream_key, extent, pieces, low, largest):
    def one(dim, shards_of):
        steps = jax.random.uniform(jax.random.fold_in(jax.random.fold_in(stream_key, 6), dim), (shards_of,), jnp.float32, low / len(pieces), largest / len(pieces))
        return jnp.repeat(jnp.exp(steps), extent[dim] // shards_of).reshape((-1,) + (1,) * (len(extent) - dim - 1))

    loudness = one(*pieces[0])
    for cut in pieces[1:]:
        loudness = loudness * one(*cut)
    return loudness


def normal_values(own_key, shape, scale, bound, cuts=(), kind=jnp.bfloat16):
    result = jax.random.normal(own_key, shape, jnp.float32) * scale
    if len(cuts) > 0:
        result = steps_of(own_key, shape, cuts, -0.22, 0.18) * result
    return jnp.clip(result, min=-bound, max=bound).astype(kind)


def setup_inputs(seed: int = 0) -> dict:
    key_list = jax.random.split(jax.random.key(seed), 9)
    tokens = normal_values(key_list[0], (TOKENS, MODEL_WIDTH), 1.0, 6.0, ((0, 128),))
    gain = jnp.clip(1.0 + 0.15 * jax.random.normal(key_list[1], (MODEL_WIDTH,), jnp.float32), 0.25, 1.75)
    q_weight = normal_values(key_list[2], (MODEL_WIDTH, HQ * HEAD_SIZE), MODEL_WIDTH ** -0.5, 0.09375, ((0, 128),))
    key_value_weight = normal_values(key_list[3], (MODEL_WIDTH, 2 * KEY_VALUE_HEADS * HEAD_SIZE), MODEL_WIDTH ** -0.5, 0.09375, ((0, 128),))
    q_bias = draw_q_bias(jax.random.fold_in(key_list[8], 71), 0)
    kv_bias = draw_kv_bias(jax.random.fold_in(key_list[8], 71), 0)
    plan = draw_plan(jax.random.fold_in(key_list[8], 71), 0)
    home_offsets = draw_home_offsets(jax.random.fold_in(key_list[8], 71), 0)
    return dict(tokens=tokens, gain=gain, q_weight=q_weight, key_value_weight=key_value_weight, q_bias=q_bias, kv_bias=kv_bias, plan=plan, home_offsets=home_offsets)


def apply_rotation(value_rows, positions):
    half = value_rows.shape[-1] // 2
    freqs = 1000000.0 ** (-(jnp.arange(half, dtype=jnp.float32) * 2.0 / value_rows.shape[-1]))
    angles = positions.astype(jnp.float32)[:, None] * freqs[None, :]
    cosine = jnp.cos(angles)[:, None, :]
    sine = jnp.sin(angles)[:, None, :]
    first_half = value_rows[..., :half]
    second_half = value_rows[..., half:]
    return jnp.concatenate([first_half * cosine - second_half * sine, second_half * cosine + first_half * sine], axis=-1)

def slot_rank(plan):
    order = jnp.arange(plan.shape[1], dtype=jnp.int32)
    same = plan[:, :, None] == plan[:, None, :]
    earlier = order[None, None, :] < order[None, :, None]
    return lax.optimization_barrier(jnp.sum(jnp.where(same & earlier, 1, 0), axis=2)).astype(jnp.int32)

def reference(tokens, gain, q_weight, key_value_weight, q_bias, kv_bias, plan, home_offsets):
    running_total = tokens.shape[0]
    floats = tokens.astype(jnp.float32)
    normed = (floats * lax.rsqrt(lax.optimization_barrier(jnp.mean(floats * floats, axis=1, keepdims=True)) + 1e-06) * gain[None, :]).astype(jnp.bfloat16)
    query = jnp.dot(normed, q_weight, preferred_element_type=jnp.float32) + q_bias[None, :]
    key_value_pair = jnp.dot(normed, key_value_weight, preferred_element_type=jnp.float32) + kv_bias[None, :]
    index = jnp.arange(running_total, dtype=jnp.int32)
    stretch = index // TOK_DEV
    row_of = stretch // N_SEQ
    col_of = stretch % N_SEQ
    first = home_offsets[row_of, col_of]
    token_position = (col_of - first) * TOK_DEV + index % TOK_DEV
    ident = row_of * N_SEQ + first
    q_rot = apply_rotation(query.reshape(running_total, HQ, HEAD_SIZE), token_position).astype(jnp.bfloat16)
    key_rotated = apply_rotation(key_value_pair[:, :KEY_VALUE_HEADS * HEAD_SIZE].reshape(running_total, KEY_VALUE_HEADS, HEAD_SIZE), token_position).astype(jnp.bfloat16)
    value_rows = key_value_pair[:, KEY_VALUE_HEADS * HEAD_SIZE:].astype(jnp.bfloat16).reshape(running_total, KEY_VALUE_HEADS, HEAD_SIZE)
    span = N_SEQ * TOK_DEV
    scale = HEAD_SIZE ** (-0.5)

    def one_row(row):
        start = row * span
        q_row = lax.dynamic_slice_in_dim(q_rot, start, span, 0)
        k_row = lax.dynamic_slice_in_dim(key_rotated, start, span, 0)
        v_row = lax.dynamic_slice_in_dim(value_rows, start, span, 0)
        p_row = lax.dynamic_slice_in_dim(token_position, start, span, 0)
        i_row = lax.dynamic_slice_in_dim(ident, start, span, 0)
        allowed = (i_row[:, None] == i_row[None, :]) & (p_row[None, :] <= p_row[:, None])

        def one_head(head):
            q_head = lax.dynamic_index_in_dim(q_row, head, 1, keepdims=False)
            k_head = lax.dynamic_index_in_dim(k_row, head // GROUP, 1, keepdims=False)
            v_head = lax.dynamic_index_in_dim(v_row, head // GROUP, 1, keepdims=False)
            scores = jnp.dot(q_head, k_head.T, preferred_element_type=jnp.float32) * scale
            scores = jnp.where(allowed, scores, -1e+30)
            top = lax.optimization_barrier(jnp.max(scores, axis=1, keepdims=True))
            weights = jnp.where(allowed, jnp.exp(scores - top), 0.0)
            mass = lax.optimization_barrier(jnp.sum(weights, axis=1, keepdims=True))
            mixed = jnp.dot(weights.astype(jnp.bfloat16), v_head, preferred_element_type=jnp.float32) / mass
            return mixed.astype(jnp.bfloat16)
        heads = lax.map(one_head, jnp.arange(HQ, dtype=jnp.int32))
        return jnp.transpose(heads, (1, 0, 2)).reshape(span, HQ * HEAD_SIZE)
    attended = lax.map(one_row, jnp.arange(N_DP, dtype=jnp.int32)).reshape(running_total, HQ * HEAD_SIZE)
    rank = slot_rank(plan)
    group_ids = jnp.arange(N_DP, dtype=jnp.int32)
    slot_ids = jnp.arange(HOME_STRETCHES, dtype=jnp.int32)
    columns = jnp.arange(N_SEQ, dtype=jnp.int32)
    chosen = (plan[None, :, None, :] == group_ids[:, None, None, None]) & (rank[None, :, None, :] == slot_ids[None, None, :, None])
    hit = jnp.any(chosen, axis=3)
    home_col = lax.optimization_barrier(jnp.sum(jnp.where(chosen, columns[None, None, None, :], 0), axis=3)).astype(jnp.int32)
    sequence_piece = TOK_DEV // N_SEQ
    inner = jnp.arange(sequence_piece, dtype=jnp.int32)
    token_entry = (group_ids[None, None, :, None, None] * N_SEQ + home_col[:, None, :, :, None]) * TOK_DEV + inner[None, None, None, None, :] * N_SEQ + columns[None, :, None, None, None]
    cached_rows = jnp.concatenate([key_rotated.reshape(running_total, KEY_VALUE_HEADS * HEAD_SIZE), value_rows.reshape(running_total, KEY_VALUE_HEADS * HEAD_SIZE)], axis=1)
    cache_buffer = cached_rows[token_entry.reshape(-1)].reshape(N_DP, N_SEQ, N_DP, HOME_STRETCHES, sequence_piece, 2 * KEY_VALUE_HEADS * HEAD_SIZE)
    cache_buffer = jnp.where(hit[:, None, :, :, None, None], cache_buffer, jnp.zeros_like(cache_buffer))
    return (attended, cache_buffer.reshape(N_DP, N_SEQ, N_DP * HOME_STRETCHES * sequence_piece, 2 * KEY_VALUE_HEADS * HEAD_SIZE))
```

```python
import functools

import jax
import jax.numpy as jnp
import numpy as np
from jax import lax
from jax.experimental import pallas as pl
from jax.experimental.pallas import tpu as pltpu
from jax.sharding import Mesh
from jax.sharding import PartitionSpec as P

HEAD = 128
KV_SLOT = (0, 1, 1, 2)
NEG = -1e30
ROW_TOK = 256


def normalize(rows, gain):
    floats = rows.astype(jnp.float32)
    scaled = (
        floats * lax.rsqrt(jnp.mean(floats * floats, axis=1, keepdims=True) + 1e-06) * gain[None, :]
    )
    return scaled.astype(jnp.bfloat16)


def rotate(v, cos, sin):
    a = v[:, :64]
    b = v[:, 64:]
    return jnp.concatenate([a * cos - b * sin, b * cos + a * sin], axis=1)


def kv_kernel(info, n0, n1, n2a, n2b, n3, w, b, cos, sin, x_out, kv_out):
    x = info[0]

    def place(j):
        return pl.ds(pl.multiple_of(lax.rem(x + j, 4) * 64, 64), 64)

    x_out[place(0), :] = n0[...]
    x_out[place(1), :] = n1[...]
    x_out[place(2), :] = jnp.concatenate([n2a[...], n2b[...]], axis=0)
    x_out[place(3), :] = n3[...]
    acc = jnp.dot(x_out[...], w[...], preferred_element_type=jnp.float32) + b[...]
    k = rotate(acc[:, :HEAD], cos[...], sin[...])
    kv_out[:, :HEAD] = k.astype(jnp.bfloat16)
    kv_out[:, HEAD:] = acc[:, HEAD:].astype(jnp.bfloat16)


def q_kernel(x_in, w, b, cos, sin, q_out):
    acc = jnp.dot(x_in[...], w[...], preferred_element_type=jnp.float32) + b[...]
    for h in range(2):
        q = rotate(acc[:, h * HEAD : (h + 1) * HEAD], cos[...], sin[...])
        q_out[:, h * HEAD : (h + 1) * HEAD] = q.astype(jnp.bfloat16)


def attend_kernel(info, q, a0, a1, a2, a3, b0, b1, b2, b3, out, mask):
    x = info[0]
    y = info[1]
    h = pl.program_id(0)

    @pl.when(h == 0)
    def _():
        qi = lax.broadcasted_iota(jnp.int32, (ROW_TOK, ROW_TOK), 0)
        ki = lax.broadcasted_iota(jnp.int32, (ROW_TOK, ROW_TOK), 1)
        start = jnp.where(
            qi < 128,
            jnp.where(qi < 64, info[2], info[3]),
            jnp.where(qi < 192, info[4], info[5]),
        )
        for j in range(4):
            key = ki + lax.rem(y + j, 4) * ROW_TOK
            ok = (key >= start) & (key <= qi + y * ROW_TOK)
            mask[:, j * ROW_TOK : (j + 1) * ROW_TOK] = jnp.where(ok, 0.0, NEG)

    use_b = ((x == 1) & (h < 3)) | ((x == 3) & (h < 2))
    pick = jnp.where(use_b, 1, 0)
    qh = q[...]
    parts = []
    vals = []
    for j, (pa, pb) in enumerate(((a0, b0), (a1, b1), (a2, b2), (a3, b3))):
        kv = jnp.where(pick == 1, pb[...], pa[...])
        s = lax.dot_general(
            qh, kv[:, :HEAD], (((1,), (1,)), ((), ())), preferred_element_type=jnp.float32
        )
        parts.append(s * (HEAD**-0.5) + mask[:, j * ROW_TOK : (j + 1) * ROW_TOK])
        vals.append(kv[:, HEAD:])
    top = functools.reduce(jnp.maximum, [jnp.max(s, axis=1, keepdims=True) for s in parts])
    mass = jnp.zeros((ROW_TOK, 1), jnp.float32)
    acc = jnp.zeros((ROW_TOK, HEAD), jnp.float32)
    for s, v in zip(parts, vals):
        p = jnp.exp(s - top)
        mass += jnp.sum(p, axis=1, keepdims=True)
        acc += jnp.dot(p.astype(jnp.bfloat16), v, preferred_element_type=jnp.float32)
    out[...] = (acc / mass).astype(jnp.bfloat16)


VM = pl.BlockSpec(memory_space=pltpu.VMEM)
SM = pl.BlockSpec(memory_space=pltpu.SMEM)
BIG = pltpu.CompilerParams(vmem_limit_bytes=48 * 1024 * 1024)


def yx_perm(dy, xmap):
    return [(y * 4 + x, ((y + dy) % 4) * 4 + xmap[x]) for y in range(4) for x in range(4)]


def per_device(tokens, gain, q_weight, key_value_weight, q_bias, kv_bias, plan, home_offsets):
    z = lax.axis_index("z")
    core = lax.axis_index("core")
    y = lax.axis_index("y")
    x = lax.axis_index("x")
    e = z * 2 + core
    bf = jnp.bfloat16

    wq = q_weight.reshape(28, 4, 512).transpose(1, 0, 2)
    wkv = jnp.stack(
        [
            jnp.concatenate(
                [
                    key_value_weight[:, k * HEAD : (k + 1) * HEAD],
                    key_value_weight[:, (3 + k) * HEAD : (4 + k) * HEAD],
                ],
                axis=1,
            )
            for k in KV_SLOT
        ]
    )
    w = lax.all_to_all(jnp.concatenate([wkv, wq], axis=2), "x", 0, 0, tiled=True).reshape(112, 768)
    w_kv = lax.all_gather(w[:, :256], ("z", "core", "y"), axis=0, tiled=True)
    w_q = lax.all_gather(w[:, 256:], ("z", "core", "y"), axis=0, tiled=True)

    normed = normalize(tokens, gain)
    up = [(i, (i + 1) % 4) for i in range(4)]
    down = [(i, (i + 3) % 4) for i in range(4)]
    n3 = lax.ppermute(normed, "x", up)
    n1 = lax.ppermute(normed, "x", down)
    n2a = lax.ppermute(n1[:32], "x", down)
    n2b = lax.ppermute(n3[32:], "x", up)

    first = lax.dynamic_slice(home_offsets, (e, y * 4), (1, 4)).reshape(4)
    idx = jnp.arange(ROW_TOK, dtype=jnp.int32)
    stretch = y * 4 + idx // 64
    pos = (stretch - jnp.repeat(first, 64)) * 64 + idx % 64
    freqs = 1000000.0 ** (-(jnp.arange(64, dtype=jnp.float32) * 2.0 / HEAD))
    angles = pos.astype(jnp.float32)[:, None] * freqs[None, :]
    cos = jnp.cos(angles)
    sin = jnp.sin(angles)
    info = jnp.concatenate([jnp.stack([x, y]), first * 64]).astype(jnp.int32)

    slot = jnp.array(KV_SLOT, jnp.int32)[x]
    kvb = kv_bias.reshape(6, HEAD)
    b_kv = jnp.concatenate([kvb[slot], kvb[slot + 3]]).reshape(1, 256)
    b_q = lax.dynamic_slice(q_bias, (x * 512,), (512,)).reshape(1, 512)

    x_all, kv = pl.pallas_call(
        kv_kernel,
        out_shape=(
            jax.ShapeDtypeStruct((ROW_TOK, 3584), bf),
            jax.ShapeDtypeStruct((ROW_TOK, 256), bf),
        ),
        in_specs=[SM] + [VM] * 9,
        out_specs=(VM, VM),
        compiler_params=BIG,
        name="kv_proj",
    )(info, normed, n1, n2a, n2b, n3, w_kv, b_kv, cos, sin)

    own = (0, 1, 2, 3)
    swap = (1, 0, 3, 2)
    a = [kv] + [lax.ppermute(kv, ("y", "x"), yx_perm(-j, own)) for j in (1, 2, 3)]
    b = [lax.ppermute(kv, ("y", "x"), yx_perm(-j, swap)) for j in (0, 1, 2, 3)]

    send = kv.reshape(16, 16, 256).transpose(1, 0, 2)
    got = lax.all_to_all(send, ("y", "x"), 0, 0, tiled=True).reshape(4, 4, 16, 256)
    mine = jnp.concatenate(
        [got[:, 0, :, :HEAD], got[:, 2, :, :HEAD], got[:, 3, :, :HEAD]]
        + [got[:, 0, :, HEAD:], got[:, 2, :, HEAD:], got[:, 3, :, HEAD:]],
        axis=2,
    ).reshape(64, 768)
    rows = lax.all_gather(mine, ("z", "core"), axis=0, tiled=False)
    hit = plan[:, 0] == e
    cache = jnp.where(hit[:, None, None], rows, jnp.zeros_like(rows)).reshape(1, 1, 512, 768)

    q = pl.pallas_call(
        q_kernel,
        grid=(2,),
        out_shape=jax.ShapeDtypeStruct((ROW_TOK, 512), bf),
        in_specs=[
            pl.BlockSpec((ROW_TOK, 3584), lambda i: (0, 0)),
            pl.BlockSpec((3584, 256), lambda i: (0, i)),
            pl.BlockSpec((1, 256), lambda i: (0, i)),
            pl.BlockSpec((ROW_TOK, 64), lambda i: (0, 0)),
            pl.BlockSpec((ROW_TOK, 64), lambda i: (0, 0)),
        ],
        out_specs=pl.BlockSpec((ROW_TOK, 256), lambda i: (0, i)),
        compiler_params=BIG,
        name="q_proj",
    )(x_all, w_q, b_q, cos, sin)

    kv_spec = pl.BlockSpec((ROW_TOK, 256), lambda i: (0, 0))
    out = pl.pallas_call(
        attend_kernel,
        grid=(4,),
        out_shape=jax.ShapeDtypeStruct((ROW_TOK, 512), bf),
        in_specs=[SM, pl.BlockSpec((ROW_TOK, HEAD), lambda i: (0, i))] + [kv_spec] * 8,
        out_specs=pl.BlockSpec((ROW_TOK, HEAD), lambda i: (0, i)),
        scratch_shapes=[pltpu.VMEM((ROW_TOK, 1024), jnp.float32)],
        compiler_params=BIG,
        name="attend",
    )(info, q, *a, *b)
    back = lax.all_to_all(out.reshape(4, 64, 512), "x", 0, 0, tiled=True)
    attended = back.transpose(1, 0, 2).reshape(64, 2048)
    return attended, cache


def solution(mesh):
    fine = Mesh(mesh.devices.reshape(4, 2, 4, 4), ("z", "core", "y", "x"))
    every = ("z", "core", "y", "x")
    in_specs = (P(every, None), P(), P(every, None), P(every, None), P(), P(), P(), P())
    out_specs = (P(every, None), P(("z", "core"), ("y", "x"), None, None))
    return jax.shard_map(
        per_device, mesh=fine, in_specs=in_specs, out_specs=out_specs, check_vma=False
    )
```

```python
import functools

import jax
import jax.numpy as jnp
import numpy as np
from jax import lax
from jax.experimental import pallas as pl
from jax.experimental.pallas import tpu as pltpu
from jax.sharding import Mesh
from jax.sharding import PartitionSpec as P

HEAD = 128
KV_SLOT = (0, 1, 1, 2)
NEG = -1e30
ROW_TOK = 256


def normalize(rows, gain):
    floats = rows.astype(jnp.float32)
    scaled = (
        floats * lax.rsqrt(jnp.mean(floats * floats, axis=1, keepdims=True) + 1e-06) * gain[None, :]
    )
    return scaled.astype(jnp.bfloat16)


def rotate(v, cos, sin):
    a = v[:, :64]
    b = v[:, 64:]
    return jnp.concatenate([a * cos - b * sin, b * cos + a * sin], axis=1)


def load_weights(info, own, other, buf, sem):
    y = info[1]
    z = info[2]
    core = info[3]
    copies = []
    for half, (ref, t) in enumerate(((own, core), (other, 1 - core))):
        for j in range(4):
            for i in range(4):
                zz = jnp.where(t == 0, i, lax.rem(z + j, 4))
                yy = jnp.where(t == 0, lax.rem(y + j, 4), i)
                row = pl.multiple_of(((2 * zz + t) * 4 + yy) * 112, 16)
                copy = pltpu.make_async_copy(
                    ref.at[j * 4 + i], buf.at[pl.ds(row, 112), :], sem.at[half * 16 + j * 4 + i]
                )
                copy.start()
                copies.append(copy)
    return copies


def kv_kernel(info, n0, n1, n2a, n2b, n3, own, other, b, cos, sin, x_out, kv_out, w, sem, xsem):
    x = info[0]
    copies = []
    for n, (ref, j, low, size) in enumerate(
        ((n0, 0, 0, 64), (n1, 1, 0, 64), (n2a, 2, 0, 32), (n2b, 2, 32, 32), (n3, 3, 0, 64))
    ):
        row = pl.multiple_of(lax.rem(x + j, 4) * 64 + low, 32)
        copy = pltpu.make_async_copy(ref, x_out.at[pl.ds(row, size), :], xsem.at[n])
        copy.start()
        copies.append(copy)
    copies += load_weights(info, own, other, w, sem)
    for copy in copies:
        copy.wait()
    acc = jnp.dot(x_out[...], w[...], preferred_element_type=jnp.float32) + b[...]
    k = rotate(acc[:, :HEAD], cos[...], sin[...])
    kv_out[:, :HEAD] = k.astype(jnp.bfloat16)
    kv_out[:, HEAD:] = acc[:, HEAD:].astype(jnp.bfloat16)


def q_kernel(info, x_in, own, other, b, cos, sin, q_out, w, sem):
    for copy in load_weights(info, own, other, w, sem):
        copy.wait()
    for g in range(2):
        part = slice(g * 256, (g + 1) * 256)
        acc = jnp.dot(x_in[...], w[:, part], preferred_element_type=jnp.float32) + b[:, part]
        for h in range(2):
            q = rotate(acc[:, h * HEAD : (h + 1) * HEAD], cos[...], sin[...])
            low = (2 * g + h) * HEAD
            q_out[:, low : low + HEAD] = q.astype(jnp.bfloat16)


def attend_kernel(info, q, a0, a1, a2, a3, b0, b1, b2, b3, out, mask):
    x = info[0]
    y = info[1]
    h = pl.program_id(0)

    @pl.when(h == 0)
    def _():
        qi = lax.broadcasted_iota(jnp.int32, (ROW_TOK, ROW_TOK), 0)
        ki = lax.broadcasted_iota(jnp.int32, (ROW_TOK, ROW_TOK), 1)
        start = jnp.where(
            qi < 128,
            jnp.where(qi < 64, info[4], info[5]),
            jnp.where(qi < 192, info[6], info[7]),
        )
        for j in range(4):
            key = ki + lax.rem(y + j, 4) * ROW_TOK
            ok = (key >= start) & (key <= qi + y * ROW_TOK)
            mask[:, j * ROW_TOK : (j + 1) * ROW_TOK] = jnp.where(ok, 0.0, NEG)

    use_b = ((x == 1) & (h < 3)) | ((x == 3) & (h < 2))
    pick = jnp.where(use_b, 1, 0)
    qh = q[...]
    parts = []
    vals = []
    for j, (pa, pb) in enumerate(((a0, b0), (a1, b1), (a2, b2), (a3, b3))):
        kv = jnp.where(pick == 1, pb[...], pa[...])
        s = lax.dot_general(
            qh, kv[:, :HEAD], (((1,), (1,)), ((), ())), preferred_element_type=jnp.float32
        )
        parts.append(s * (HEAD**-0.5) + mask[:, j * ROW_TOK : (j + 1) * ROW_TOK])
        vals.append(kv[:, HEAD:])
    top = functools.reduce(jnp.maximum, [jnp.max(s, axis=1, keepdims=True) for s in parts])
    mass = jnp.zeros((ROW_TOK, 1), jnp.float32)
    acc = jnp.zeros((ROW_TOK, HEAD), jnp.float32)
    for s, v in zip(parts, vals):
        p = jnp.exp(s - top)
        mass += jnp.sum(p, axis=1, keepdims=True)
        acc += jnp.dot(p.astype(jnp.bfloat16), v, preferred_element_type=jnp.float32)
    out[...] = (acc / mass).astype(jnp.bfloat16)


VM = pl.BlockSpec(memory_space=pltpu.VMEM)
SM = pl.BlockSpec(memory_space=pltpu.SMEM)
ANY = pl.BlockSpec(memory_space=pl.ANY)
BIG = pltpu.CompilerParams(vmem_limit_bytes=48 * 1024 * 1024)


EVERY = ("z", "core", "y", "x")
SIZES = (4, 2, 4, 4)


def flat(z, c, y, x):
    return ((z % 4 * 2 + c % 2) * 4 + y % 4) * 4 + x % 4


PLACES = [(z, c, y, x) for z in range(4) for c in range(2) for y in range(4) for x in range(4)]


def send(v, move):
    return lax.ppermute(v, EVERY, [(flat(*p), flat(*move(*p))) for p in PLACES])


def along_x(j):
    return lambda z, c, y, x: (z, c, y, x + j)


def along_second(j):
    return lambda z, c, y, x: (z, c, y + j, x) if c == 0 else (z + j, c, y, x)


def other_core(z, c, y, x):
    return (z, 1 - c, y, x)


def kv_move(j, swap):
    return lambda z, c, y, x: (z, c, y + j, x ^ swap)


FIRST = [[flat(z, 0, y, x) for z in range(4) for x in range(4)] for y in range(4)] + [
    [flat(z, 1, y, x) for y in range(4) for x in range(4)] for z in range(4)
]


def per_device(tokens, gain, q_weight, key_value_weight, q_bias, kv_bias, plan, home_offsets):
    z = lax.axis_index("z")
    core = lax.axis_index("core")
    y = lax.axis_index("y")
    x = lax.axis_index("x")
    e = z * 2 + core
    bf = jnp.bfloat16

    normed = normalize(tokens, gain)
    n3 = send(normed, along_x(1))
    n1 = send(normed, along_x(-1))

    wq = q_weight.reshape(28, 4, 512).transpose(1, 0, 2)
    wkv = jnp.stack(
        [
            jnp.concatenate(
                [
                    key_value_weight[:, k * HEAD : (k + 1) * HEAD],
                    key_value_weight[:, (3 + k) * HEAD : (4 + k) * HEAD],
                ],
                axis=1,
            )
            for k in KV_SLOT
        ]
    )
    w = jnp.concatenate([wkv, wq], axis=2)
    w = jnp.broadcast_to(w[None], (4, 4, 28, 768)).reshape(16, 28, 768)
    w = lax.all_to_all(w, EVERY, 0, 0, axis_index_groups=FIRST, tiled=True).reshape(4, 112, 768)
    kv0 = w[:, :, :256]
    q0 = w[:, :, 256:]
    w_kv = jnp.concatenate([kv0] + [send(kv0, along_second(-j)) for j in (1, 2, 3)], axis=0)
    n2a = send(n1[:32], along_x(-1))
    n2b = send(n3[32:], along_x(1))
    q1 = send(q0, along_second(-1))
    q3 = send(q0, along_second(1))
    w_kv_other = send(w_kv, other_core)
    q2a = send(q1[:2], along_second(-1))
    q2b = send(q3[2:], along_second(1))
    w_q = jnp.concatenate([q0, q1, q2a, q2b, q3], axis=0)
    w_q_other = send(w_q, other_core)

    first = lax.dynamic_slice(home_offsets, (e, y * 4), (1, 4)).reshape(4)
    idx = jnp.arange(ROW_TOK, dtype=jnp.int32)
    stretch = y * 4 + idx // 64
    pos = (stretch - jnp.repeat(first, 64)) * 64 + idx % 64
    freqs = 1000000.0 ** (-(jnp.arange(64, dtype=jnp.float32) * 2.0 / HEAD))
    angles = pos.astype(jnp.float32)[:, None] * freqs[None, :]
    cos = jnp.cos(angles)
    sin = jnp.sin(angles)
    info = jnp.concatenate([jnp.stack([x, y, z, core]), first * 64]).astype(jnp.int32)

    slot = jnp.array(KV_SLOT, jnp.int32)[x]
    kvb = kv_bias.reshape(6, HEAD)
    b_kv = jnp.concatenate([kvb[slot], kvb[slot + 3]]).reshape(1, 256)
    b_q = lax.dynamic_slice(q_bias, (x * 512,), (512,)).reshape(1, 512)

    x_all, kv = pl.pallas_call(
        kv_kernel,
        out_shape=(
            jax.ShapeDtypeStruct((ROW_TOK, 3584), bf),
            jax.ShapeDtypeStruct((ROW_TOK, 256), bf),
        ),
        in_specs=[SM] + [ANY] * 7 + [VM] * 3,
        out_specs=(VM, VM),
        scratch_shapes=[
            pltpu.VMEM((3584, 256), bf),
            pltpu.SemaphoreType.DMA((32,)),
            pltpu.SemaphoreType.DMA((5,)),
        ],
        compiler_params=BIG,
        name="kv_proj",
    )(info, normed, n1, n2a, n2b, n3, w_kv, w_kv_other, b_kv, cos, sin)

    a = [kv] + [send(kv, kv_move(-j, 0)) for j in (1, 2, 3)]
    b = [send(kv, kv_move(-j, 1)) for j in (0, 1, 2, 3)]

    got = kv.reshape(16, 16, 256).transpose(1, 0, 2)
    got = lax.all_to_all(got, ("y", "x"), 0, 0, tiled=True).reshape(4, 4, 16, 256)
    mine = jnp.concatenate(
        [got[:, 0, :, :HEAD], got[:, 2, :, :HEAD], got[:, 3, :, :HEAD]]
        + [got[:, 0, :, HEAD:], got[:, 2, :, HEAD:], got[:, 3, :, HEAD:]],
        axis=2,
    ).reshape(64, 768)
    to = plan[e, 0] == jnp.arange(8, dtype=jnp.int32)
    cache = jnp.where(to[:, None, None], mine[None], jnp.zeros_like(mine)[None])
    cache = lax.all_to_all(cache, ("z", "core"), 0, 0, tiled=True).reshape(1, 1, 512, 768)

    q = pl.pallas_call(
        q_kernel,
        out_shape=jax.ShapeDtypeStruct((ROW_TOK, 512), bf),
        in_specs=[SM, VM, ANY, ANY, VM, VM, VM],
        out_specs=VM,
        scratch_shapes=[pltpu.VMEM((3584, 512), bf), pltpu.SemaphoreType.DMA((32,))],
        compiler_params=BIG,
        name="q_proj",
    )(info, x_all, w_q, w_q_other, b_q, cos, sin)

    kv_spec = pl.BlockSpec((ROW_TOK, 256), lambda i: (0, 0))
    out = pl.pallas_call(
        attend_kernel,
        grid=(4,),
        out_shape=jax.ShapeDtypeStruct((ROW_TOK, 512), bf),
        in_specs=[SM, pl.BlockSpec((ROW_TOK, HEAD), lambda i: (0, i))] + [kv_spec] * 8,
        out_specs=pl.BlockSpec((ROW_TOK, HEAD), lambda i: (0, i)),
        scratch_shapes=[pltpu.VMEM((ROW_TOK, 1024), jnp.float32)],
        compiler_params=BIG,
        name="attend",
    )(info, q, *a, *b)
    back = lax.all_to_all(out.reshape(4, 64, 512), "x", 0, 0, tiled=True)
    attended = back.transpose(1, 0, 2).reshape(64, 2048)
    return attended, cache


def solution(mesh):
    fine = Mesh(mesh.devices.reshape(SIZES), EVERY)
    in_specs = (P(EVERY, None), P(), P(EVERY, None), P(EVERY, None), P(), P(), P(), P())
    out_specs = (P(EVERY, None), P(("z", "core"), ("y", "x"), None, None))
    return jax.shard_map(
        per_device, mesh=fine, in_specs=in_specs, out_specs=out_specs, check_vma=False
    )
```

```python
import functools

import jax
import jax.numpy as jnp
import numpy as np
from jax import lax
from jax.experimental import pallas as pl
from jax.experimental.pallas import tpu as pltpu
from jax.sharding import Mesh
from jax.sharding import PartitionSpec as P

HEAD = 128
KV_SLOT = (0, 1, 1, 2)
NEG = -1e30
ROW_TOK = 256


def normalize(rows, gain):
    floats = rows.astype(jnp.float32)
    scaled = (
        floats * lax.rsqrt(jnp.mean(floats * floats, axis=1, keepdims=True) + 1e-06) * gain[None, :]
    )
    return scaled.astype(jnp.bfloat16)


def rotate(v, cos, sin):
    a = v[:, :64]
    b = v[:, 64:]
    return jnp.concatenate([a * cos - b * sin, b * cos + a * sin], axis=1)


def load_weights(info, own, other, buf):
    y = info[1]
    z = info[2]
    core = info[3]
    for ref, t in ((own, core), (other, 1 - core)):
        for j in range(4):
            for i in range(4):
                zz = lax.rem(z + jnp.where(t == 0, i, j), 4)
                yy = lax.rem(y + jnp.where(t == 0, j, i), 4)
                buf[(2 * zz + t) * 4 + yy] = ref[j * 4 + i]


def kv_kernel(info, n0, n1, n2a, n2b, n3, own, other, b, cos, sin, x_out, kv_out, w):
    x = info[0]
    for ref, j, low, size in (
        (n0, 0, 0, 64),
        (n1, 1, 0, 64),
        (n2a, 2, 0, 32),
        (n2b, 2, 32, 32),
        (n3, 3, 0, 64),
    ):
        row = pl.multiple_of(lax.rem(x + j, 4) * 64 + low, 32)
        x_out[pl.ds(row, size), :] = ref[...]
    load_weights(info, own, other, w)
    acc = jnp.dot(x_out[...], w[...].reshape(3584, 256), preferred_element_type=jnp.float32)
    acc += b[...]
    k = rotate(acc[:, :HEAD], cos[...], sin[...])
    kv_out[:, :HEAD] = k.astype(jnp.bfloat16)
    kv_out[:, HEAD:] = acc[:, HEAD:].astype(jnp.bfloat16)


def q_kernel(info, x_in, own, other, b, cos, sin, q_out, w):
    load_weights(info, own, other, w)
    for g in range(2):
        part = slice(g * 256, (g + 1) * 256)
        acc = jnp.dot(
            x_in[...], w[:, :, part].reshape(3584, 256), preferred_element_type=jnp.float32
        )
        acc += b[:, part]
        for h in range(2):
            q = rotate(acc[:, h * HEAD : (h + 1) * HEAD], cos[...], sin[...])
            low = (2 * g + h) * HEAD
            q_out[:, low : low + HEAD] = q.astype(jnp.bfloat16)


def attend_kernel(info, q, kv_all, out, mask):
    x = info[0]
    y = info[1]
    h = pl.program_id(0)

    @pl.when(h == 0)
    def _():
        qi = lax.broadcasted_iota(jnp.int32, (ROW_TOK, 1024), 0)
        key = lax.broadcasted_iota(jnp.int32, (ROW_TOK, 1024), 1)
        start = jnp.where(
            qi < 128,
            jnp.where(qi < 64, info[4], info[5]),
            jnp.where(qi < 192, info[6], info[7]),
        )
        mask[...] = jnp.where((key >= start) & (key <= qi + y * ROW_TOK), 0.0, NEG)

    left = ((x == 1) & (h < 3)) | ((x == 3) & (h < 2))
    side = jnp.where(left, 0, lax.rem(x, 2))
    qh = q[...]
    parts = []
    vals = []
    for j in range(4):
        kv = kv_all[2 * j + side]
        s = lax.dot_general(
            qh, kv[:, :HEAD], (((1,), (1,)), ((), ())), preferred_element_type=jnp.float32
        )
        parts.append(s * (HEAD**-0.5) + mask[:, j * ROW_TOK : (j + 1) * ROW_TOK])
        vals.append(kv[:, HEAD:])
    top = functools.reduce(jnp.maximum, [jnp.max(s, axis=1, keepdims=True) for s in parts])
    mass = jnp.zeros((ROW_TOK, 1), jnp.float32)
    acc = jnp.zeros((ROW_TOK, HEAD), jnp.float32)
    for s, v in zip(parts, vals):
        p = jnp.exp(s - top)
        mass += jnp.sum(p, axis=1, keepdims=True)
        acc += jnp.dot(p.astype(jnp.bfloat16), v, preferred_element_type=jnp.float32)
    out[...] = (acc / mass).astype(jnp.bfloat16)


def hold_kernel(v, after, out):
    out[...] = v[...]


VM = pl.BlockSpec(memory_space=pltpu.VMEM)
SM = pl.BlockSpec(memory_space=pltpu.SMEM)
BIG = pltpu.CompilerParams(vmem_limit_bytes=48 * 1024 * 1024)


EVERY = ("z", "core", "y", "x")
SIZES = (4, 2, 4, 4)


def flat(z, c, y, x):
    return ((z % 4 * 2 + c % 2) * 4 + y % 4) * 4 + x % 4


PLACES = [(z, c, y, x) for z in range(4) for c in range(2) for y in range(4) for x in range(4)]


def send(v, move):
    return lax.ppermute(v, EVERY, [(flat(*p), flat(*move(*p))) for p in PLACES])


def along_x(j):
    return lambda z, c, y, x: (z, c, y, x + j)


def along_second(j):
    return lambda z, c, y, x: (z, c, y + j, x) if c == 0 else (z + j, c, y, x)


def other_core(z, c, y, x):
    return (z, 1 - c, y, x)


def along_first(j):
    return lambda z, c, y, x: (z + j, c, y, x) if c == 0 else (z, c, y + j, x)


PAIR = [
    [flat(z, c, y, 2 * p + i) for y in range(4) for i in range(2)]
    for z in range(4)
    for c in range(2)
    for p in range(2)
]


def hold(v, after):
    return pl.pallas_call(
        hold_kernel,
        out_shape=jax.ShapeDtypeStruct(v.shape, v.dtype),
        in_specs=[VM, pl.BlockSpec(memory_space=pl.ANY)],
        out_specs=VM,
        name="hold",
    )(v, after)


def per_device(tokens, gain, q_weight, key_value_weight, q_bias, kv_bias, plan, home_offsets):
    z = lax.axis_index("z")
    core = lax.axis_index("core")
    y = lax.axis_index("y")
    x = lax.axis_index("x")
    e = z * 2 + core
    bf = jnp.bfloat16

    normed = normalize(tokens, gain)
    n3 = send(normed, along_x(1))
    n1 = send(normed, along_x(-1))

    wq = q_weight.reshape(28, 4, 512).transpose(1, 0, 2)
    wkv = jnp.stack(
        [
            jnp.concatenate(
                [
                    key_value_weight[:, k * HEAD : (k + 1) * HEAD],
                    key_value_weight[:, (3 + k) * HEAD : (4 + k) * HEAD],
                ],
                axis=1,
            )
            for k in KV_SLOT
        ]
    )
    w = jnp.concatenate([wkv, wq], axis=2)
    w = lax.all_to_all(w, "x", 0, 0, tiled=True).reshape(112, 768)
    w = jnp.stack([w] + [send(w, along_first(-j)) for j in (1, 2, 3)])
    kv0 = w[:, :, :256]
    q0 = w[:, :, 256:]
    w_kv = jnp.concatenate([kv0] + [send(kv0, along_second(-j)) for j in (1, 2, 3)], axis=0)
    n2a = send(n1[:32], along_x(-1))
    n2b = send(n3[32:], along_x(1))
    q1 = send(q0, along_second(-1))
    q3 = send(q0, along_second(1))
    w_kv_other = send(w_kv, other_core)
    q2a = send(q1[:2], along_second(-1))
    q2b = send(q3[2:], along_second(1))
    w_q = jnp.concatenate([q0, q1, q2a, q2b, q3], axis=0)
    w_q_other = send(w_q, other_core)

    first = lax.dynamic_slice(home_offsets, (e, y * 4), (1, 4)).reshape(4)
    idx = jnp.arange(ROW_TOK, dtype=jnp.int32)
    stretch = y * 4 + idx // 64
    pos = (stretch - jnp.repeat(first, 64)) * 64 + idx % 64
    freqs = 1000000.0 ** (-(jnp.arange(64, dtype=jnp.float32) * 2.0 / HEAD))
    angles = pos.astype(jnp.float32)[:, None] * freqs[None, :]
    cos = jnp.cos(angles)
    sin = jnp.sin(angles)
    info = jnp.concatenate([jnp.stack([x, y, z, core]), first * 64]).astype(jnp.int32)

    slot = jnp.array(KV_SLOT, jnp.int32)[x]
    kvb = kv_bias.reshape(6, HEAD)
    b_kv = jnp.concatenate([kvb[slot], kvb[slot + 3]]).reshape(1, 256)
    b_q = lax.dynamic_slice(q_bias, (x * 512,), (512,)).reshape(1, 512)

    x_all, kv = pl.pallas_call(
        kv_kernel,
        out_shape=(
            jax.ShapeDtypeStruct((ROW_TOK, 3584), bf),
            jax.ShapeDtypeStruct((ROW_TOK, 256), bf),
        ),
        in_specs=[SM] + [VM] * 10,
        out_specs=(VM, VM),
        scratch_shapes=[pltpu.VMEM((32, 112, 256), bf)],
        compiler_params=BIG,
        name="kv_proj",
    )(info, normed, n1, n2a, n2b, n3, w_kv, w_kv_other, b_kv, cos, sin)

    kv_all = lax.all_to_all(
        jnp.broadcast_to(kv[None], (8, ROW_TOK, 256)),
        EVERY,
        0,
        0,
        axis_index_groups=PAIR,
        tiled=True,
    )

    got = hold(kv, w_q_other).reshape(16, 16, 256).transpose(1, 0, 2)
    got = lax.all_to_all(got, ("y", "x"), 0, 0, tiled=True).reshape(4, 4, 16, 256)
    mine = jnp.concatenate(
        [got[:, 0, :, :HEAD], got[:, 2, :, :HEAD], got[:, 3, :, :HEAD]]
        + [got[:, 0, :, HEAD:], got[:, 2, :, HEAD:], got[:, 3, :, HEAD:]],
        axis=2,
    ).reshape(64, 768)
    to = plan[e, 0] == jnp.arange(8, dtype=jnp.int32)
    cache = jnp.where(to[:, None, None], mine[None], jnp.zeros_like(mine)[None])
    cache = lax.all_to_all(cache, ("z", "core"), 0, 0, tiled=True).reshape(1, 1, 512, 768)

    q = pl.pallas_call(
        q_kernel,
        out_shape=jax.ShapeDtypeStruct((ROW_TOK, 512), bf),
        in_specs=[SM] + [VM] * 6,
        out_specs=VM,
        scratch_shapes=[pltpu.VMEM((32, 112, 512), bf)],
        compiler_params=BIG,
        name="q_proj",
    )(info, x_all, w_q, w_q_other, b_q, cos, sin)

    out = pl.pallas_call(
        attend_kernel,
        grid=(4,),
        out_shape=jax.ShapeDtypeStruct((ROW_TOK, 512), bf),
        in_specs=[
            SM,
            pl.BlockSpec((ROW_TOK, HEAD), lambda i: (0, i)),
            pl.BlockSpec((8, ROW_TOK, 256), lambda i: (0, 0, 0)),
        ],
        out_specs=pl.BlockSpec((ROW_TOK, HEAD), lambda i: (0, i)),
        scratch_shapes=[pltpu.VMEM((ROW_TOK, 1024), jnp.float32)],
        compiler_params=BIG,
        name="attend",
    )(info, q, kv_all)
    back = lax.all_to_all(out.reshape(4, 64, 512), "x", 0, 0, tiled=True)
    attended = back.transpose(1, 0, 2).reshape(64, 2048)
    return attended, cache


def solution(mesh):
    fine = Mesh(mesh.devices.reshape(SIZES), EVERY)
    in_specs = (P(EVERY, None), P(), P(EVERY, None), P(EVERY, None), P(), P(), P(), P())
    out_specs = (P(EVERY, None), P(("z", "core"), ("y", "x"), None, None))
    return jax.shard_map(
        per_device, mesh=fine, in_specs=in_specs, out_specs=out_specs, check_vma=False
    )
```

```python
import functools

import jax
import jax.numpy as jnp
import numpy as np
from jax import lax
from jax.experimental import pallas as pl
from jax.experimental.pallas import tpu as pltpu
from jax.sharding import Mesh
from jax.sharding import PartitionSpec as P

HEAD = 128
KV_SLOT = (0, 1, 1, 2)
NEG = -1e30
ROW_TOK = 256


def rotate(v, cos, sin):
    a = v[:, :64]
    b = v[:, 64:]
    return jnp.concatenate([a * cos - b * sin, b * cos + a * sin], axis=1)


def prep_kernel(info, tokens, gain, wq, wkv, normed, *blocks):
    x = info[0]
    floats = tokens[...].astype(jnp.float32)
    mean = jnp.mean(floats * floats, axis=1, keepdims=True)
    normed[...] = (floats * lax.rsqrt(mean + 1e-06) * gain[...]).astype(jnp.bfloat16)
    for j, block in enumerate(blocks):
        to = lax.rem(x + j, 4)
        slot = (to + 1) // 2
        for n in range(2):
            low = pl.multiple_of((slot + 3 * n) * HEAD, HEAD)
            block[:, n * HEAD : (n + 1) * HEAD] = wkv[:, pl.ds(low, HEAD)]
        block[:, 256:] = wq[:, pl.ds(pl.multiple_of(to * 512, 512), 512)]


def place_kernel(info, p0, p1, p2, p3, n1, n3, out, low, high):
    for j, p in enumerate((p0, p1, p2, p3)):
        out[lax.rem(info[0] + 4 - j, 4)] = p[...]
    low[...] = n1[:32, :]
    high[...] = n3[32:, :]


def stage_kernel(s0, s1, s2, s3, after1, after2, kv0, q0):
    for i, s in enumerate((s0, s1, s2, s3)):
        kv0[i] = s[:, :256]
        q0[i] = s[:, 256:]


def join_kernel(*refs):
    out = refs[-1]
    low = 0
    for ref in refs[:-1]:
        n = ref.shape[0]
        out[low : low + n] = ref[...]
        low += n


def load_weights(info, sources, buf):
    y = info[1]
    z = info[2]
    core = info[3]
    for ref, other, places in sources:
        t = jnp.where(other == 1, 1 - core, core)
        for n, (j, i) in enumerate(places):
            zz = lax.rem(z + jnp.where(t == 0, i, j), 4)
            yy = lax.rem(y + jnp.where(t == 0, j, i), 4)
            buf[(2 * zz + t) * 4 + yy] = ref[n]


def pieces(*blocks):
    return [(j, i) for j in blocks for i in range(4)]


def kv_kernel(info, n0, n1, n2a, n2b, n3, own, other, b, cos, sin, x_out, kv_out, w):
    x = info[0]
    for ref, j, low, size in (
        (n0, 0, 0, 64),
        (n1, 1, 0, 64),
        (n2a, 2, 0, 32),
        (n2b, 2, 32, 32),
        (n3, 3, 0, 64),
    ):
        row = pl.multiple_of(lax.rem(x + j, 4) * 64 + low, 32)
        x_out[pl.ds(row, size), :] = ref[...]
    every = pieces(0, 1, 2, 3)
    load_weights(info, [(own, 0, every), (other, 1, every)], w)
    acc = jnp.dot(x_out[...], w[...].reshape(3584, 256), preferred_element_type=jnp.float32)
    acc += b[...]
    k = rotate(acc[:, :HEAD], cos[...], sin[...])
    kv_out[:, :HEAD] = k.astype(jnp.bfloat16)
    kv_out[:, HEAD:] = acc[:, HEAD:].astype(jnp.bfloat16)


def q_kernel(info, x_in, own1, own2, other1, other2, b, cos, sin, q_out, w):
    first = pieces(0, 1, 3)
    last = pieces(2)
    load_weights(
        info, [(own1, 0, first), (own2, 0, last), (other1, 1, first), (other2, 1, last)], w
    )
    for g in range(2):
        part = slice(g * 256, (g + 1) * 256)
        acc = jnp.dot(
            x_in[...], w[:, :, part].reshape(3584, 256), preferred_element_type=jnp.float32
        )
        acc += b[:, part]
        for h in range(2):
            q = rotate(acc[:, h * HEAD : (h + 1) * HEAD], cos[...], sin[...])
            low = (2 * g + h) * HEAD
            q_out[:, low : low + HEAD] = q.astype(jnp.bfloat16)


def cache_kernel(info, got, *refs):
    out = refs[-1]
    out[...] = jnp.zeros(out.shape, out.dtype)
    to = info[8]
    for y in range(4):
        for n, x in enumerate((0, 2, 3)):
            for part in range(2):
                low = (3 * part + n) * HEAD
                out[to, y * 16 : (y + 1) * 16, low : low + HEAD] = got[
                    4 * y + x, :, part * HEAD : (part + 1) * HEAD
                ]


def merge_kernel(info, r0, r1, r2, r3, out):
    for j, r in enumerate((r0, r1, r2, r3)):
        low = pl.multiple_of(lax.rem(info[0] + 4 - j, 4) * 512, 512)
        out[:, pl.ds(low, 512)] = r[...]


def attend_kernel(info, q, a0, a1, a2, a3, b0, b1, b2, b3, o0, o1, o2, o3, mask, full):
    x = info[0]
    y = info[1]
    h = pl.program_id(0)

    @pl.when(h == 0)
    def _():
        qi = lax.broadcasted_iota(jnp.int32, (ROW_TOK, ROW_TOK), 0)
        ki = lax.broadcasted_iota(jnp.int32, (ROW_TOK, ROW_TOK), 1)
        start = jnp.where(
            qi < 128,
            jnp.where(qi < 64, info[4], info[5]),
            jnp.where(qi < 192, info[6], info[7]),
        )
        for j in range(4):
            key = ki + lax.rem(y + j, 4) * ROW_TOK
            ok = (key >= start) & (key <= qi + y * ROW_TOK)
            mask[:, j * ROW_TOK : (j + 1) * ROW_TOK] = jnp.where(ok, 0.0, NEG)

    left = ((x == 1) & (h < 3)) | ((x == 3) & (h < 2))
    pick = jnp.where(left, 1, 0)
    qh = q[...]
    parts = []
    vals = []
    for j, (pa, pb) in enumerate(((a0, b0), (a1, b1), (a2, b2), (a3, b3))):
        kv = jnp.where(pick == 1, pb[...], pa[...])
        s = lax.dot_general(
            qh, kv[:, :HEAD], (((1,), (1,)), ((), ())), preferred_element_type=jnp.float32
        )
        parts.append(s * (HEAD**-0.5) + mask[:, j * ROW_TOK : (j + 1) * ROW_TOK])
        vals.append(kv[:, HEAD:])
    top = functools.reduce(jnp.maximum, [jnp.max(s, axis=1, keepdims=True) for s in parts])
    mass = jnp.zeros((ROW_TOK, 1), jnp.float32)
    acc = jnp.zeros((ROW_TOK, HEAD), jnp.float32)
    for s, v in zip(parts, vals):
        p = jnp.exp(s - top)
        mass += jnp.sum(p, axis=1, keepdims=True)
        acc += jnp.dot(p.astype(jnp.bfloat16), v, preferred_element_type=jnp.float32)
    full[...] = (acc / mass).astype(jnp.bfloat16)
    for j, o in enumerate((o0, o1, o2, o3)):
        o[...] = full[pl.ds(pl.multiple_of(lax.rem(x + j, 4) * 64, 64), 64), :]


VM = pl.BlockSpec(memory_space=pltpu.VMEM)
SM = pl.BlockSpec(memory_space=pltpu.SMEM)
LATER = pl.BlockSpec(memory_space=pl.ANY)
BIG = pltpu.CompilerParams(vmem_limit_bytes=20 * 1024 * 1024)


EVERY = ("z", "core", "y", "x")
SIZES = (4, 2, 4, 4)


def flat(z, c, y, x):
    return ((z % 4 * 2 + c % 2) * 4 + y % 4) * 4 + x % 4


PLACES = [(z, c, y, x) for z in range(4) for c in range(2) for y in range(4) for x in range(4)]


def send(v, move):
    return lax.ppermute(v, EVERY, [(flat(*p), flat(*move(*p))) for p in PLACES])


def along_x(j):
    return lambda z, c, y, x: (z, c, y, x + j)


def along_second(j):
    return lambda z, c, y, x: (z, c, y + j, x) if c == 0 else (z + j, c, y, x)


def other_core(z, c, y, x):
    return (z, 1 - c, y, x)


def kv_move(j, swap):
    return lambda z, c, y, x: (z, c, y + j, x ^ swap)


def along_first(j):
    return lambda z, c, y, x: (z + j, c, y, x) if c == 0 else (z, c, y + j, x)


def join(*parts):
    shape = (sum(p.shape[0] for p in parts), *parts[0].shape[1:])
    return pl.pallas_call(
        join_kernel,
        out_shape=jax.ShapeDtypeStruct(shape, parts[0].dtype),
        in_specs=[VM] * len(parts),
        out_specs=VM,
        compiler_params=BIG,
        name="join",
    )(*parts)


def per_device(tokens, gain, q_weight, key_value_weight, q_bias, kv_bias, plan, home_offsets):
    z = lax.axis_index("z")
    core = lax.axis_index("core")
    y = lax.axis_index("y")
    x = lax.axis_index("x")
    e = z * 2 + core
    bf = jnp.bfloat16

    first = lax.dynamic_slice(home_offsets, (e, y * 4), (1, 4)).reshape(4)
    info = jnp.concatenate([jnp.stack([x, y, z, core]), first * 64, plan[e, :1]]).astype(jnp.int32)

    normed, *blocks = pl.pallas_call(
        prep_kernel,
        out_shape=(jax.ShapeDtypeStruct((64, 3584), bf),)
        + (jax.ShapeDtypeStruct((28, 768), bf),) * 4,
        in_specs=[SM] + [VM] * 4,
        out_specs=(VM,) * 5,
        compiler_params=BIG,
        name="prep",
    )(info, tokens, gain.reshape(1, 3584), q_weight, key_value_weight)

    n3 = send(normed, along_x(1))
    n1 = send(normed, along_x(-1))
    got = [blocks[0]] + [send(blocks[j], along_x(j)) for j in (1, 2, 3)]
    w, low, high = pl.pallas_call(
        place_kernel,
        out_shape=(jax.ShapeDtypeStruct((4, 28, 768), bf),)
        + (jax.ShapeDtypeStruct((32, 3584), bf),) * 2,
        in_specs=[SM] + [VM] * 6,
        out_specs=(VM,) * 3,
        compiler_params=BIG,
        name="place",
    )(info, *got, n1, n3)
    w = w.reshape(112, 768)
    n2a = send(low, along_x(-1))
    n2b = send(high, along_x(1))
    kv0, q0 = pl.pallas_call(
        stage_kernel,
        out_shape=(
            jax.ShapeDtypeStruct((4, 112, 256), bf),
            jax.ShapeDtypeStruct((4, 112, 512), bf),
        ),
        in_specs=[VM] * 4 + [LATER] * 2,
        out_specs=(VM, VM),
        compiler_params=BIG,
        name="stage",
    )(w, *[send(w, along_first(-j)) for j in (1, 2, 3)], n2a, n2b)
    w_kv = join(kv0, *[send(kv0, along_second(-j)) for j in (1, 2, 3)])
    w_kv_other = send(w_kv, other_core)
    q1 = send(q0, along_second(-1))
    q3 = send(q0, along_second(1))
    q2a = send(q1[:2], along_second(-1))
    q2b = send(q3[2:], along_second(1))
    w_q1 = join(q0, q1, q3)
    w_q1_other = send(w_q1, other_core)
    w_q2 = join(q2a, q2b)
    w_q2_other = send(w_q2, other_core)

    idx = jnp.arange(ROW_TOK, dtype=jnp.int32)
    stretch = y * 4 + idx // 64
    pos = (stretch - jnp.repeat(first, 64)) * 64 + idx % 64
    freqs = 1000000.0 ** (-(jnp.arange(64, dtype=jnp.float32) * 2.0 / HEAD))
    angles = pos.astype(jnp.float32)[:, None] * freqs[None, :]
    cos = jnp.cos(angles)
    sin = jnp.sin(angles)

    slot = jnp.array(KV_SLOT, jnp.int32)[x]
    kvb = kv_bias.reshape(6, HEAD)
    b_kv = jnp.concatenate([kvb[slot], kvb[slot + 3]]).reshape(1, 256)
    b_q = lax.dynamic_slice(q_bias, (x * 512,), (512,)).reshape(1, 512)

    x_all, kv = pl.pallas_call(
        kv_kernel,
        out_shape=(
            jax.ShapeDtypeStruct((ROW_TOK, 3584), bf),
            jax.ShapeDtypeStruct((ROW_TOK, 256), bf),
        ),
        in_specs=[SM] + [VM] * 10,
        out_specs=(VM, VM),
        scratch_shapes=[pltpu.VMEM((32, 112, 256), bf)],
        compiler_params=BIG,
        name="kv_proj",
    )(info, normed, n1, n2a, n2b, n3, w_kv, w_kv_other, b_kv, cos, sin)

    a = [kv] + [send(kv, kv_move(-j, 0)) for j in (1, 2, 3)]
    b = [send(kv, kv_move(-j, 1)) for j in (0, 1, 2, 3)]

    got = kv.reshape(16, 16, 256).transpose(1, 0, 2)
    got = lax.all_to_all(got, ("y", "x"), 0, 0, tiled=True)
    cache = pl.pallas_call(
        cache_kernel,
        out_shape=jax.ShapeDtypeStruct((8, 64, 768), bf),
        in_specs=[SM, VM] + [LATER] * 7,
        out_specs=VM,
        compiler_params=BIG,
        name="cache_send",
    )(info, got, *a[1:], *b)
    cache = lax.all_to_all(cache, ("z", "core"), 0, 0, tiled=True).reshape(1, 1, 512, 768)

    q = pl.pallas_call(
        q_kernel,
        out_shape=jax.ShapeDtypeStruct((ROW_TOK, 512), bf),
        in_specs=[SM] + [VM] * 8,
        out_specs=VM,
        scratch_shapes=[pltpu.VMEM((32, 112, 512), bf)],
        compiler_params=BIG,
        name="q_proj",
    )(info, x_all, w_q1, w_q2, w_q1_other, w_q2_other, b_q, cos, sin)

    kv_spec = pl.BlockSpec((ROW_TOK, 256), lambda i: (0, 0))
    outs = pl.pallas_call(
        attend_kernel,
        grid=(4,),
        out_shape=(jax.ShapeDtypeStruct((64, 512), bf),) * 4,
        in_specs=[SM, pl.BlockSpec((ROW_TOK, HEAD), lambda i: (0, i))] + [kv_spec] * 8,
        out_specs=(pl.BlockSpec((64, HEAD), lambda i: (0, i)),) * 4,
        scratch_shapes=[
            pltpu.VMEM((ROW_TOK, 1024), jnp.float32),
            pltpu.VMEM((ROW_TOK, HEAD), bf),
        ],
        compiler_params=BIG,
        name="attend",
    )(info, q, *a, *b)
    back = [outs[0]] + [send(outs[j], along_x(j)) for j in (1, 2, 3)]
    attended = pl.pallas_call(
        merge_kernel,
        out_shape=jax.ShapeDtypeStruct((64, 2048), bf),
        in_specs=[SM] + [VM] * 4,
        out_specs=VM,
        compiler_params=BIG,
        name="merge",
    )(info, *back)
    return attended, cache


def solution(mesh):
    fine = Mesh(mesh.devices.reshape(SIZES), EVERY)
    in_specs = (P(EVERY, None), P(), P(EVERY, None), P(EVERY, None), P(), P(), P(), P())
    out_specs = (P(EVERY, None), P(("z", "core"), ("y", "x"), None, None))
    return jax.shard_map(
        per_device, mesh=fine, in_specs=in_specs, out_specs=out_specs, check_vma=False
    )
```

```python
import functools

import jax
import jax.numpy as jnp
import numpy as np
from jax import lax
from jax.experimental import pallas as pl
from jax.experimental.pallas import tpu as pltpu
from jax.sharding import Mesh
from jax.sharding import PartitionSpec as P

HEAD = 128
NEG = -1e30
ROW_TOK = 256
COLS = 768

EVERY = ("z", "core", "y", "x")
SIZES = (4, 2, 4, 4)
VM = pl.BlockSpec(memory_space=pltpu.VMEM)
SM = pl.BlockSpec(memory_space=pltpu.SMEM)
ANY = pl.BlockSpec(memory_space=pl.ANY)
BIG = pltpu.CompilerParams(vmem_limit_bytes=20 * 1024 * 1024)


def rotary_table():
    angles = np.arange(1024)[:, None] * 1000000.0 ** (-np.arange(64) * 2.0 / HEAD)[None, :]
    return np.concatenate([np.cos(angles), np.sin(angles)], axis=1).astype(np.float32)


def flat(z, c, y, x):
    return ((z % 4 * 2 + c % 2) * 4 + y % 4) * 4 + x % 4


PLACES = [(z, c, y, x) for z in range(4) for c in range(2) for y in range(4) for x in range(4)]


def send(v, move):
    return lax.ppermute(v, EVERY, [(flat(*p), flat(*move(*p))) for p in PLACES])


def along_x(j):
    return lambda z, c, y, x: (z, c, y, x + j)


def along_z(j):
    return lambda z, c, y, x: (z + j, c, y, x)


def along_first(j):
    return lambda z, c, y, x: (z + j, c, y, x) if c == 0 else (z, c, y + j, x)


def along_second(j):
    return lambda z, c, y, x: (z, c, y + j, x) if c == 0 else (z + j, c, y, x)


def other_core(z, c, y, x):
    return (z, 1 - c, y, x)


def kv_move(j, swap):
    return lambda z, c, y, x: (z, c, y + j, x ^ swap)


def across_x(z, c, y, x):
    return (z, c, y, x ^ 2)


def call(kernel, outs, operands, in_specs=None, scratch=(), **more):
    outs = tuple(jax.ShapeDtypeStruct(s, d) for s, d in outs)
    return pl.pallas_call(
        kernel,
        out_shape=outs,
        in_specs=[VM] * len(operands) if in_specs is None else in_specs,
        out_specs=(VM,) * len(outs),
        scratch_shapes=list(scratch),
        compiler_params=BIG,
        name=kernel.__name__,
        **more,
    )(*operands)


def prep(tokens, gain, wq, wkv, normed, b0, b1, b2, b3, t_buf, g_buf, q_buf, kv_buf, sem):
    copies = [
        pltpu.make_async_copy(a, b, sem.at[n])
        for n, (a, b) in enumerate(((tokens, t_buf), (gain, g_buf), (wq, q_buf), (wkv, kv_buf)))
    ]
    for copy in copies:
        copy.start()
    copies[2].wait()
    copies[3].wait()
    x = lax.axis_index("x")
    for j, block in enumerate((b0, b1, b2, b3)):
        to = lax.rem(x + j, 4)
        slot = lax.div(to + 1, 2)
        for n in range(2):
            low = pl.multiple_of((slot + 3 * n) * HEAD, HEAD)
            block[:, n * HEAD : (n + 1) * HEAD] = kv_buf[:, pl.ds(low, HEAD)]
        block[:, 256:] = q_buf[:, pl.ds(pl.multiple_of(to * 512, 512), 512)]
    copies[0].wait()
    copies[1].wait()
    floats = t_buf[...].astype(jnp.float32)
    mean = jnp.mean(floats * floats, axis=1, keepdims=True)
    normed[...] = (floats * lax.rsqrt(mean + 1e-06) * g_buf[...][None, :]).astype(jnp.bfloat16)


def place(p0, p1, p2, p3, normed, out, n0, buf):
    x = lax.axis_index("x")
    for j, p in enumerate((p0, p1, p2, p3)):
        buf[lax.rem(x + 4 - j, 4)] = p[...].astype(jnp.float32)
    out[...] = jnp.concatenate([buf[k] for k in range(4)], axis=0).astype(jnp.bfloat16)
    n0[...] = normed[...]


def stage(s0, s1, s2, s3, n1, n3, block, low, high):
    for i, s in enumerate((s0, s1, s2, s3)):
        block[i] = s[...]
    low[...] = n1[:32, :]
    high[...] = n3[32:, :]


def relay(s0, s1, s3, n2a, n2b, joined, r1, r3):
    for n, s in enumerate((s0, s1, s3)):
        joined[4 * n : 4 * n + 4] = s[...]
    r1[...] = s1[:2]
    r3[...] = s3[2:]


def join2(a, b, out):
    out[:2] = a[...]
    out[2:] = b[...]


def load_weights(ref, t, places, buf):
    y = lax.axis_index("y")
    z = lax.axis_index("z")
    for n, (j, i) in enumerate(places):
        zz = lax.rem(z + jnp.where(t == 0, i, j), 4)
        yy = lax.rem(y + jnp.where(t == 0, j, i), 4)
        buf[(2 * zz + t) * 4 + yy] = ref[n]


FIRST = [(j, i) for j in (0, 1, 3) for i in range(4)]
LAST = [(2, i) for i in range(4)]


def gather(
    offsets, own1, own2, other1, n0, n1, n2a, n2b, n3, table, qb, kvb, w, x_out, cs, qb_out, kvb_out, sem
):
    e = 2 * lax.axis_index("z") + lax.axis_index("core")
    y = lax.axis_index("y")
    x = lax.axis_index("x")
    core = lax.axis_index("core")
    copies = []
    for k in range(4):
        s = 4 * y + k
        row = pl.multiple_of((s - offsets[e, s]) * 64, 64)
        copies.append(
            pltpu.make_async_copy(
                table.at[pl.ds(row, 64), :], cs.at[k * 64 : (k + 1) * 64, :], sem.at[k]
            )
        )
    copies.append(
        pltpu.make_async_copy(qb.at[pl.ds(pl.multiple_of(x * 512, 512), 512)], qb_out, sem.at[4])
    )
    slot = lax.div(x + 1, 2)
    for n in range(2):
        low = pl.multiple_of((slot + 3 * n) * HEAD, HEAD)
        copies.append(
            pltpu.make_async_copy(kvb.at[pl.ds(low, HEAD)], kvb_out.at[n], sem.at[5 + n])
        )
    for copy in copies:
        copy.start()
    for ref, j, low, size in (
        (n0, 0, 0, 64),
        (n1, 1, 0, 64),
        (n2a, 2, 0, 32),
        (n2b, 2, 32, 32),
        (n3, 3, 0, 64),
    ):
        row = pl.multiple_of(lax.rem(x + j, 4) * 64 + low, 32)
        x_out[pl.ds(row, size), :] = ref[...]
    load_weights(own1, core, FIRST, w)
    load_weights(own2, core, LAST, w)
    load_weights(other1, 1 - core, FIRST, w)
    for copy in copies:
        copy.wait()


def rotate(v, cos, sin):
    a = v[:, :64]
    b = v[:, 64:]
    return jnp.concatenate([a * cos - b * sin, b * cos + a * sin], axis=1).astype(jnp.bfloat16)


def project(w_in, other2, x_in, cs, qb, kvb, w, kv, q):
    del w_in
    load_weights(other2, 1 - lax.axis_index("core"), LAST, w)
    cos = cs[:, :64]
    sin = cs[:, 64:]
    for g in range(3):
        part = slice(g * 256, (g + 1) * 256)
        acc = jnp.dot(
            x_in[...], w[:, :, part].reshape(3584, 256), preferred_element_type=jnp.float32
        )
        if g == 0:
            kv[:, :HEAD] = rotate(acc[:, :HEAD] + kvb[0][None, :], cos, sin)
            kv[:, HEAD:] = (acc[:, HEAD:] + kvb[1][None, :]).astype(jnp.bfloat16)
        else:
            for h in range(2):
                low = (2 * (g - 1) + h) * HEAD
                bias = qb[low : low + HEAD][None, :]
                q[:, low : low + HEAD] = rotate(acc[:, h * HEAD : (h + 1) * HEAD] + bias, cos, sin)


def attend(offsets, q, a0, a1, a2, a3, b0, b1, b2, b3, o0, o1, o2, o3, mask, full):
    x = lax.axis_index("x")
    y = lax.axis_index("y")
    e = 2 * lax.axis_index("z") + lax.axis_index("core")
    qi = lax.broadcasted_iota(jnp.int32, (ROW_TOK, ROW_TOK), 0)
    ki = lax.broadcasted_iota(jnp.int32, (ROW_TOK, ROW_TOK), 1)
    starts = [offsets[e, 4 * y + k] * 64 for k in range(4)]
    start = jnp.where(
        qi < 128,
        jnp.where(qi < 64, starts[0], starts[1]),
        jnp.where(qi < 192, starts[2], starts[3]),
    )
    for j in range(4):
        key = ki + lax.rem(y + j, 4) * ROW_TOK
        ok = (key >= start) & (key <= qi + y * ROW_TOK)
        mask[:, j * ROW_TOK : (j + 1) * ROW_TOK] = jnp.where(ok, 0.0, NEG)

    for h in range(4):
        left = (x == 1) if h == 2 else ((x == 1) | (x == 3))
        pick = jnp.where(left, 1, 0) if h < 3 else 0
        qh = q[:, h * HEAD : (h + 1) * HEAD]
        parts = []
        vals = []
        for j, (pa, pb) in enumerate(((a0, b0), (a1, b1), (a2, b2), (a3, b3))):
            kv = jnp.where(pick == 1, pb[...], pa[...]) if h < 3 else pa[...]
            s = lax.dot_general(
                qh, kv[:, :HEAD], (((1,), (1,)), ((), ())), preferred_element_type=jnp.float32
            )
            parts.append(s * (HEAD**-0.5) + mask[:, j * ROW_TOK : (j + 1) * ROW_TOK])
            vals.append(kv[:, HEAD:])
        top = functools.reduce(jnp.maximum, [jnp.max(s, axis=1, keepdims=True) for s in parts])
        mass = jnp.zeros((ROW_TOK, 1), jnp.float32)
        acc = jnp.zeros((ROW_TOK, HEAD), jnp.float32)
        for s, v in zip(parts, vals):
            p = jnp.exp(s - top)
            mass += jnp.sum(p, axis=1, keepdims=True)
            acc += jnp.dot(p.astype(jnp.bfloat16), v, preferred_element_type=jnp.float32)
        full[:, h * HEAD : (h + 1) * HEAD] = (acc / mass).astype(jnp.bfloat16)
    for j, o in enumerate((o0, o1, o2, o3)):
        o[...] = full[pl.ds(pl.multiple_of(lax.rem(x + j, 4) * 64, 64), 64), :]


def merge(r0, r1, r2, r3, out):
    x = lax.axis_index("x")
    for j, r in enumerate((r0, r1, r2, r3)):
        low = pl.multiple_of(lax.rem(x + 4 - j, 4) * 512, 512)
        out[:, pl.ds(low, 512)] = r[...]


def cache_rows(a0, a1, a2, a3, b0, b1, b2, b3, own_a, own_b, third):
    x = lax.axis_index("x")
    y = lax.axis_index("y")
    i = lax.broadcasted_iota(jnp.int32, (32, ROW_TOK), 0)
    t = lax.broadcasted_iota(jnp.int32, (32, ROW_TOK), 1)
    here = 4 * y + x
    there = 4 * y + lax.rem(x + 2, 4)
    want = jnp.where(i < 16, 16 * i + here, 16 * (i - 16) + there)
    select = jnp.where(t == want, 1.0, 0.0).astype(jnp.bfloat16)
    send_b = jnp.where((x == 1) | (x == 2), 1, 0)
    for j, (a, b) in enumerate(((a0, b0), (a1, b1), (a2, b2), (a3, b3))):
        ra = jnp.dot(select, a[...], preferred_element_type=jnp.float32).astype(jnp.bfloat16)
        rb = jnp.dot(select, b[...], preferred_element_type=jnp.float32).astype(jnp.bfloat16)
        rows = pl.ds(pl.multiple_of(lax.rem(y + j, 4) * 16, 16), 16)
        own_a[rows, :] = ra[:16]
        own_b[rows, :] = rb[:16]
        third[rows, :] = jnp.where(send_b == 1, rb[16:], ra[16:])


def cache_heads(a, b, t, after, out):
    x = lax.axis_index("x")
    av, bv, tv = a[...], b[...], t[...]
    heads = (
        jnp.where(x == 0, av, jnp.where(x == 1, bv, tv)),
        jnp.where((x == 0) | (x == 3), bv, av),
        jnp.where(x == 3, av, jnp.where(x == 2, bv, tv)),
    )
    for k, v in enumerate(heads):
        out[:, k * HEAD : (k + 1) * HEAD] = v[:, :HEAD]
        out[:, (3 + k) * HEAD : (4 + k) * HEAD] = v[:, HEAD:]


def cache_join(c0, c1, c2, c3, out):
    for n, c in enumerate((c0, c1, c2, c3)):
        out[n] = c[...]


def cache_write(plan, own, other, out):
    z = lax.axis_index("z")
    core = lax.axis_index("core")
    group = 2 * z + core
    for ref, t in ((own, core), (other, 1 - core)):
        for j in range(4):
            e = 2 * lax.rem(z + j, 4) + t
            rows = pl.ds(pl.multiple_of(e * 64, 64), 64)
            v = ref[j]
            out[0, 0, rows, :] = jnp.where(plan[e, 0] == group, v, jnp.zeros_like(v))


def per_device(tokens, gain, q_weight, key_value_weight, q_bias, kv_bias, plan, home_offsets):
    bf = jnp.bfloat16
    f32 = jnp.float32
    normed, *blocks = call(
        prep,
        [((64, 3584), bf)] + [((28, COLS), bf)] * 4,
        (tokens, gain, q_weight, key_value_weight),
        [ANY] * 4,
        [
            pltpu.VMEM((64, 3584), bf),
            pltpu.VMEM((3584,), f32),
            pltpu.VMEM((28, 2048), bf),
            pltpu.VMEM((28, 768), bf),
            pltpu.SemaphoreType.DMA((4,)),
        ],
    )
    got = [blocks[0]] + [send(blocks[j], along_x(j)) for j in (1, 2, 3)]
    w0, n0 = call(
        place,
        [((112, COLS), bf), ((64, 3584), bf)],
        (*got, normed),
        scratch=[pltpu.VMEM((4, 28, COLS), f32)],
    )
    w1, w2, w3 = [send(w0, along_first(-j)) for j in (1, 2, 3)]
    n1 = send(n0, along_x(-1))
    n3 = send(n0, along_x(1))
    s0, low, high = call(
        stage,
        [((4, 112, COLS), bf), ((32, 3584), bf), ((32, 3584), bf)],
        (w0, w1, w2, w3, n1, n3),
    )
    s1 = send(s0, along_second(-1))
    s3 = send(s0, along_second(1))
    n2a = send(low, along_x(-1))
    n2b = send(high, along_x(1))
    own1, r1, r3 = call(
        relay,
        [((12, 112, COLS), bf), ((2, 112, COLS), bf), ((2, 112, COLS), bf)],
        (s0, s1, s3, n2a, n2b),
        [VM] * 3 + [ANY] * 2,
    )
    s2a = send(r1, along_second(-1))
    s2b = send(r3, along_second(1))
    other1 = send(own1, other_core)
    (own2,) = call(join2, [((4, 112, COLS), bf)], (s2a, s2b))
    other2 = send(own2, other_core)
    w, x_all, cs, qb, kvb = call(
        gather,
        [
            ((32, 112, COLS), bf),
            ((ROW_TOK, 3584), bf),
            ((ROW_TOK, HEAD), f32),
            ((512,), f32),
            ((2, HEAD), f32),
        ],
        (
            home_offsets, own1, own2, other1, n0, n1, n2a, n2b, n3,
            jnp.asarray(rotary_table()), q_bias, kv_bias,
        ),
        [SM] + [VM] * 8 + [ANY] * 3,
        [pltpu.SemaphoreType.DMA((7,))],
    )
    _, kv, q = call(
        project,
        [((32, 112, COLS), bf), ((ROW_TOK, 256), bf), ((ROW_TOK, 512), bf)],
        (w, other2, x_all, cs, qb, kvb),
        input_output_aliases={0: 0},
    )

    a = [kv] + [send(kv, kv_move(-j, 0)) for j in (1, 2, 3)]
    b = [send(kv, kv_move(-j, 1)) for j in (0, 1, 2, 3)]
    own_a, own_b, third = call(cache_rows, [((64, 256), bf)] * 3, (*a, *b))
    outs = call(
        attend,
        [((64, 512), bf)] * 4,
        (home_offsets, q, *a, *b),
        [SM] + [VM] * 9,
        [pltpu.VMEM((ROW_TOK, 1024), f32), pltpu.VMEM((ROW_TOK, 512), bf)],
    )
    (mine,) = call(
        cache_heads,
        [((64, 768), bf)],
        (own_a, own_b, send(third, across_x), outs[0]),
        [VM] * 3 + [ANY],
    )
    (attended,) = call(
        merge, [((64, 2048), bf)], (outs[0], *[send(outs[j], along_x(j)) for j in (1, 2, 3)])
    )
    (cached,) = call(
        cache_join, [((4, 64, 768), bf)], (mine, *[send(mine, along_z(-j)) for j in (1, 2, 3)])
    )
    (cache,) = call(
        cache_write,
        [((1, 1, 512, 768), bf)],
        (plan, cached, send(cached, other_core)),
        [SM, VM, VM],
    )
    return attended, cache


def solution(mesh):
    fine = Mesh(mesh.devices.reshape(SIZES), EVERY)
    in_specs = (P(EVERY, None), P(), P(EVERY, None), P(EVERY, None), P(), P(), P(), P())
    out_specs = (P(EVERY, None), P(("z", "core"), ("y", "x"), None, None))
    return jax.shard_map(
        per_device, mesh=fine, in_specs=in_specs, out_specs=out_specs, check_vma=False
    )
```

```python
import functools

import jax
import jax.numpy as jnp
import numpy as np
from jax import lax
from jax.experimental import pallas as pl
from jax.experimental.pallas import tpu as pltpu
from jax.sharding import Mesh
from jax.sharding import PartitionSpec as P

HEAD = 128
NEG = -1e30
ROW_TOK = 256
COLS = 768

EVERY = ("z", "core", "y", "x")
SIZES = (4, 2, 4, 4)
VM = pl.BlockSpec(memory_space=pltpu.VMEM)
SM = pl.BlockSpec(memory_space=pltpu.SMEM)
ANY = pl.BlockSpec(memory_space=pl.ANY)


def rotary_table():
    angles = np.arange(1024)[:, None] * 1000000.0 ** (-np.arange(64) * 2.0 / HEAD)[None, :]
    return np.concatenate([np.cos(angles), np.sin(angles)], axis=1).astype(np.float32)


def flat(z, c, y, x):
    return ((z % 4 * 2 + c % 2) * 4 + y % 4) * 4 + x % 4


PLACES = [(z, c, y, x) for z in range(4) for c in range(2) for y in range(4) for x in range(4)]


def send(v, move):
    return lax.ppermute(v, EVERY, [(flat(*p), flat(*move(*p))) for p in PLACES])


def along_x(j):
    return lambda z, c, y, x: (z, c, y, x + j)


def along_z(j):
    return lambda z, c, y, x: (z + j, c, y, x)


def along_first(j):
    return lambda z, c, y, x: (z + j, c, y, x) if c == 0 else (z, c, y + j, x)


def along_second(j):
    return lambda z, c, y, x: (z, c, y + j, x) if c == 0 else (z + j, c, y, x)


def other_core(z, c, y, x):
    return (z, 1 - c, y, x)


def along_y(j):
    return lambda z, c, y, x: (z, c, y + j, x)


def pair_x(z, c, y, x):
    return (z, c, y, x ^ 1)


def call(kernel, outs, operands, in_specs=None, scratch=(), grant=20, **more):
    outs = tuple(jax.ShapeDtypeStruct(s, d) for s, d in outs)
    return pl.pallas_call(
        kernel,
        out_shape=outs,
        in_specs=[VM] * len(operands) if in_specs is None else in_specs,
        out_specs=(VM,) * len(outs),
        scratch_shapes=list(scratch),
        compiler_params=pltpu.CompilerParams(vmem_limit_bytes=grant * 1024 * 1024),
        name=kernel.__name__,
        **more,
    )(*operands)


def cut(wq, wkv, b0, b1, b2, b3, q_buf, kv_buf, sem):
    copies = [
        pltpu.make_async_copy(wq, q_buf, sem.at[0]),
        pltpu.make_async_copy(wkv, kv_buf, sem.at[1]),
    ]
    for copy in copies:
        copy.start()
    for copy in copies:
        copy.wait()
    x = lax.axis_index("x")
    for j, block in enumerate((b0, b1, b2, b3)):
        to = lax.rem(x + j, 4)
        slot = lax.div(to + 1, 2)
        for n in range(2):
            low = pl.multiple_of((slot + 3 * n) * HEAD, HEAD)
            block[:, n * HEAD : (n + 1) * HEAD] = kv_buf[:, pl.ds(low, HEAD)]
        block[:, 256:] = q_buf[:, pl.ds(pl.multiple_of(to * 512, 512), 512)]


def norm(tokens, gain, after, out):
    floats = tokens[...].astype(jnp.float32)
    mean = jnp.mean(floats * floats, axis=1, keepdims=True)
    out[...] = (floats * lax.rsqrt(mean + 1e-06) * gain[...][None, :]).astype(jnp.bfloat16)


def place(p0, p1, p2, p3, out, buf):
    x = lax.axis_index("x")
    for j, p in enumerate((p0, p1, p2, p3)):
        buf[lax.rem(x + 4 - j, 4)] = p[...].astype(jnp.float32)
    out[...] = jnp.concatenate([buf[k] for k in range(4)], axis=0).astype(jnp.bfloat16)


def stage(s0, s1, s2, s3, after, block):
    for i, s in enumerate((s0, s1, s2, s3)):
        block[i] = s[...]


def relay(s0, s1, s3, n1, n3, joined, r1, r3, low, high):
    for n, s in enumerate((s0, s1, s3)):
        joined[4 * n : 4 * n + 4] = s[...]
    r1[...] = s1[:2]
    r3[...] = s3[2:]
    low[...] = n1[:32, :]
    high[...] = n3[32:, :]


def join2(a, b, after1, after2, out):
    out[:2] = a[...]
    out[2:] = b[...]


def load_weights(ref, t, places, buf):
    y = lax.axis_index("y")
    z = lax.axis_index("z")
    for n, (j, i) in enumerate(places):
        zz = lax.rem(z + jnp.where(t == 0, i, j), 4)
        yy = lax.rem(y + jnp.where(t == 0, j, i), 4)
        buf[(2 * zz + t) * 4 + yy] = ref[n]


FIRST = [(j, i) for j in (0, 1, 3) for i in range(4)]
LAST = [(2, i) for i in range(4)]


def gather(
    offsets, own1, own2, other1, n0, n1, n2a, n2b, n3, table, qb, kvb, w, x_out, cs, qb_out, kvb_out, sem
):
    e = 2 * lax.axis_index("z") + lax.axis_index("core")
    y = lax.axis_index("y")
    x = lax.axis_index("x")
    core = lax.axis_index("core")
    copies = []
    for k in range(4):
        s = 4 * y + k
        row = pl.multiple_of((s - offsets[e, s]) * 64, 64)
        copies.append(
            pltpu.make_async_copy(
                table.at[pl.ds(row, 64), :], cs.at[k * 64 : (k + 1) * 64, :], sem.at[k]
            )
        )
    copies.append(
        pltpu.make_async_copy(qb.at[pl.ds(pl.multiple_of(x * 512, 512), 512)], qb_out, sem.at[4])
    )
    slot = lax.div(x + 1, 2)
    for n in range(2):
        low = pl.multiple_of((slot + 3 * n) * HEAD, HEAD)
        copies.append(
            pltpu.make_async_copy(kvb.at[pl.ds(low, HEAD)], kvb_out.at[n], sem.at[5 + n])
        )
    for copy in copies:
        copy.start()
    for ref, j, low, size in (
        (n0, 0, 0, 64),
        (n1, 1, 0, 64),
        (n2a, 2, 0, 32),
        (n2b, 2, 32, 32),
        (n3, 3, 0, 64),
    ):
        row = pl.multiple_of(lax.rem(x + j, 4) * 64 + low, 32)
        x_out[pl.ds(row, size), :] = ref[...]
    load_weights(own1, core, FIRST, w)
    load_weights(own2, core, LAST, w)
    load_weights(other1, 1 - core, FIRST, w)
    for copy in copies:
        copy.wait()


def rotate(v, cos, sin):
    a = v[:, :64]
    b = v[:, 64:]
    return jnp.concatenate([a * cos - b * sin, b * cos + a * sin], axis=1).astype(jnp.bfloat16)


def project(w_in, other2, x_in, cs, qb, kvb, w, kv, q):
    del w_in
    load_weights(other2, 1 - lax.axis_index("core"), LAST, w)
    cos = cs[:, :64]
    sin = cs[:, 64:]
    for g in range(3):
        part = slice(g * 256, (g + 1) * 256)
        acc = jnp.dot(
            x_in[...], w[:, :, part].reshape(3584, 256), preferred_element_type=jnp.float32
        )
        if g == 0:
            kv[:, :HEAD] = rotate(acc[:, :HEAD] + kvb[0][None, :], cos, sin)
            kv[:, HEAD:] = (acc[:, HEAD:] + kvb[1][None, :]).astype(jnp.bfloat16)
        else:
            for h in range(2):
                low = (2 * (g - 1) + h) * HEAD
                bias = qb[low : low + HEAD][None, :]
                q[:, low : low + HEAD] = rotate(acc[:, h * HEAD : (h + 1) * HEAD] + bias, cos, sin)


def attend(offsets, q, a0, a1, a2, a3, b0, b1, b2, b3, after, o0, o1, o2, o3, mask, full):
    x = lax.axis_index("x")
    y = lax.axis_index("y")
    e = 2 * lax.axis_index("z") + lax.axis_index("core")
    qi = lax.broadcasted_iota(jnp.int32, (ROW_TOK, ROW_TOK), 0)
    ki = lax.broadcasted_iota(jnp.int32, (ROW_TOK, ROW_TOK), 1)
    starts = [offsets[e, 4 * y + k] * 64 for k in range(4)]
    start = jnp.where(
        qi < 128,
        jnp.where(qi < 64, starts[0], starts[1]),
        jnp.where(qi < 192, starts[2], starts[3]),
    )
    for j in range(4):
        key = ki + lax.rem(y + j, 4) * ROW_TOK
        ok = (key >= start) & (key <= qi + y * ROW_TOK)
        mask[:, j * ROW_TOK : (j + 1) * ROW_TOK] = jnp.where(ok, 0.0, NEG)

    for h in range(4):
        left = (x == 1) if h == 2 else ((x == 1) | (x == 3))
        pick = jnp.where(left, 1, 0) if h < 3 else 0
        qh = q[:, h * HEAD : (h + 1) * HEAD]
        parts = []
        vals = []
        for j, (pa, pb) in enumerate(((a0, b0), (a1, b1), (a2, b2), (a3, b3))):
            kv = jnp.where(pick == 1, pb[...], pa[...]) if h < 3 else pa[...]
            s = lax.dot_general(
                qh, kv[:, :HEAD], (((1,), (1,)), ((), ())), preferred_element_type=jnp.float32
            )
            parts.append(s * (HEAD**-0.5) + mask[:, j * ROW_TOK : (j + 1) * ROW_TOK])
            vals.append(kv[:, HEAD:])
        top = functools.reduce(jnp.maximum, [jnp.max(s, axis=1, keepdims=True) for s in parts])
        mass = jnp.zeros((ROW_TOK, 1), jnp.float32)
        acc = jnp.zeros((ROW_TOK, HEAD), jnp.float32)
        for s, v in zip(parts, vals):
            p = jnp.exp(s - top)
            mass += jnp.sum(p, axis=1, keepdims=True)
            acc += jnp.dot(p.astype(jnp.bfloat16), v, preferred_element_type=jnp.float32)
        full[:, h * HEAD : (h + 1) * HEAD] = (acc / mass).astype(jnp.bfloat16)
    for j, o in enumerate((o0, o1, o2, o3)):
        o[...] = full[pl.ds(pl.multiple_of(lax.rem(x + j, 4) * 64, 64), 64), :]


def merge(r0, r1, r2, r3, out):
    x = lax.axis_index("x")
    for j, r in enumerate((r0, r1, r2, r3)):
        low = pl.multiple_of(lax.rem(x + 4 - j, 4) * 512, 512)
        out[:, pl.ds(low, 512)] = r[...]


def cache_rows(a0, a1, a2, a3, t0, t1, t2, t3):
    x = lax.axis_index("x")
    y = lax.axis_index("y")
    i = lax.broadcasted_iota(jnp.int32, (64, ROW_TOK), 0)
    t = lax.broadcasted_iota(jnp.int32, (64, ROW_TOK), 1)
    want = 16 * lax.rem(i, 16) + 4 * y + lax.rem(x + lax.div(i, 16), 4)
    select = jnp.where(t == want, 1.0, 0.0).astype(jnp.bfloat16)
    for j, a in enumerate((a0, a1, a2, a3)):
        got = jnp.dot(select, a[...], preferred_element_type=jnp.float32).astype(jnp.bfloat16)
        rows = pl.ds(pl.multiple_of(lax.rem(y + j, 4) * 16, 16), 16)
        for k, out in enumerate((t0, t1, t2, t3)):
            out[rows, :] = got[16 * k : 16 * k + 16]


def cache_heads(t0, t1, t2, t3, out, buf):
    x = lax.axis_index("x")
    for j, t in enumerate((t0, t1, t2, t3)):
        buf[lax.rem(x + 4 - j, 4)] = t[...]
    for k, src in enumerate((0, 1, 3)):
        out[:, k * HEAD : (k + 1) * HEAD] = buf[src, :, :HEAD]
        out[:, (3 + k) * HEAD : (4 + k) * HEAD] = buf[src, :, HEAD:]


def cache_join(c0, c1, c2, c3, after, out):
    for n, c in enumerate((c0, c1, c2, c3)):
        out[n] = c[...]


def cache_write(plan, own, other, out):
    z = lax.axis_index("z")
    core = lax.axis_index("core")
    group = 2 * z + core
    for ref, t in ((own, core), (other, 1 - core)):
        for j in range(4):
            e = 2 * lax.rem(z + j, 4) + t
            rows = pl.ds(pl.multiple_of(e * 64, 64), 64)
            v = ref[j]
            out[0, 0, rows, :] = jnp.where(plan[e, 0] == group, v, jnp.zeros_like(v))


def per_device(tokens, gain, q_weight, key_value_weight, q_bias, kv_bias, plan, home_offsets):
    bf = jnp.bfloat16
    f32 = jnp.float32
    blocks = call(
        cut,
        [((28, COLS), bf)] * 4,
        (q_weight, key_value_weight),
        [ANY] * 2,
        [
            pltpu.VMEM((28, 2048), bf),
            pltpu.VMEM((28, 768), bf),
            pltpu.SemaphoreType.DMA((2,)),
        ],
        grant=60,
    )
    got = [blocks[0]] + [send(blocks[j], along_x(j)) for j in (1, 2, 3)]
    (w0,) = call(place, [((112, COLS), bf)], got, scratch=[pltpu.VMEM((4, 28, COLS), f32)])
    (n0,) = call(norm, [((64, 3584), bf)], (tokens, gain, w0), [VM, VM, ANY])
    (s0,) = call(
        stage,
        [((4, 112, COLS), bf)],
        (w0, *[send(w0, along_first(-j)) for j in (1, 2, 3)], n0),
        [VM] * 4 + [ANY],
    )
    n1 = send(n0, along_x(-1))
    n3 = send(n0, along_x(1))
    s1 = send(s0, along_second(-1))
    s3 = send(s0, along_second(1))
    own1, r1, r3, low, high = call(
        relay,
        [((12, 112, COLS), bf)] + [((2, 112, COLS), bf)] * 2 + [((32, 3584), bf)] * 2,
        (s0, s1, s3, n1, n3),
    )
    n2a = send(low, along_x(-1))
    n2b = send(high, along_x(1))
    s2a = send(r1, along_second(-1))
    s2b = send(r3, along_second(1))
    other1 = send(own1, other_core)
    (own2,) = call(
        join2, [((4, 112, COLS), bf)], (s2a, s2b, n2a, n2b), [VM] * 2 + [ANY] * 2
    )
    other2 = send(own2, other_core)
    w, x_all, cs, qb, kvb = call(
        gather,
        [
            ((32, 112, COLS), bf),
            ((ROW_TOK, 3584), bf),
            ((ROW_TOK, HEAD), f32),
            ((512,), f32),
            ((2, HEAD), f32),
        ],
        (
            home_offsets, own1, own2, other1, n0, n1, n2a, n2b, n3,
            jnp.asarray(rotary_table()), q_bias, kv_bias,
        ),
        [SM] + [VM] * 8 + [ANY] * 3,
        [pltpu.SemaphoreType.DMA((7,))],
    )
    _, kv, q = call(
        project,
        [((32, 112, COLS), bf), ((ROW_TOK, 256), bf), ((ROW_TOK, 512), bf)],
        (w, other2, x_all, cs, qb, kvb),
        input_output_aliases={0: 0},
    )

    a = [kv] + [send(kv, along_y(-j)) for j in (1, 2, 3)]
    b = [send(v, pair_x) for v in a]
    rows = call(cache_rows, [((64, 256), bf)] * 4, a)
    (mine,) = call(
        cache_heads,
        [((64, 768), bf)],
        (rows[0], *[send(rows[j], along_x(j)) for j in (1, 2, 3)]),
        scratch=[pltpu.VMEM((4, 64, 256), bf)],
    )
    outs = call(
        attend,
        [((64, 512), bf)] * 4,
        (home_offsets, q, *a, *b, mine),
        [SM] + [VM] * 9 + [ANY],
        [pltpu.VMEM((ROW_TOK, 1024), f32), pltpu.VMEM((ROW_TOK, 512), bf)],
    )
    (attended,) = call(
        merge, [((64, 2048), bf)], (outs[0], *[send(outs[j], along_x(j)) for j in (1, 2, 3)])
    )
    (cached,) = call(
        cache_join,
        [((4, 64, 768), bf)],
        (mine, *[send(mine, along_z(-j)) for j in (1, 2, 3)], outs[0]),
        [VM] * 4 + [ANY],
    )
    (cache,) = call(
        cache_write,
        [((1, 1, 512, 768), bf)],
        (plan, cached, send(cached, other_core)),
        [SM, VM, VM],
    )
    return attended, cache


def solution(mesh):
    fine = Mesh(mesh.devices.reshape(SIZES), EVERY)
    in_specs = (P(EVERY, None), P(), P(EVERY, None), P(EVERY, None), P(), P(), P(), P())
    out_specs = (P(EVERY, None), P(("z", "core"), ("y", "x"), None, None))
    return jax.shard_map(
        per_device, mesh=fine, in_specs=in_specs, out_specs=out_specs, check_vma=False
    )
```

```python
import functools

import jax
import jax.numpy as jnp
import numpy as np
from jax import lax
from jax.experimental import pallas as pl
from jax.experimental.pallas import tpu as pltpu
from jax.sharding import Mesh
from jax.sharding import PartitionSpec as P

HEAD = 128
NEG = -1e30
ROW_TOK = 256
COLS = 768

EVERY = ("z", "core", "y", "x")
SIZES = (4, 2, 4, 4)
VM = pl.BlockSpec(memory_space=pltpu.VMEM)
SM = pl.BlockSpec(memory_space=pltpu.SMEM)
ANY = pl.BlockSpec(memory_space=pl.ANY)


def rotary_table():
    angles = np.arange(1024)[:, None] * 1000000.0 ** (-np.arange(64) * 2.0 / HEAD)[None, :]
    return np.concatenate([np.cos(angles), np.sin(angles)], axis=1).astype(np.float32)


def flat(z, c, y, x):
    return ((z % 4 * 2 + c % 2) * 4 + y % 4) * 4 + x % 4


PLACES = [(z, c, y, x) for z in range(4) for c in range(2) for y in range(4) for x in range(4)]


def send(v, move):
    return lax.ppermute(v, EVERY, [(flat(*p), flat(*move(*p))) for p in PLACES])


def along_x(j):
    return lambda z, c, y, x: (z, c, y, x + j)


def along_z(j):
    return lambda z, c, y, x: (z + j, c, y, x)


def along_second(j):
    return lambda z, c, y, x: (z, c, y + j, x) if c == 0 else (z + j, c, y, x)


GROUPS = [[flat(z, 0, y, x) for z in range(4) for x in range(4)] for y in range(4)] + [
    [flat(z, 1, y, x) for y in range(4) for x in range(4)] for z in range(4)
]


def other_core(z, c, y, x):
    return (z, 1 - c, y, x)


def along_y(j):
    return lambda z, c, y, x: (z, c, y + j, x)


def pair_x(z, c, y, x):
    return (z, c, y, x ^ 1)


def call(kernel, outs, operands, in_specs=None, scratch=(), grant=20, **more):
    outs = tuple(jax.ShapeDtypeStruct(s, d) for s, d in outs)
    return pl.pallas_call(
        kernel,
        out_shape=outs,
        in_specs=[VM] * len(operands) if in_specs is None else in_specs,
        out_specs=(VM,) * len(outs),
        scratch_shapes=list(scratch),
        compiler_params=pltpu.CompilerParams(vmem_limit_bytes=grant * 1024 * 1024),
        name=kernel.__name__,
        **more,
    )(*operands)


def cut(wq, wkv, out, q_buf, kv_buf, sem):
    copies = [
        pltpu.make_async_copy(wq, q_buf, sem.at[0]),
        pltpu.make_async_copy(wkv, kv_buf, sem.at[1]),
    ]
    for copy in copies:
        copy.start()
    for copy in copies:
        copy.wait()
    for n in range(16):
        to = n % 4
        slot = (to + 1) // 2
        for k in range(2):
            low = (slot + 3 * k) * HEAD
            out[n, :, k * HEAD : (k + 1) * HEAD] = kv_buf[:, low : low + HEAD]
        out[n, :, 256:] = q_buf[:, to * 512 : (to + 1) * 512]


def norm(tokens, gain, after, out):
    floats = tokens[...].astype(jnp.float32)
    mean = jnp.mean(floats * floats, axis=1, keepdims=True)
    out[...] = (floats * lax.rsqrt(mean + 1e-06) * gain[...][None, :]).astype(jnp.bfloat16)


def stage(got, n1, n3, kv0, q0, low, high):
    for i in range(4):
        rows = [got[4 * i + k].astype(jnp.float32) for k in range(4)]
        piece = jnp.concatenate(rows, axis=0).astype(jnp.bfloat16)
        kv0[i] = piece[:, :256]
        q0[i] = piece[:, 256:]
    low[...] = n1[:32, :]
    high[...] = n3[32:, :]


def kv_join(k0, k1, k2, k3, q_in, after1, after2, own, q_out):
    for n, k in enumerate((k0, k1, k2, k3)):
        own[4 * n : 4 * n + 4] = k[...]
    q_out[...] = q_in[...]


def q_relay(q1, q3, after, r1, r3):
    r1[...] = q1[:2]
    r3[...] = q3[2:]


def q_join(q0, q1, q2a, q2b, q3, own):
    low = 0
    for q in (q0, q1, q2a, q2b, q3):
        own[low : low + q.shape[0]] = q[...]
        low += q.shape[0]


def load_weights(ref, t, buf):
    y = lax.axis_index("y")
    z = lax.axis_index("z")
    for j in range(4):
        for i in range(4):
            zz = jnp.where(t == 0, i, lax.rem(z + j, 4))
            yy = jnp.where(t == 0, lax.rem(y + j, 4), i)
            buf[(2 * zz + t) * 4 + yy] = ref[4 * j + i]


def gather(
    offsets, own, n0, n1, n2a, n2b, n3, table, qb, kvb, w, x_out, cs, qb_out, kvb_out, sem
):
    e = 2 * lax.axis_index("z") + lax.axis_index("core")
    y = lax.axis_index("y")
    x = lax.axis_index("x")
    copies = []
    for k in range(4):
        s = 4 * y + k
        row = pl.multiple_of((s - offsets[e, s]) * 64, 64)
        copies.append(
            pltpu.make_async_copy(
                table.at[pl.ds(row, 64), :], cs.at[k * 64 : (k + 1) * 64, :], sem.at[k]
            )
        )
    copies.append(
        pltpu.make_async_copy(qb.at[pl.ds(pl.multiple_of(x * 512, 512), 512)], qb_out, sem.at[4])
    )
    slot = lax.div(x + 1, 2)
    for n in range(2):
        low = pl.multiple_of((slot + 3 * n) * HEAD, HEAD)
        copies.append(
            pltpu.make_async_copy(kvb.at[pl.ds(low, HEAD)], kvb_out.at[n], sem.at[5 + n])
        )
    for copy in copies:
        copy.start()
    for ref, j, low, size in (
        (n0, 0, 0, 64),
        (n1, 1, 0, 64),
        (n2a, 2, 0, 32),
        (n2b, 2, 32, 32),
        (n3, 3, 0, 64),
    ):
        row = pl.multiple_of(lax.rem(x + j, 4) * 64 + low, 32)
        x_out[pl.ds(row, size), :] = ref[...]
    load_weights(own, lax.axis_index("core"), w)
    for copy in copies:
        copy.wait()


def q_gather(own, w):
    load_weights(own, lax.axis_index("core"), w)


def rotate(v, cos, sin):
    a = v[:, :64]
    b = v[:, 64:]
    return jnp.concatenate([a * cos - b * sin, b * cos + a * sin], axis=1).astype(jnp.bfloat16)


def kv_project(w_in, other, x_in, cs, kvb, w, kv):
    del w_in
    load_weights(other, 1 - lax.axis_index("core"), w)
    acc = jnp.dot(x_in[...], w[...].reshape(3584, 256), preferred_element_type=jnp.float32)
    kv[:, :HEAD] = rotate(acc[:, :HEAD] + kvb[0][None, :], cs[:, :64], cs[:, 64:])
    kv[:, HEAD:] = (acc[:, HEAD:] + kvb[1][None, :]).astype(jnp.bfloat16)


def q_project(w_in, other, x_in, cs, qb, w, q):
    del w_in
    load_weights(other, 1 - lax.axis_index("core"), w)
    for g in range(2):
        part = slice(g * 256, (g + 1) * 256)
        acc = jnp.dot(
            x_in[...], w[:, :, part].reshape(3584, 256), preferred_element_type=jnp.float32
        )
        for h in range(2):
            low = (2 * g + h) * HEAD
            head = acc[:, h * HEAD : (h + 1) * HEAD] + qb[low : low + HEAD][None, :]
            q[:, low : low + HEAD] = rotate(head, cs[:, :64], cs[:, 64:])


def attend(offsets, q, a0, a1, a2, a3, b0, b1, b2, b3, after, o0, o1, o2, o3, mask, full):
    x = lax.axis_index("x")
    y = lax.axis_index("y")
    e = 2 * lax.axis_index("z") + lax.axis_index("core")
    qi = lax.broadcasted_iota(jnp.int32, (ROW_TOK, ROW_TOK), 0)
    ki = lax.broadcasted_iota(jnp.int32, (ROW_TOK, ROW_TOK), 1)
    starts = [offsets[e, 4 * y + k] * 64 for k in range(4)]
    start = jnp.where(
        qi < 128,
        jnp.where(qi < 64, starts[0], starts[1]),
        jnp.where(qi < 192, starts[2], starts[3]),
    )
    for j in range(4):
        key = ki + lax.rem(y + j, 4) * ROW_TOK
        ok = (key >= start) & (key <= qi + y * ROW_TOK)
        mask[:, j * ROW_TOK : (j + 1) * ROW_TOK] = jnp.where(ok, 0.0, NEG)

    for h in range(4):
        left = (x == 1) if h == 2 else ((x == 1) | (x == 3))
        pick = jnp.where(left, 1, 0) if h < 3 else 0
        qh = q[:, h * HEAD : (h + 1) * HEAD]
        parts = []
        vals = []
        for j, (pa, pb) in enumerate(((a0, b0), (a1, b1), (a2, b2), (a3, b3))):
            kv = jnp.where(pick == 1, pb[...], pa[...]) if h < 3 else pa[...]
            s = lax.dot_general(
                qh, kv[:, :HEAD], (((1,), (1,)), ((), ())), preferred_element_type=jnp.float32
            )
            parts.append(s * (HEAD**-0.5) + mask[:, j * ROW_TOK : (j + 1) * ROW_TOK])
            vals.append(kv[:, HEAD:])
        top = functools.reduce(jnp.maximum, [jnp.max(s, axis=1, keepdims=True) for s in parts])
        mass = jnp.zeros((ROW_TOK, 1), jnp.float32)
        acc = jnp.zeros((ROW_TOK, HEAD), jnp.float32)
        for s, v in zip(parts, vals):
            p = jnp.exp(s - top)
            mass += jnp.sum(p, axis=1, keepdims=True)
            acc += jnp.dot(p.astype(jnp.bfloat16), v, preferred_element_type=jnp.float32)
        full[:, h * HEAD : (h + 1) * HEAD] = (acc / mass).astype(jnp.bfloat16)
    for j, o in enumerate((o0, o1, o2, o3)):
        o[...] = full[pl.ds(pl.multiple_of(lax.rem(x + j, 4) * 64, 64), 64), :]


def merge(r0, r1, r2, r3, out):
    x = lax.axis_index("x")
    for j, r in enumerate((r0, r1, r2, r3)):
        low = pl.multiple_of(lax.rem(x + 4 - j, 4) * 512, 512)
        out[:, pl.ds(low, 512)] = r[...]


def cache_rows(a0, a1, a2, a3, t0, t1, t2, t3):
    x = lax.axis_index("x")
    y = lax.axis_index("y")
    i = lax.broadcasted_iota(jnp.int32, (64, ROW_TOK), 0)
    t = lax.broadcasted_iota(jnp.int32, (64, ROW_TOK), 1)
    want = 16 * lax.rem(i, 16) + 4 * y + lax.rem(x + lax.div(i, 16), 4)
    select = jnp.where(t == want, 1.0, 0.0).astype(jnp.bfloat16)
    for j, a in enumerate((a0, a1, a2, a3)):
        got = jnp.dot(select, a[...], preferred_element_type=jnp.float32).astype(jnp.bfloat16)
        rows = pl.ds(pl.multiple_of(lax.rem(y + j, 4) * 16, 16), 16)
        for k, out in enumerate((t0, t1, t2, t3)):
            out[rows, :] = got[16 * k : 16 * k + 16]


def cache_heads(t0, t1, t2, t3, out, buf):
    x = lax.axis_index("x")
    for j, t in enumerate((t0, t1, t2, t3)):
        buf[lax.rem(x + 4 - j, 4)] = t[...]
    for k, src in enumerate((0, 1, 3)):
        out[:, k * HEAD : (k + 1) * HEAD] = buf[src, :, :HEAD]
        out[:, (3 + k) * HEAD : (4 + k) * HEAD] = buf[src, :, HEAD:]


def cache_join(c0, c1, c2, c3, after, out):
    for n, c in enumerate((c0, c1, c2, c3)):
        out[n] = c[...]


def cache_zero(out, buf, sem):
    buf[...] = jnp.zeros(buf.shape, buf.dtype)
    copies = [
        pltpu.make_async_copy(buf, out.at[0, 0, pl.ds(64 * e, 64), :], sem.at[e]) for e in range(8)
    ]
    for copy in copies:
        copy.start()
    for copy in copies:
        copy.wait()


def cache_write(plan, own, other, zeros, out, sem):
    del zeros
    z = lax.axis_index("z")
    core = lax.axis_index("core")
    group = 2 * z + core
    steps = []
    for ref, t in ((own, core), (other, 1 - core)):
        for j in range(4):
            e = 2 * lax.rem(z + j, 4) + t
            rows = pl.ds(pl.multiple_of(e * 64, 64), 64)
            copy = pltpu.make_async_copy(ref.at[j], out.at[0, 0, rows, :], sem.at[len(steps)])
            steps.append((plan[e, 0] == group, copy))
    for hit, copy in steps:
        pl.when(hit)(copy.start)
    for hit, copy in steps:
        pl.when(hit)(copy.wait)


def per_device(tokens, gain, q_weight, key_value_weight, q_bias, kv_bias, plan, home_offsets):
    bf = jnp.bfloat16
    f32 = jnp.float32
    (w,) = call(
        cut,
        [((16, 28, COLS), bf)],
        (q_weight, key_value_weight),
        [ANY] * 2,
        [
            pltpu.VMEM((28, 2048), bf),
            pltpu.VMEM((28, 768), bf),
            pltpu.SemaphoreType.DMA((2,)),
        ],
        grant=60,
    )
    (n0,) = call(norm, [((64, 3584), bf)], (tokens, gain, w), [VM, VM, ANY])
    n1 = send(n0, along_x(-1))
    n3 = send(n0, along_x(1))
    got = lax.all_to_all(w, EVERY, 0, 0, axis_index_groups=GROUPS, tiled=True)
    kv0, q0, low, high = call(
        stage,
        [((4, 112, 256), bf), ((4, 112, 512), bf)] + [((32, 3584), bf)] * 2,
        (got, n1, n3),
    )
    n2a = send(low, along_x(-1))
    n2b = send(high, along_x(1))
    own_kv, q0 = call(
        kv_join,
        [((16, 112, 256), bf), ((4, 112, 512), bf)],
        (kv0, *[send(kv0, along_second(-j)) for j in (1, 2, 3)], q0, n2a, n2b),
        [VM] * 5 + [ANY] * 2,
    )
    other_kv = send(own_kv, other_core)
    q1 = send(q0, along_second(-1))
    q3 = send(q0, along_second(1))
    w, x_all, cs, qb, kvb = call(
        gather,
        [
            ((32, 112, 256), bf),
            ((ROW_TOK, 3584), bf),
            ((ROW_TOK, HEAD), f32),
            ((512,), f32),
            ((2, HEAD), f32),
        ],
        (home_offsets, own_kv, n0, n1, n2a, n2b, n3, jnp.asarray(rotary_table()), q_bias, kv_bias),
        [SM] + [VM] * 6 + [ANY] * 3,
        [pltpu.SemaphoreType.DMA((7,))],
    )
    _, kv = call(
        kv_project,
        [((32, 112, 256), bf), ((ROW_TOK, 256), bf)],
        (w, other_kv, x_all, cs, kvb),
        input_output_aliases={0: 0},
    )
    r1, r3 = call(q_relay, [((2, 112, 512), bf)] * 2, (q1, q3, kv), [VM] * 2 + [ANY])
    q2a = send(r1, along_second(-1))
    q2b = send(r3, along_second(1))
    (own_q,) = call(q_join, [((16, 112, 512), bf)], (q0, q1, q2a, q2b, q3))
    other_q = send(own_q, other_core)
    (w,) = call(q_gather, [((32, 112, 512), bf)], (own_q,))
    _, q = call(
        q_project,
        [((32, 112, 512), bf), ((ROW_TOK, 512), bf)],
        (w, other_q, x_all, cs, qb),
        input_output_aliases={0: 0},
    )

    a = [kv] + [send(kv, along_y(-j)) for j in (1, 2, 3)]
    b = [send(v, pair_x) for v in a]
    rows = call(cache_rows, [((64, 256), bf)] * 4, a)
    (mine,) = call(
        cache_heads,
        [((64, 768), bf)],
        (rows[0], *[send(rows[j], along_x(j)) for j in (1, 2, 3)]),
        scratch=[pltpu.VMEM((4, 64, 256), bf)],
    )
    outs = call(
        attend,
        [((64, 512), bf)] * 4,
        (home_offsets, q, *a, *b, mine),
        [SM] + [VM] * 9 + [ANY],
        [pltpu.VMEM((ROW_TOK, 1024), f32), pltpu.VMEM((ROW_TOK, 512), bf)],
    )
    (attended,) = call(
        merge, [((64, 2048), bf)], (outs[0], *[send(outs[j], along_x(j)) for j in (1, 2, 3)])
    )
    (cached,) = call(
        cache_join,
        [((4, 64, 768), bf)],
        (mine, *[send(mine, along_z(-j)) for j in (1, 2, 3)], outs[0]),
        [VM] * 4 + [ANY],
    )
    whole = jax.ShapeDtypeStruct((1, 1, 512, 768), bf)
    zeros = pl.pallas_call(
        cache_zero,
        out_shape=whole,
        out_specs=ANY,
        scratch_shapes=[pltpu.VMEM((64, 768), bf), pltpu.SemaphoreType.DMA((8,))],
        name="cache_zero",
    )()
    cache = pl.pallas_call(
        cache_write,
        out_shape=whole,
        in_specs=[SM, VM, VM, ANY],
        out_specs=ANY,
        scratch_shapes=[pltpu.SemaphoreType.DMA((8,))],
        input_output_aliases={3: 0},
        name="cache_write",
    )(plan, cached, send(cached, other_core), zeros)
    return attended, cache


def solution(mesh):
    fine = Mesh(mesh.devices.reshape(SIZES), EVERY)
    in_specs = (P(EVERY, None), P(), P(EVERY, None), P(EVERY, None), P(), P(), P(), P())
    out_specs = (P(EVERY, None), P(("z", "core"), ("y", "x"), None, None))
    return jax.shard_map(
        per_device, mesh=fine, in_specs=in_specs, out_specs=out_specs, check_vma=False
    )
```

```python
import functools

import jax
import jax.numpy as jnp
import numpy as np
from jax import lax
from jax.experimental import pallas as pl
from jax.experimental.pallas import tpu as pltpu
from jax.sharding import Mesh
from jax.sharding import PartitionSpec as P

HEAD = 128
NEG = -1e30
ROW_TOK = 256
COLS = 768

EVERY = ("z", "core", "y", "x")
SIZES = (4, 2, 4, 4)
VM = pl.BlockSpec(memory_space=pltpu.VMEM)
SM = pl.BlockSpec(memory_space=pltpu.SMEM)
ANY = pl.BlockSpec(memory_space=pl.ANY)


def rotary_table():
    angles = np.arange(1024)[:, None] * 1000000.0 ** (-np.arange(64) * 2.0 / HEAD)[None, :]
    return np.concatenate([np.cos(angles), np.sin(angles)], axis=1).astype(np.float32)


def flat(z, c, y, x):
    return ((z % 4 * 2 + c % 2) * 4 + y % 4) * 4 + x % 4


PLACES = [(z, c, y, x) for z in range(4) for c in range(2) for y in range(4) for x in range(4)]


def send(v, move):
    return lax.ppermute(v, EVERY, [(flat(*p), flat(*move(*p))) for p in PLACES])


def along_x(j):
    return lambda z, c, y, x: (z, c, y, x + j)


def along_z(j):
    return lambda z, c, y, x: (z + j, c, y, x)


def along_second(j):
    return lambda z, c, y, x: (z, c, y + j, x) if c == 0 else (z + j, c, y, x)


def along_first(j):
    return lambda z, c, y, x: (z + j, c, y, x) if c == 0 else (z, c, y + j, x)


def other_core(z, c, y, x):
    return (z, 1 - c, y, x)


def along_y(j):
    return lambda z, c, y, x: (z, c, y + j, x)


def pair_x(z, c, y, x):
    return (z, c, y, x ^ 1)


def call(kernel, outs, operands, in_specs=None, scratch=(), grant=20, **more):
    outs = tuple(jax.ShapeDtypeStruct(s, d) for s, d in outs)
    return pl.pallas_call(
        kernel,
        out_shape=outs,
        in_specs=[VM] * len(operands) if in_specs is None else in_specs,
        out_specs=(VM,) * len(outs),
        scratch_shapes=list(scratch),
        compiler_params=pltpu.CompilerParams(vmem_limit_bytes=grant * 1024 * 1024),
        name=kernel.__name__,
        **more,
    )(*operands)


def cut(wq, wkv, b0, b1, b2, b3, q_buf, kv_buf, sem):
    copies = [
        pltpu.make_async_copy(wq, q_buf, sem.at[0]),
        pltpu.make_async_copy(wkv, kv_buf, sem.at[1]),
    ]
    for copy in copies:
        copy.start()
    for copy in copies:
        copy.wait()
    x = lax.axis_index("x")
    for j, block in enumerate((b0, b1, b2, b3)):
        to = lax.rem(x + j, 4)
        slot = lax.div(to + 1, 2)
        for n in range(2):
            low = pl.multiple_of((slot + 3 * n) * HEAD, HEAD)
            block[:, n * HEAD : (n + 1) * HEAD] = kv_buf[:, pl.ds(low, HEAD)]
        block[:, 256:] = q_buf[:, pl.ds(pl.multiple_of(to * 512, 512), 512)]


def place(p0, p1, p2, p3, out, buf):
    x = lax.axis_index("x")
    for j, p in enumerate((p0, p1, p2, p3)):
        buf[lax.rem(x + 4 - j, 4)] = p[...].astype(jnp.float32)
    out[...] = jnp.concatenate([buf[k] for k in range(4)], axis=0).astype(jnp.bfloat16)


def norm(tokens, gain, after, out):
    floats = tokens[...].astype(jnp.float32)
    mean = jnp.mean(floats * floats, axis=1, keepdims=True)
    out[...] = (floats * lax.rsqrt(mean + 1e-06) * gain[...][None, :]).astype(jnp.bfloat16)


def stage(s0, s1, s2, s3, n1, n3, kv0, q0, low, high):
    for i, s in enumerate((s0, s1, s2, s3)):
        kv0[i] = s[:, :256]
        q0[i] = s[:, 256:]
    low[...] = n1[:32, :]
    high[...] = n3[32:, :]


def kv_join(k0, k1, k2, k3, q_in, after1, after2, own, q_out):
    for n, k in enumerate((k0, k1, k2, k3)):
        own[4 * n : 4 * n + 4] = k[...]
    q_out[...] = q_in[...]


def q_relay(q1, q3, after1, after2, after3, r1, r3):
    r1[...] = q1[:2]
    r3[...] = q3[2:]


def q_join(q0, q1, q2a, q2b, q3, after1, after2, after3, after4, own):
    low = 0
    for q in (q0, q1, q2a, q2b, q3):
        own[low : low + q.shape[0]] = q[...]
        low += q.shape[0]


def load_weights(ref, t, buf):
    y = lax.axis_index("y")
    z = lax.axis_index("z")
    for j in range(4):
        for i in range(4):
            zz = lax.rem(z + jnp.where(t == 0, i, j), 4)
            yy = lax.rem(y + jnp.where(t == 0, j, i), 4)
            buf[(2 * zz + t) * 4 + yy] = ref[4 * j + i]


def gather(
    offsets, own, n0, n1, n2a, n2b, n3, table, qb, kvb, w, x_out, cs, qb_out, kvb_out, sem
):
    e = 2 * lax.axis_index("z") + lax.axis_index("core")
    y = lax.axis_index("y")
    x = lax.axis_index("x")
    copies = []
    for k in range(4):
        s = 4 * y + k
        row = pl.multiple_of((s - offsets[e, s]) * 64, 64)
        copies.append(
            pltpu.make_async_copy(
                table.at[pl.ds(row, 64), :], cs.at[k * 64 : (k + 1) * 64, :], sem.at[k]
            )
        )
    copies.append(
        pltpu.make_async_copy(qb.at[pl.ds(pl.multiple_of(x * 512, 512), 512)], qb_out, sem.at[4])
    )
    slot = lax.div(x + 1, 2)
    for n in range(2):
        low = pl.multiple_of((slot + 3 * n) * HEAD, HEAD)
        copies.append(
            pltpu.make_async_copy(kvb.at[pl.ds(low, HEAD)], kvb_out.at[n], sem.at[5 + n])
        )
    for copy in copies:
        copy.start()
    for ref, j, low, size in (
        (n0, 0, 0, 64),
        (n1, 1, 0, 64),
        (n2a, 2, 0, 32),
        (n2b, 2, 32, 32),
        (n3, 3, 0, 64),
    ):
        row = pl.multiple_of(lax.rem(x + j, 4) * 64 + low, 32)
        x_out[pl.ds(row, size), :] = ref[...]
    load_weights(own, lax.axis_index("core"), w)
    for copy in copies:
        copy.wait()


def q_gather(own, w):
    load_weights(own, lax.axis_index("core"), w)


def rotate(v, cos, sin):
    a = v[:, :64]
    b = v[:, 64:]
    return jnp.concatenate([a * cos - b * sin, b * cos + a * sin], axis=1).astype(jnp.bfloat16)


def kv_project(w_in, other, x_in, cs, kvb, w, kv):
    del w_in
    load_weights(other, 1 - lax.axis_index("core"), w)
    acc = jnp.dot(x_in[...], w[...].reshape(3584, 256), preferred_element_type=jnp.float32)
    kv[:, :HEAD] = rotate(acc[:, :HEAD] + kvb[0][None, :], cs[:, :64], cs[:, 64:])
    kv[:, HEAD:] = (acc[:, HEAD:] + kvb[1][None, :]).astype(jnp.bfloat16)


def q_project(w_in, other, x_in, cs, qb, w, q):
    del w_in
    load_weights(other, 1 - lax.axis_index("core"), w)
    for g in range(2):
        part = slice(g * 256, (g + 1) * 256)
        acc = jnp.dot(
            x_in[...], w[:, :, part].reshape(3584, 256), preferred_element_type=jnp.float32
        )
        for h in range(2):
            low = (2 * g + h) * HEAD
            head = acc[:, h * HEAD : (h + 1) * HEAD] + qb[low : low + HEAD][None, :]
            q[:, low : low + HEAD] = rotate(head, cs[:, :64], cs[:, 64:])


def attend(offsets, q, a0, a1, a2, a3, b0, b1, b2, b3, after, o0, o1, o2, o3, mask, full):
    x = lax.axis_index("x")
    y = lax.axis_index("y")
    e = 2 * lax.axis_index("z") + lax.axis_index("core")
    qi = lax.broadcasted_iota(jnp.int32, (ROW_TOK, ROW_TOK), 0)
    ki = lax.broadcasted_iota(jnp.int32, (ROW_TOK, ROW_TOK), 1)
    starts = [offsets[e, 4 * y + k] * 64 for k in range(4)]
    start = jnp.where(
        qi < 128,
        jnp.where(qi < 64, starts[0], starts[1]),
        jnp.where(qi < 192, starts[2], starts[3]),
    )
    for j in range(4):
        key = ki + lax.rem(y + j, 4) * ROW_TOK
        ok = (key >= start) & (key <= qi + y * ROW_TOK)
        mask[:, j * ROW_TOK : (j + 1) * ROW_TOK] = jnp.where(ok, 0.0, NEG)

    for h in range(4):
        left = (x == 1) if h == 2 else ((x == 1) | (x == 3))
        pick = jnp.where(left, 1, 0) if h < 3 else 0
        qh = q[:, h * HEAD : (h + 1) * HEAD]
        parts = []
        vals = []
        for j, (pa, pb) in enumerate(((a0, b0), (a1, b1), (a2, b2), (a3, b3))):
            kv = jnp.where(pick == 1, pb[...], pa[...]) if h < 3 else pa[...]
            s = lax.dot_general(
                qh, kv[:, :HEAD], (((1,), (1,)), ((), ())), preferred_element_type=jnp.float32
            )
            parts.append(s * (HEAD**-0.5) + mask[:, j * ROW_TOK : (j + 1) * ROW_TOK])
            vals.append(kv[:, HEAD:])
        top = functools.reduce(jnp.maximum, [jnp.max(s, axis=1, keepdims=True) for s in parts])
        mass = jnp.zeros((ROW_TOK, 1), jnp.float32)
        acc = jnp.zeros((ROW_TOK, HEAD), jnp.float32)
        for s, v in zip(parts, vals):
            p = jnp.exp(s - top)
            mass += jnp.sum(p, axis=1, keepdims=True)
            acc += jnp.dot(p.astype(jnp.bfloat16), v, preferred_element_type=jnp.float32)
        full[:, h * HEAD : (h + 1) * HEAD] = (acc / mass).astype(jnp.bfloat16)
    for j, o in enumerate((o0, o1, o2, o3)):
        o[...] = full[pl.ds(pl.multiple_of(lax.rem(x + j, 4) * 64, 64), 64), :]


def merge(r0, r1, r2, r3, out):
    x = lax.axis_index("x")
    for j, r in enumerate((r0, r1, r2, r3)):
        low = pl.multiple_of(lax.rem(x + 4 - j, 4) * 512, 512)
        out[:, pl.ds(low, 512)] = r[...]


def cache_rows(a0, a1, a2, a3, t0, t1, t2, t3):
    x = lax.axis_index("x")
    y = lax.axis_index("y")
    i = lax.broadcasted_iota(jnp.int32, (64, ROW_TOK), 0)
    t = lax.broadcasted_iota(jnp.int32, (64, ROW_TOK), 1)
    want = 16 * lax.rem(i, 16) + 4 * y + lax.rem(x + lax.div(i, 16), 4)
    select = jnp.where(t == want, 1.0, 0.0).astype(jnp.bfloat16)
    for j, a in enumerate((a0, a1, a2, a3)):
        got = jnp.dot(select, a[...], preferred_element_type=jnp.float32).astype(jnp.bfloat16)
        rows = pl.ds(pl.multiple_of(lax.rem(y + j, 4) * 16, 16), 16)
        for k, out in enumerate((t0, t1, t2, t3)):
            out[rows, :] = got[16 * k : 16 * k + 16]


def cache_heads(t0, t1, t2, t3, out, buf):
    x = lax.axis_index("x")
    for j, t in enumerate((t0, t1, t2, t3)):
        buf[lax.rem(x + 4 - j, 4)] = t[...]
    for k, src in enumerate((0, 1, 3)):
        out[:, k * HEAD : (k + 1) * HEAD] = buf[src, :, :HEAD]
        out[:, (3 + k) * HEAD : (4 + k) * HEAD] = buf[src, :, HEAD:]


def cache_join(c0, c1, c2, c3, after, out):
    for n, c in enumerate((c0, c1, c2, c3)):
        out[n] = c[...]


def cache_zero(out, buf, sem):
    buf[...] = jnp.zeros(buf.shape, buf.dtype)
    copies = [
        pltpu.make_async_copy(buf, out.at[0, 0, pl.ds(64 * e, 64), :], sem.at[e]) for e in range(8)
    ]
    for copy in copies:
        copy.start()
    for copy in copies:
        copy.wait()


def cache_write(plan, own, other, zeros, out, sem):
    del zeros
    z = lax.axis_index("z")
    core = lax.axis_index("core")
    group = 2 * z + core
    steps = []
    for ref, t in ((own, core), (other, 1 - core)):
        for j in range(4):
            e = 2 * lax.rem(z + j, 4) + t
            rows = pl.ds(pl.multiple_of(e * 64, 64), 64)
            copy = pltpu.make_async_copy(ref.at[j], out.at[0, 0, rows, :], sem.at[len(steps)])
            steps.append((plan[e, 0] == group, copy))
    for hit, copy in steps:
        pl.when(hit)(copy.start)
    for hit, copy in steps:
        pl.when(hit)(copy.wait)


def per_device(tokens, gain, q_weight, key_value_weight, q_bias, kv_bias, plan, home_offsets):
    bf = jnp.bfloat16
    f32 = jnp.float32
    blocks = call(
        cut,
        [((28, COLS), bf)] * 4,
        (q_weight, key_value_weight),
        [ANY] * 2,
        [
            pltpu.VMEM((28, 2048), bf),
            pltpu.VMEM((28, 768), bf),
            pltpu.SemaphoreType.DMA((2,)),
        ],
        grant=60,
    )
    got = [blocks[0]] + [send(blocks[j], along_x(j)) for j in (1, 2, 3)]
    (w0,) = call(place, [((112, COLS), bf)], got, scratch=[pltpu.VMEM((4, 28, COLS), f32)])
    w1, w2, w3 = [send(w0, along_first(-j)) for j in (1, 2, 3)]
    (n0,) = call(norm, [((64, 3584), bf)], (tokens, gain, w0), [VM, VM, ANY])
    n1 = send(n0, along_x(-1))
    n3 = send(n0, along_x(1))
    kv0, q0, low, high = call(
        stage,
        [((4, 112, 256), bf), ((4, 112, 512), bf)] + [((32, 3584), bf)] * 2,
        (w0, w1, w2, w3, n1, n3),
    )
    n2a = send(low, along_x(-1))
    n2b = send(high, along_x(1))
    own_kv, q0 = call(
        kv_join,
        [((16, 112, 256), bf), ((4, 112, 512), bf)],
        (kv0, *[send(kv0, along_second(-j)) for j in (1, 2, 3)], q0, n2a, n2b),
        [VM] * 5 + [ANY] * 2,
    )
    other_kv = send(own_kv, other_core)
    q1 = send(q0, along_second(-1))
    q3 = send(q0, along_second(1))
    w, x_all, cs, qb, kvb = call(
        gather,
        [
            ((32, 112, 256), bf),
            ((ROW_TOK, 3584), bf),
            ((ROW_TOK, HEAD), f32),
            ((512,), f32),
            ((2, HEAD), f32),
        ],
        (home_offsets, own_kv, n0, n1, n2a, n2b, n3, jnp.asarray(rotary_table()), q_bias, kv_bias),
        [SM] + [VM] * 6 + [ANY] * 3,
        [pltpu.SemaphoreType.DMA((7,))],
    )
    _, kv = call(
        kv_project,
        [((32, 112, 256), bf), ((ROW_TOK, 256), bf)],
        (w, other_kv, x_all, cs, kvb),
        input_output_aliases={0: 0},
    )
    a = [kv] + [send(kv, along_y(-j)) for j in (1, 2, 3)]
    b = [send(v, pair_x) for v in a]
    r1, r3 = call(q_relay, [((2, 112, 512), bf)] * 2, (q1, q3, *a[1:]), [VM] * 2 + [ANY] * 3)
    q2a = send(r1, along_second(-1))
    q2b = send(r3, along_second(1))
    rows = call(cache_rows, [((64, 256), bf)] * 4, a)
    (mine,) = call(
        cache_heads,
        [((64, 768), bf)],
        (rows[0], *[send(rows[j], along_x(j)) for j in (1, 2, 3)]),
        scratch=[pltpu.VMEM((4, 64, 256), bf)],
    )
    (own_q,) = call(
        q_join,
        [((16, 112, 512), bf)],
        (q0, q1, q2a, q2b, q3, mine, *b[1:]),
        [VM] * 5 + [ANY] * 4,
    )
    other_q = send(own_q, other_core)
    (w,) = call(q_gather, [((32, 112, 512), bf)], (own_q,))
    _, q = call(
        q_project,
        [((32, 112, 512), bf), ((ROW_TOK, 512), bf)],
        (w, other_q, x_all, cs, qb),
        input_output_aliases={0: 0},
    )
    outs = call(
        attend,
        [((64, 512), bf)] * 4,
        (home_offsets, q, *a, *b, mine),
        [SM] + [VM] * 9 + [ANY],
        [pltpu.VMEM((ROW_TOK, 1024), f32), pltpu.VMEM((ROW_TOK, 512), bf)],
    )
    (attended,) = call(
        merge, [((64, 2048), bf)], (outs[0], *[send(outs[j], along_x(j)) for j in (1, 2, 3)])
    )
    (cached,) = call(
        cache_join,
        [((4, 64, 768), bf)],
        (mine, *[send(mine, along_z(-j)) for j in (1, 2, 3)], outs[0]),
        [VM] * 4 + [ANY],
    )
    whole = jax.ShapeDtypeStruct((1, 1, 512, 768), bf)
    zeros = pl.pallas_call(
        cache_zero,
        out_shape=whole,
        out_specs=ANY,
        scratch_shapes=[pltpu.VMEM((64, 768), bf), pltpu.SemaphoreType.DMA((8,))],
        name="cache_zero",
    )()
    cache = pl.pallas_call(
        cache_write,
        out_shape=whole,
        in_specs=[SM, ANY, ANY, ANY],
        out_specs=ANY,
        scratch_shapes=[pltpu.SemaphoreType.DMA((8,))],
        input_output_aliases={3: 0},
        name="cache_write",
    )(plan, cached, send(cached, other_core), zeros)
    return attended, cache


def solution(mesh):
    fine = Mesh(mesh.devices.reshape(SIZES), EVERY)
    in_specs = (P(EVERY, None), P(), P(EVERY, None), P(EVERY, None), P(), P(), P(), P())
    out_specs = (P(EVERY, None), P(("z", "core"), ("y", "x"), None, None))
    return jax.shard_map(
        per_device, mesh=fine, in_specs=in_specs, out_specs=out_specs, check_vma=False
    )
```

```python
import functools

import jax
import jax.numpy as jnp
import numpy as np
from jax import lax
from jax.experimental import pallas as pl
from jax.experimental.pallas import tpu as pltpu
from jax.sharding import Mesh
from jax.sharding import PartitionSpec as P

HEAD = 128
NEG = -1e30
ROW_TOK = 256
COLS = 768

EVERY = ("z", "core", "y", "x")
SIZES = (4, 2, 4, 4)
VM = pl.BlockSpec(memory_space=pltpu.VMEM)
SM = pl.BlockSpec(memory_space=pltpu.SMEM)
ANY = pl.BlockSpec(memory_space=pl.ANY)


def rotary_table():
    angles = np.arange(1024)[:, None] * 1000000.0 ** (-np.arange(64) * 2.0 / HEAD)[None, :]
    return np.concatenate([np.cos(angles), np.sin(angles)], axis=1).astype(np.float32)


def flat(z, c, y, x):
    return ((z % 4 * 2 + c % 2) * 4 + y % 4) * 4 + x % 4


PLACES = [(z, c, y, x) for z in range(4) for c in range(2) for y in range(4) for x in range(4)]


def send(v, move):
    return lax.ppermute(v, EVERY, [(flat(*p), flat(*move(*p))) for p in PLACES])


def along_x(j):
    return lambda z, c, y, x: (z, c, y, x + j)


def along_z(j):
    return lambda z, c, y, x: (z + j, c, y, x)


def along_second(j):
    return lambda z, c, y, x: (z, c, y + j, x) if c == 0 else (z + j, c, y, x)


GROUPS = [[flat(z, 0, y, x) for z in range(4) for x in range(4)] for y in range(4)] + [
    [flat(z, 1, y, x) for y in range(4) for x in range(4)] for z in range(4)
]


def other_core(z, c, y, x):
    return (z, 1 - c, y, x)


def along_y(j):
    return lambda z, c, y, x: (z, c, y + j, x)


def pair_x(z, c, y, x):
    return (z, c, y, x ^ 1)


def call(kernel, outs, operands, in_specs=None, scratch=(), grant=20, **more):
    outs = tuple(jax.ShapeDtypeStruct(s, d) for s, d in outs)
    return pl.pallas_call(
        kernel,
        out_shape=outs,
        in_specs=[VM] * len(operands) if in_specs is None else in_specs,
        out_specs=(VM,) * len(outs),
        scratch_shapes=list(scratch),
        compiler_params=pltpu.CompilerParams(vmem_limit_bytes=grant * 1024 * 1024),
        name=kernel.__name__,
        **more,
    )(*operands)


def cut(wq, wkv, out, q_buf, kv_buf, sem):
    copies = [
        pltpu.make_async_copy(wq, q_buf, sem.at[0]),
        pltpu.make_async_copy(wkv, kv_buf, sem.at[1]),
    ]
    for copy in copies:
        copy.start()
    for copy in copies:
        copy.wait()
    for n in range(16):
        to = n % 4
        slot = (to + 1) // 2
        for k in range(2):
            low = (slot + 3 * k) * HEAD
            out[n, :, k * HEAD : (k + 1) * HEAD] = kv_buf[:, low : low + HEAD]
        out[n, :, 256:] = q_buf[:, to * 512 : (to + 1) * 512]


def norm(tokens, gain, after, out):
    floats = tokens[...].astype(jnp.float32)
    mean = jnp.mean(floats * floats, axis=1, keepdims=True)
    out[...] = (floats * lax.rsqrt(mean + 1e-06) * gain[...][None, :]).astype(jnp.bfloat16)


def stage(got, after, block):
    for i in range(4):
        rows = [got[4 * i + k].astype(jnp.float32) for k in range(4)]
        block[i] = jnp.concatenate(rows, axis=0).astype(jnp.bfloat16)


def relay(s0, s1, s3, n1, n3, joined, r1, r3, low, high):
    for n, s in enumerate((s0, s1, s3)):
        joined[4 * n : 4 * n + 4] = s[...]
    r1[...] = s1[:2]
    r3[...] = s3[2:]
    low[...] = n1[:32, :]
    high[...] = n3[32:, :]


def join2(a, b, after1, after2, out):
    out[:2] = a[...]
    out[2:] = b[...]


def load_weights(ref, t, places, buf):
    y = lax.axis_index("y")
    z = lax.axis_index("z")
    for n, (j, i) in enumerate(places):
        zz = jnp.where(t == 0, i, lax.rem(z + j, 4))
        yy = jnp.where(t == 0, lax.rem(y + j, 4), i)
        buf[(2 * zz + t) * 4 + yy] = ref[n]


FIRST = [(j, i) for j in (0, 1, 3) for i in range(4)]
LAST = [(2, i) for i in range(4)]


def gather(
    offsets, own1, own2, other1, n0, n1, n2a, n2b, n3, table, qb, kvb, w, x_out, cs, qb_out, kvb_out, sem
):
    e = 2 * lax.axis_index("z") + lax.axis_index("core")
    y = lax.axis_index("y")
    x = lax.axis_index("x")
    core = lax.axis_index("core")
    copies = []
    for k in range(4):
        s = 4 * y + k
        row = pl.multiple_of((s - offsets[e, s]) * 64, 64)
        copies.append(
            pltpu.make_async_copy(
                table.at[pl.ds(row, 64), :], cs.at[k * 64 : (k + 1) * 64, :], sem.at[k]
            )
        )
    copies.append(
        pltpu.make_async_copy(qb.at[pl.ds(pl.multiple_of(x * 512, 512), 512)], qb_out, sem.at[4])
    )
    slot = lax.div(x + 1, 2)
    for n in range(2):
        low = pl.multiple_of((slot + 3 * n) * HEAD, HEAD)
        copies.append(
            pltpu.make_async_copy(kvb.at[pl.ds(low, HEAD)], kvb_out.at[n], sem.at[5 + n])
        )
    for copy in copies:
        copy.start()
    for ref, j, low, size in (
        (n0, 0, 0, 64),
        (n1, 1, 0, 64),
        (n2a, 2, 0, 32),
        (n2b, 2, 32, 32),
        (n3, 3, 0, 64),
    ):
        row = pl.multiple_of(lax.rem(x + j, 4) * 64 + low, 32)
        x_out[pl.ds(row, size), :] = ref[...]
    load_weights(own1, core, FIRST, w)
    load_weights(own2, core, LAST, w)
    load_weights(other1, 1 - core, FIRST, w)
    for copy in copies:
        copy.wait()


def rotate(v, cos, sin):
    a = v[:, :64]
    b = v[:, 64:]
    return jnp.concatenate([a * cos - b * sin, b * cos + a * sin], axis=1).astype(jnp.bfloat16)


def kv_project(w_in, other2, x_in, cs, kvb, w, kv):
    del w_in
    load_weights(other2, 1 - lax.axis_index("core"), LAST, w)
    acc = jnp.dot(
        x_in[...], w[:, :, :256].reshape(3584, 256), preferred_element_type=jnp.float32
    )
    kv[:, :HEAD] = rotate(acc[:, :HEAD] + kvb[0][None, :], cs[:, :64], cs[:, 64:])
    kv[:, HEAD:] = (acc[:, HEAD:] + kvb[1][None, :]).astype(jnp.bfloat16)


def q_project(w, x_in, cs, qb, q):
    for g in range(2):
        part = slice((g + 1) * 256, (g + 2) * 256)
        acc = jnp.dot(
            x_in[...], w[:, :, part].reshape(3584, 256), preferred_element_type=jnp.float32
        )
        for h in range(2):
            low = (2 * g + h) * HEAD
            head = acc[:, h * HEAD : (h + 1) * HEAD] + qb[low : low + HEAD][None, :]
            q[:, low : low + HEAD] = rotate(head, cs[:, :64], cs[:, 64:])


def attend(offsets, q, a0, a1, a2, a3, b0, b1, b2, b3, after, o0, o1, o2, o3, mask, full):
    x = lax.axis_index("x")
    y = lax.axis_index("y")
    e = 2 * lax.axis_index("z") + lax.axis_index("core")
    qi = lax.broadcasted_iota(jnp.int32, (ROW_TOK, ROW_TOK), 0)
    ki = lax.broadcasted_iota(jnp.int32, (ROW_TOK, ROW_TOK), 1)
    starts = [offsets[e, 4 * y + k] * 64 for k in range(4)]
    start = jnp.where(
        qi < 128,
        jnp.where(qi < 64, starts[0], starts[1]),
        jnp.where(qi < 192, starts[2], starts[3]),
    )
    for j in range(4):
        key = ki + lax.rem(y + j, 4) * ROW_TOK
        ok = (key >= start) & (key <= qi + y * ROW_TOK)
        mask[:, j * ROW_TOK : (j + 1) * ROW_TOK] = jnp.where(ok, 0.0, NEG)

    for h in range(4):
        left = (x == 1) if h == 2 else ((x == 1) | (x == 3))
        pick = jnp.where(left, 1, 0) if h < 3 else 0
        qh = q[:, h * HEAD : (h + 1) * HEAD]
        parts = []
        vals = []
        for j, (pa, pb) in enumerate(((a0, b0), (a1, b1), (a2, b2), (a3, b3))):
            kv = jnp.where(pick == 1, pb[...], pa[...]) if h < 3 else pa[...]
            s = lax.dot_general(
                qh, kv[:, :HEAD], (((1,), (1,)), ((), ())), preferred_element_type=jnp.float32
            )
            parts.append(s * (HEAD**-0.5) + mask[:, j * ROW_TOK : (j + 1) * ROW_TOK])
            vals.append(kv[:, HEAD:])
        top = functools.reduce(jnp.maximum, [jnp.max(s, axis=1, keepdims=True) for s in parts])
        mass = jnp.zeros((ROW_TOK, 1), jnp.float32)
        acc = jnp.zeros((ROW_TOK, HEAD), jnp.float32)
        for s, v in zip(parts, vals):
            p = jnp.exp(s - top)
            mass += jnp.sum(p, axis=1, keepdims=True)
            acc += jnp.dot(p.astype(jnp.bfloat16), v, preferred_element_type=jnp.float32)
        full[:, h * HEAD : (h + 1) * HEAD] = (acc / mass).astype(jnp.bfloat16)
    for j, o in enumerate((o0, o1, o2, o3)):
        o[...] = full[pl.ds(pl.multiple_of(lax.rem(x + j, 4) * 64, 64), 64), :]


def merge(r0, r1, r2, r3, out):
    x = lax.axis_index("x")
    for j, r in enumerate((r0, r1, r2, r3)):
        low = pl.multiple_of(lax.rem(x + 4 - j, 4) * 512, 512)
        out[:, pl.ds(low, 512)] = r[...]


def cache_rows(a0, a1, a2, a3, t0, t1, t2, t3):
    x = lax.axis_index("x")
    y = lax.axis_index("y")
    i = lax.broadcasted_iota(jnp.int32, (64, ROW_TOK), 0)
    t = lax.broadcasted_iota(jnp.int32, (64, ROW_TOK), 1)
    want = 16 * lax.rem(i, 16) + 4 * y + lax.rem(x + lax.div(i, 16), 4)
    select = jnp.where(t == want, 1.0, 0.0).astype(jnp.bfloat16)
    for j, a in enumerate((a0, a1, a2, a3)):
        got = jnp.dot(select, a[...], preferred_element_type=jnp.float32).astype(jnp.bfloat16)
        rows = pl.ds(pl.multiple_of(lax.rem(y + j, 4) * 16, 16), 16)
        for k, out in enumerate((t0, t1, t2, t3)):
            out[rows, :] = got[16 * k : 16 * k + 16]


def cache_heads(t0, t1, t2, t3, out, buf):
    x = lax.axis_index("x")
    for j, t in enumerate((t0, t1, t2, t3)):
        buf[lax.rem(x + 4 - j, 4)] = t[...]
    for k, src in enumerate((0, 1, 3)):
        out[:, k * HEAD : (k + 1) * HEAD] = buf[src, :, :HEAD]
        out[:, (3 + k) * HEAD : (4 + k) * HEAD] = buf[src, :, HEAD:]


def cache_join(c0, c1, c2, c3, after, out):
    for n, c in enumerate((c0, c1, c2, c3)):
        out[n] = c[...]


def cache_write(plan, own, other, out):
    z = lax.axis_index("z")
    core = lax.axis_index("core")
    group = 2 * z + core
    for ref, t in ((own, core), (other, 1 - core)):
        for j in range(4):
            e = 2 * lax.rem(z + j, 4) + t
            rows = pl.ds(pl.multiple_of(e * 64, 64), 64)
            v = ref[j]
            out[0, 0, rows, :] = jnp.where(plan[e, 0] == group, v, jnp.zeros_like(v))


def per_device(tokens, gain, q_weight, key_value_weight, q_bias, kv_bias, plan, home_offsets):
    bf = jnp.bfloat16
    f32 = jnp.float32
    (w,) = call(
        cut,
        [((16, 28, COLS), bf)],
        (q_weight, key_value_weight),
        [ANY] * 2,
        [
            pltpu.VMEM((28, 2048), bf),
            pltpu.VMEM((28, 768), bf),
            pltpu.SemaphoreType.DMA((2,)),
        ],
        grant=60,
    )
    got = lax.all_to_all(w, EVERY, 0, 0, axis_index_groups=GROUPS, tiled=True)
    (n0,) = call(norm, [((64, 3584), bf)], (tokens, gain, w), [VM, VM, ANY])
    (s0,) = call(stage, [((4, 112, COLS), bf)], (got, n0), [VM, ANY])
    n1 = send(n0, along_x(-1))
    n3 = send(n0, along_x(1))
    s1 = send(s0, along_second(-1))
    s3 = send(s0, along_second(1))
    own1, r1, r3, low, high = call(
        relay,
        [((12, 112, COLS), bf)] + [((2, 112, COLS), bf)] * 2 + [((32, 3584), bf)] * 2,
        (s0, s1, s3, n1, n3),
    )
    n2a = send(low, along_x(-1))
    n2b = send(high, along_x(1))
    s2a = send(r1, along_second(-1))
    s2b = send(r3, along_second(1))
    other1 = send(own1, other_core)
    (own2,) = call(
        join2, [((4, 112, COLS), bf)], (s2a, s2b, n2a, n2b), [VM] * 2 + [ANY] * 2
    )
    other2 = send(own2, other_core)
    w, x_all, cs, qb, kvb = call(
        gather,
        [
            ((32, 112, COLS), bf),
            ((ROW_TOK, 3584), bf),
            ((ROW_TOK, HEAD), f32),
            ((512,), f32),
            ((2, HEAD), f32),
        ],
        (
            home_offsets, own1, own2, other1, n0, n1, n2a, n2b, n3,
            jnp.asarray(rotary_table()), q_bias, kv_bias,
        ),
        [SM] + [VM] * 8 + [ANY] * 3,
        [pltpu.SemaphoreType.DMA((7,))],
    )
    w, kv = call(
        kv_project,
        [((32, 112, COLS), bf), ((ROW_TOK, 256), bf)],
        (w, other2, x_all, cs, kvb),
        input_output_aliases={0: 0},
    )
    (q,) = call(q_project, [((ROW_TOK, 512), bf)], (w, x_all, cs, qb))

    a = [kv] + [send(kv, along_y(-j)) for j in (1, 2, 3)]
    b = [send(v, pair_x) for v in a]
    rows = call(cache_rows, [((64, 256), bf)] * 4, a)
    (mine,) = call(
        cache_heads,
        [((64, 768), bf)],
        (rows[0], *[send(rows[j], along_x(j)) for j in (1, 2, 3)]),
        scratch=[pltpu.VMEM((4, 64, 256), bf)],
    )
    outs = call(
        attend,
        [((64, 512), bf)] * 4,
        (home_offsets, q, *a, *b, mine),
        [SM] + [VM] * 9 + [ANY],
        [pltpu.VMEM((ROW_TOK, 1024), f32), pltpu.VMEM((ROW_TOK, 512), bf)],
    )
    (attended,) = call(
        merge, [((64, 2048), bf)], (outs[0], *[send(outs[j], along_x(j)) for j in (1, 2, 3)])
    )
    (cached,) = call(
        cache_join,
        [((4, 64, 768), bf)],
        (mine, *[send(mine, along_z(-j)) for j in (1, 2, 3)], outs[0]),
        [VM] * 4 + [ANY],
    )
    (cache,) = call(
        cache_write,
        [((1, 1, 512, 768), bf)],
        (plan, cached, send(cached, other_core)),
        [SM, VM, VM],
    )
    return attended, cache


def solution(mesh):
    fine = Mesh(mesh.devices.reshape(SIZES), EVERY)
    in_specs = (P(EVERY, None), P(), P(EVERY, None), P(EVERY, None), P(), P(), P(), P())
    out_specs = (P(EVERY, None), P(("z", "core"), ("y", "x"), None, None))
    return jax.shard_map(
        per_device, mesh=fine, in_specs=in_specs, out_specs=out_specs, check_vma=False
    )
```

```python
import functools

import jax
import jax.numpy as jnp
import numpy as np
from jax import lax
from jax.experimental import pallas as pl
from jax.experimental.pallas import tpu as pltpu
from jax.sharding import Mesh
from jax.sharding import PartitionSpec as P

HEAD = 128
NEG = -1e30
ROW_TOK = 256
COLS = 768

EVERY = ("z", "core", "y", "x")
SIZES = (4, 2, 4, 4)
VM = pl.BlockSpec(memory_space=pltpu.VMEM)
SM = pl.BlockSpec(memory_space=pltpu.SMEM)
ANY = pl.BlockSpec(memory_space=pl.ANY)


def rotary_table():
    angles = np.arange(1024)[:, None] * 1000000.0 ** (-np.arange(64) * 2.0 / HEAD)[None, :]
    return np.concatenate([np.cos(angles), np.sin(angles)], axis=1).astype(np.float32)


def flat(z, c, y, x):
    return ((z % 4 * 2 + c % 2) * 4 + y % 4) * 4 + x % 4


PLACES = [(z, c, y, x) for z in range(4) for c in range(2) for y in range(4) for x in range(4)]


def send(v, move):
    return lax.ppermute(v, EVERY, [(flat(*p), flat(*move(*p))) for p in PLACES])


def along_x(j):
    return lambda z, c, y, x: (z, c, y, x + j)


def along_z(j):
    return lambda z, c, y, x: (z + j, c, y, x)


def along_first(j):
    return lambda z, c, y, x: (z + j, c, y, x) if c == 0 else (z, c, y + j, x)


def along_second(j):
    return lambda z, c, y, x: (z, c, y + j, x) if c == 0 else (z + j, c, y, x)


def other_core(z, c, y, x):
    return (z, 1 - c, y, x)


def along_y(j):
    return lambda z, c, y, x: (z, c, y + j, x)


def pair_x(z, c, y, x):
    return (z, c, y, x ^ 1)


def call(kernel, outs, operands, in_specs=None, scratch=(), grant=20, **more):
    outs = tuple(jax.ShapeDtypeStruct(s, d) for s, d in outs)
    return pl.pallas_call(
        kernel,
        out_shape=outs,
        in_specs=[VM] * len(operands) if in_specs is None else in_specs,
        out_specs=(VM,) * len(outs),
        scratch_shapes=list(scratch),
        compiler_params=pltpu.CompilerParams(vmem_limit_bytes=grant * 1024 * 1024),
        name=kernel.__name__,
        **more,
    )(*operands)


def cut(wq, wkv, b0, b1, b2, b3, q_buf, kv_buf, sem):
    copies = [
        pltpu.make_async_copy(wq, q_buf, sem.at[0]),
        pltpu.make_async_copy(wkv, kv_buf, sem.at[1]),
    ]
    for copy in copies:
        copy.start()
    for copy in copies:
        copy.wait()
    x = lax.axis_index("x")
    for j, block in enumerate((b0, b1, b2, b3)):
        to = lax.rem(x + j, 4)
        slot = lax.div(to + 1, 2)
        for n in range(2):
            low = pl.multiple_of((slot + 3 * n) * HEAD, HEAD)
            block[:, n * HEAD : (n + 1) * HEAD] = kv_buf[:, pl.ds(low, HEAD)]
        block[:, 256:] = q_buf[:, pl.ds(pl.multiple_of(to * 512, 512), 512)]


def norm(tokens, gain, after, out):
    floats = tokens[...].astype(jnp.float32)
    mean = jnp.mean(floats * floats, axis=1, keepdims=True)
    out[...] = (floats * lax.rsqrt(mean + 1e-06) * gain[...][None, :]).astype(jnp.bfloat16)


def place(p0, p1, p2, p3, out, buf):
    x = lax.axis_index("x")
    for j, p in enumerate((p0, p1, p2, p3)):
        buf[lax.rem(x + 4 - j, 4)] = p[...].astype(jnp.float32)
    out[...] = jnp.concatenate([buf[k] for k in range(4)], axis=0).astype(jnp.bfloat16)


def stage(s0, s1, s2, s3, after, block):
    for i, s in enumerate((s0, s1, s2, s3)):
        block[i] = s[...]


def relay(s0, s1, s3, n1, n3, joined, r1, r3, low, high):
    for n, s in enumerate((s0, s1, s3)):
        joined[4 * n : 4 * n + 4] = s[...]
    r1[...] = s1[:2]
    r3[...] = s3[2:]
    low[...] = n1[:32, :]
    high[...] = n3[32:, :]


def join2(a, b, after1, after2, out):
    out[:2] = a[...]
    out[2:] = b[...]


def load_weights(ref, t, places, buf):
    y = lax.axis_index("y")
    z = lax.axis_index("z")
    for n, (j, i) in enumerate(places):
        zz = lax.rem(z + jnp.where(t == 0, i, j), 4)
        yy = lax.rem(y + jnp.where(t == 0, j, i), 4)
        buf[(2 * zz + t) * 4 + yy] = ref[n]


FIRST = [(j, i) for j in (0, 1, 3) for i in range(4)]
LAST = [(2, i) for i in range(4)]


def gather(
    offsets, own1, own2, other1, n0, n1, n2a, n2b, n3, table, qb, kvb, w, x_out, cs, qb_out, kvb_out, sem
):
    e = 2 * lax.axis_index("z") + lax.axis_index("core")
    y = lax.axis_index("y")
    x = lax.axis_index("x")
    core = lax.axis_index("core")
    copies = []
    for k in range(4):
        s = 4 * y + k
        row = pl.multiple_of((s - offsets[e, s]) * 64, 64)
        copies.append(
            pltpu.make_async_copy(
                table.at[pl.ds(row, 64), :], cs.at[k * 64 : (k + 1) * 64, :], sem.at[k]
            )
        )
    copies.append(
        pltpu.make_async_copy(qb.at[pl.ds(pl.multiple_of(x * 512, 512), 512)], qb_out, sem.at[4])
    )
    slot = lax.div(x + 1, 2)
    for n in range(2):
        low = pl.multiple_of((slot + 3 * n) * HEAD, HEAD)
        copies.append(
            pltpu.make_async_copy(kvb.at[pl.ds(low, HEAD)], kvb_out.at[n], sem.at[5 + n])
        )
    for copy in copies:
        copy.start()
    for ref, j, low, size in (
        (n0, 0, 0, 64),
        (n1, 1, 0, 64),
        (n2a, 2, 0, 32),
        (n2b, 2, 32, 32),
        (n3, 3, 0, 64),
    ):
        row = pl.multiple_of(lax.rem(x + j, 4) * 64 + low, 32)
        x_out[pl.ds(row, size), :] = ref[...]
    load_weights(own1, core, FIRST, w)
    load_weights(own2, core, LAST, w)
    load_weights(other1, 1 - core, FIRST, w)
    for copy in copies:
        copy.wait()


def rotate(v, cos, sin):
    a = v[:, :64]
    b = v[:, 64:]
    return jnp.concatenate([a * cos - b * sin, b * cos + a * sin], axis=1).astype(jnp.bfloat16)


def kv_project(w_in, other2, x_in, cs, kvb, w, kv):
    del w_in
    load_weights(other2, 1 - lax.axis_index("core"), LAST, w)
    acc = jnp.dot(
        x_in[...], w[:, :, :256].reshape(3584, 256), preferred_element_type=jnp.float32
    )
    kv[:, :HEAD] = rotate(acc[:, :HEAD] + kvb[0][None, :], cs[:, :64], cs[:, 64:])
    kv[:, HEAD:] = (acc[:, HEAD:] + kvb[1][None, :]).astype(jnp.bfloat16)


def q_project(w, x_in, cs, qb, q):
    for g in range(2):
        part = slice((g + 1) * 256, (g + 2) * 256)
        acc = jnp.dot(
            x_in[...], w[:, :, part].reshape(3584, 256), preferred_element_type=jnp.float32
        )
        for h in range(2):
            low = (2 * g + h) * HEAD
            head = acc[:, h * HEAD : (h + 1) * HEAD] + qb[low : low + HEAD][None, :]
            q[:, low : low + HEAD] = rotate(head, cs[:, :64], cs[:, 64:])


def attend(offsets, q, a0, a1, a2, a3, b0, b1, b2, b3, after, o0, o1, o2, o3, mask, full):
    x = lax.axis_index("x")
    y = lax.axis_index("y")
    e = 2 * lax.axis_index("z") + lax.axis_index("core")
    qi = lax.broadcasted_iota(jnp.int32, (ROW_TOK, ROW_TOK), 0)
    ki = lax.broadcasted_iota(jnp.int32, (ROW_TOK, ROW_TOK), 1)
    starts = [offsets[e, 4 * y + k] * 64 for k in range(4)]
    start = jnp.where(
        qi < 128,
        jnp.where(qi < 64, starts[0], starts[1]),
        jnp.where(qi < 192, starts[2], starts[3]),
    )
    for j in range(4):
        key = ki + lax.rem(y + j, 4) * ROW_TOK
        ok = (key >= start) & (key <= qi + y * ROW_TOK)
        mask[:, j * ROW_TOK : (j + 1) * ROW_TOK] = jnp.where(ok, 0.0, NEG)

    for h in range(4):
        left = (x == 1) if h == 2 else ((x == 1) | (x == 3))
        pick = jnp.where(left, 1, 0) if h < 3 else 0
        qh = q[:, h * HEAD : (h + 1) * HEAD]
        parts = []
        vals = []
        for j, (pa, pb) in enumerate(((a0, b0), (a1, b1), (a2, b2), (a3, b3))):
            kv = jnp.where(pick == 1, pb[...], pa[...]) if h < 3 else pa[...]
            s = lax.dot_general(
                qh, kv[:, :HEAD], (((1,), (1,)), ((), ())), preferred_element_type=jnp.float32
            )
            parts.append(s * (HEAD**-0.5) + mask[:, j * ROW_TOK : (j + 1) * ROW_TOK])
            vals.append(kv[:, HEAD:])
        top = functools.reduce(jnp.maximum, [jnp.max(s, axis=1, keepdims=True) for s in parts])
        mass = jnp.zeros((ROW_TOK, 1), jnp.float32)
        acc = jnp.zeros((ROW_TOK, HEAD), jnp.float32)
        for s, v in zip(parts, vals):
            p = jnp.exp(s - top)
            mass += jnp.sum(p, axis=1, keepdims=True)
            acc += jnp.dot(p.astype(jnp.bfloat16), v, preferred_element_type=jnp.float32)
        full[:, h * HEAD : (h + 1) * HEAD] = (acc / mass).astype(jnp.bfloat16)
    for j, o in enumerate((o0, o1, o2, o3)):
        o[...] = full[pl.ds(pl.multiple_of(lax.rem(x + j, 4) * 64, 64), 64), :]


def merge(r0, r1, r2, r3, out):
    x = lax.axis_index("x")
    for j, r in enumerate((r0, r1, r2, r3)):
        low = pl.multiple_of(lax.rem(x + 4 - j, 4) * 512, 512)
        out[:, pl.ds(low, 512)] = r[...]


def cache_rows(a0, a1, a2, a3, after, t0, t1, t2, t3):
    x = lax.axis_index("x")
    y = lax.axis_index("y")
    i = lax.broadcasted_iota(jnp.int32, (64, ROW_TOK), 0)
    t = lax.broadcasted_iota(jnp.int32, (64, ROW_TOK), 1)
    want = 16 * lax.rem(i, 16) + 4 * y + lax.rem(x + lax.div(i, 16), 4)
    select = jnp.where(t == want, 1.0, 0.0).astype(jnp.bfloat16)
    for j, a in enumerate((a0, a1, a2, a3)):
        got = jnp.dot(select, a[...], preferred_element_type=jnp.float32).astype(jnp.bfloat16)
        rows = pl.ds(pl.multiple_of(lax.rem(y + j, 4) * 16, 16), 16)
        for k, out in enumerate((t0, t1, t2, t3)):
            out[rows, :] = got[16 * k : 16 * k + 16]


def cache_heads(t0, t1, t2, t3, out, buf):
    x = lax.axis_index("x")
    for j, t in enumerate((t0, t1, t2, t3)):
        buf[lax.rem(x + 4 - j, 4)] = t[...]
    for k, src in enumerate((0, 1, 3)):
        out[:, k * HEAD : (k + 1) * HEAD] = buf[src, :, :HEAD]
        out[:, (3 + k) * HEAD : (4 + k) * HEAD] = buf[src, :, HEAD:]


def cache_join(c0, c1, c2, c3, after, out):
    for n, c in enumerate((c0, c1, c2, c3)):
        out[n] = c[...]


def write_slots(plan, ref, t, out, buf, sem):
    z = lax.axis_index("z")
    group = 2 * z + lax.axis_index("core")
    copies = []
    for j in range(4):
        e = 2 * lax.rem(z + j, 4) + t
        v = ref[j]
        buf[j] = jnp.where(plan[e, 0] == group, v, jnp.zeros_like(v))
        rows = pl.ds(pl.multiple_of(e * 64, 64), 64)
        copies.append(pltpu.make_async_copy(buf.at[j], out.at[0, 0, rows, :], sem.at[j]))
        copies[j].start()
    for copy in copies:
        copy.wait()


def cache_own(plan, ref, out, buf, sem):
    write_slots(plan, ref, lax.axis_index("core"), out, buf, sem)


def cache_other(plan, ref, half, out, buf, sem):
    del half
    write_slots(plan, ref, 1 - lax.axis_index("core"), out, buf, sem)


def per_device(tokens, gain, q_weight, key_value_weight, q_bias, kv_bias, plan, home_offsets):
    bf = jnp.bfloat16
    f32 = jnp.float32
    blocks = call(
        cut,
        [((28, COLS), bf)] * 4,
        (q_weight, key_value_weight),
        [ANY] * 2,
        [
            pltpu.VMEM((28, 2048), bf),
            pltpu.VMEM((28, 768), bf),
            pltpu.SemaphoreType.DMA((2,)),
        ],
        grant=60,
    )
    got = [blocks[0]] + [send(blocks[j], along_x(j)) for j in (1, 2, 3)]
    (w0,) = call(place, [((112, COLS), bf)], got, scratch=[pltpu.VMEM((4, 28, COLS), f32)])
    (n0,) = call(norm, [((64, 3584), bf)], (tokens, gain, w0), [VM, VM, ANY])
    (s0,) = call(
        stage,
        [((4, 112, COLS), bf)],
        (w0, *[send(w0, along_first(-j)) for j in (1, 2, 3)], n0),
        [VM] * 4 + [ANY],
    )
    n1 = send(n0, along_x(-1))
    n3 = send(n0, along_x(1))
    s1 = send(s0, along_second(-1))
    s3 = send(s0, along_second(1))
    own1, r1, r3, low, high = call(
        relay,
        [((12, 112, COLS), bf)] + [((2, 112, COLS), bf)] * 2 + [((32, 3584), bf)] * 2,
        (s0, s1, s3, n1, n3),
    )
    n2a = send(low, along_x(-1))
    n2b = send(high, along_x(1))
    s2a = send(r1, along_second(-1))
    s2b = send(r3, along_second(1))
    other1 = send(own1, other_core)
    (own2,) = call(
        join2, [((4, 112, COLS), bf)], (s2a, s2b, n2a, n2b), [VM] * 2 + [ANY] * 2
    )
    other2 = send(own2, other_core)
    w, x_all, cs, qb, kvb = call(
        gather,
        [
            ((32, 112, COLS), bf),
            ((ROW_TOK, 3584), bf),
            ((ROW_TOK, HEAD), f32),
            ((512,), f32),
            ((2, HEAD), f32),
        ],
        (
            home_offsets, own1, own2, other1, n0, n1, n2a, n2b, n3,
            jnp.asarray(rotary_table()), q_bias, kv_bias,
        ),
        [SM] + [VM] * 8 + [ANY] * 3,
        [pltpu.SemaphoreType.DMA((7,))],
    )
    w, kv = call(
        kv_project,
        [((32, 112, COLS), bf), ((ROW_TOK, 256), bf)],
        (w, other2, x_all, cs, kvb),
        input_output_aliases={0: 0},
    )
    (q,) = call(q_project, [((ROW_TOK, 512), bf)], (w, x_all, cs, qb))

    a = [kv] + [send(kv, along_y(-j)) for j in (1, 2, 3)]
    b = [send(v, pair_x) for v in a]
    rows = call(cache_rows, [((64, 256), bf)] * 4, (*a, q), [VM] * 4 + [ANY])
    (mine,) = call(
        cache_heads,
        [((64, 768), bf)],
        (rows[0], *[send(rows[j], along_x(j)) for j in (1, 2, 3)]),
        scratch=[pltpu.VMEM((4, 64, 256), bf)],
    )
    outs = call(
        attend,
        [((64, 512), bf)] * 4,
        (home_offsets, q, *a, *b, mine),
        [SM] + [VM] * 9 + [ANY],
        [pltpu.VMEM((ROW_TOK, 1024), f32), pltpu.VMEM((ROW_TOK, 512), bf)],
    )
    (attended,) = call(
        merge, [((64, 2048), bf)], (outs[0], *[send(outs[j], along_x(j)) for j in (1, 2, 3)])
    )
    (cached,) = call(
        cache_join,
        [((4, 64, 768), bf)],
        (mine, *[send(mine, along_z(-j)) for j in (1, 2, 3)], outs[0]),
        [VM] * 4 + [ANY],
    )
    slots = dict(
        out_shape=jax.ShapeDtypeStruct((1, 1, 512, 768), bf),
        out_specs=ANY,
        scratch_shapes=[pltpu.VMEM((4, 64, 768), bf), pltpu.SemaphoreType.DMA((4,))],
    )
    half = pl.pallas_call(cache_own, in_specs=[SM, VM], name="cache_own", **slots)(plan, cached)
    cache = pl.pallas_call(
        cache_other,
        in_specs=[SM, VM, ANY],
        input_output_aliases={2: 0},
        name="cache_other",
        **slots,
    )(plan, send(cached, other_core), half)
    return attended, cache


def solution(mesh):
    fine = Mesh(mesh.devices.reshape(SIZES), EVERY)
    in_specs = (P(EVERY, None), P(), P(EVERY, None), P(EVERY, None), P(), P(), P(), P())
    out_specs = (P(EVERY, None), P(("z", "core"), ("y", "x"), None, None))
    return jax.shard_map(
        per_device, mesh=fine, in_specs=in_specs, out_specs=out_specs, check_vma=False
    )
```

```python
import functools

import jax
import jax.numpy as jnp
import numpy as np
from jax import lax
from jax.experimental import pallas as pl
from jax.experimental.pallas import tpu as pltpu
from jax.sharding import Mesh
from jax.sharding import PartitionSpec as P

HEAD = 128
NEG = -1e30
ROW_TOK = 256
COLS = 768

EVERY = ("z", "core", "y", "x")
SIZES = (4, 2, 4, 4)
VM = pl.BlockSpec(memory_space=pltpu.VMEM)
SM = pl.BlockSpec(memory_space=pltpu.SMEM)
ANY = pl.BlockSpec(memory_space=pl.ANY)


def rotary_table():
    angles = np.arange(1024)[:, None] * 1000000.0 ** (-np.arange(64) * 2.0 / HEAD)[None, :]
    return np.concatenate([np.cos(angles), np.sin(angles)], axis=1).astype(np.float32)


def flat(z, c, y, x):
    return ((z % 4 * 2 + c % 2) * 4 + y % 4) * 4 + x % 4


PLACES = [(z, c, y, x) for z in range(4) for c in range(2) for y in range(4) for x in range(4)]


def send(v, move):
    return lax.ppermute(v, EVERY, [(flat(*p), flat(*move(*p))) for p in PLACES])


def along_x(j):
    return lambda z, c, y, x: (z, c, y, x + j)


def along_z(j):
    return lambda z, c, y, x: (z + j, c, y, x)


def along_first(j):
    return lambda z, c, y, x: (z + j, c, y, x) if c == 0 else (z, c, y + j, x)


def along_second(j):
    return lambda z, c, y, x: (z, c, y + j, x) if c == 0 else (z + j, c, y, x)


def other_core(z, c, y, x):
    return (z, 1 - c, y, x)


def along_y(j):
    return lambda z, c, y, x: (z, c, y + j, x)


def pair_x(z, c, y, x):
    return (z, c, y, x ^ 1)


def call(kernel, outs, operands, in_specs=None, scratch=(), grant=20, **more):
    outs = tuple(jax.ShapeDtypeStruct(s, d) for s, d in outs)
    return pl.pallas_call(
        kernel,
        out_shape=outs,
        in_specs=[VM] * len(operands) if in_specs is None else in_specs,
        out_specs=(VM,) * len(outs),
        scratch_shapes=list(scratch),
        compiler_params=pltpu.CompilerParams(vmem_limit_bytes=grant * 1024 * 1024),
        name=kernel.__name__,
        **more,
    )(*operands)


def cut(wq, wkv, b0, b1, b2, b3, q_buf, kv_buf, sem):
    copies = [
        pltpu.make_async_copy(wq, q_buf, sem.at[0]),
        pltpu.make_async_copy(wkv, kv_buf, sem.at[1]),
    ]
    for copy in copies:
        copy.start()
    for copy in copies:
        copy.wait()
    x = lax.axis_index("x")
    for j, block in enumerate((b0, b1, b2, b3)):
        to = lax.rem(x + j, 4)
        slot = lax.div(to + 1, 2)
        for n in range(2):
            low = pl.multiple_of((slot + 3 * n) * HEAD, HEAD)
            block[:, n * HEAD : (n + 1) * HEAD] = kv_buf[:, pl.ds(low, HEAD)]
        block[:, 256:] = q_buf[:, pl.ds(pl.multiple_of(to * 512, 512), 512)]


def norm(tokens, gain, after, out):
    floats = tokens[...].astype(jnp.float32)
    mean = jnp.mean(floats * floats, axis=1, keepdims=True)
    out[...] = (floats * lax.rsqrt(mean + 1e-06) * gain[...][None, :]).astype(jnp.bfloat16)


def place(p0, p1, p2, p3, out, buf):
    x = lax.axis_index("x")
    for j, p in enumerate((p0, p1, p2, p3)):
        buf[lax.rem(x + 4 - j, 4)] = p[...].astype(jnp.float32)
    out[...] = jnp.concatenate([buf[k] for k in range(4)], axis=0).astype(jnp.bfloat16)


def stage(s0, s1, s2, s3, after, block):
    for i, s in enumerate((s0, s1, s2, s3)):
        block[i] = s[...]


def relay(s0, s1, s3, n1, n3, joined, r1, r3, low, high):
    for n, s in enumerate((s0, s1, s3)):
        joined[4 * n : 4 * n + 4] = s[...]
    r1[...] = s1[:2]
    r3[...] = s3[2:]
    low[...] = n1[:32, :]
    high[...] = n3[32:, :]


def join2(a, b, after1, after2, out):
    out[:2] = a[...]
    out[2:] = b[...]


def load_weights(ref, t, places, buf):
    y = lax.axis_index("y")
    z = lax.axis_index("z")
    for n, (j, i) in enumerate(places):
        zz = lax.rem(z + jnp.where(t == 0, i, j), 4)
        yy = lax.rem(y + jnp.where(t == 0, j, i), 4)
        buf[(2 * zz + t) * 4 + yy] = ref[n]


FIRST = [(j, i) for j in (0, 1, 3) for i in range(4)]
LAST = [(2, i) for i in range(4)]


def gather(
    offsets, own1, own2, other1, n0, n1, n2a, n2b, n3, table, qb, kvb, w, x_out, cs, qb_out, kvb_out, sem
):
    e = 2 * lax.axis_index("z") + lax.axis_index("core")
    y = lax.axis_index("y")
    x = lax.axis_index("x")
    core = lax.axis_index("core")
    copies = []
    for k in range(4):
        s = 4 * y + k
        row = pl.multiple_of((s - offsets[e, s]) * 64, 64)
        copies.append(
            pltpu.make_async_copy(
                table.at[pl.ds(row, 64), :], cs.at[k * 64 : (k + 1) * 64, :], sem.at[k]
            )
        )
    copies.append(
        pltpu.make_async_copy(qb.at[pl.ds(pl.multiple_of(x * 512, 512), 512)], qb_out, sem.at[4])
    )
    slot = lax.div(x + 1, 2)
    for n in range(2):
        low = pl.multiple_of((slot + 3 * n) * HEAD, HEAD)
        copies.append(
            pltpu.make_async_copy(kvb.at[pl.ds(low, HEAD)], kvb_out.at[n], sem.at[5 + n])
        )
    for copy in copies:
        copy.start()
    for ref, j, low, size in (
        (n0, 0, 0, 64),
        (n1, 1, 0, 64),
        (n2a, 2, 0, 32),
        (n2b, 2, 32, 32),
        (n3, 3, 0, 64),
    ):
        row = pl.multiple_of(lax.rem(x + j, 4) * 64 + low, 32)
        x_out[pl.ds(row, size), :] = ref[...]
    load_weights(own1, core, FIRST, w)
    load_weights(own2, core, LAST, w)
    load_weights(other1, 1 - core, FIRST, w)
    for copy in copies:
        copy.wait()


def rotate(v, cos, sin):
    a = v[:, :64]
    b = v[:, 64:]
    return jnp.concatenate([a * cos - b * sin, b * cos + a * sin], axis=1).astype(jnp.bfloat16)


def kv_project(w_in, other2, x_in, cs, kvb, w, kv):
    del w_in
    load_weights(other2, 1 - lax.axis_index("core"), LAST, w)
    acc = jnp.dot(
        x_in[...], w[:, :, :256].reshape(3584, 256), preferred_element_type=jnp.float32
    )
    kv[:, :HEAD] = rotate(acc[:, :HEAD] + kvb[0][None, :], cs[:, :64], cs[:, 64:])
    kv[:, HEAD:] = (acc[:, HEAD:] + kvb[1][None, :]).astype(jnp.bfloat16)


def q_project(w, x_in, cs, qb, q):
    for g in range(2):
        part = slice((g + 1) * 256, (g + 2) * 256)
        acc = jnp.dot(
            x_in[...], w[:, :, part].reshape(3584, 256), preferred_element_type=jnp.float32
        )
        for h in range(2):
            low = (2 * g + h) * HEAD
            head = acc[:, h * HEAD : (h + 1) * HEAD] + qb[low : low + HEAD][None, :]
            q[:, low : low + HEAD] = rotate(head, cs[:, :64], cs[:, 64:])


def attend(offsets, q, a0, a1, a2, a3, b0, b1, b2, b3, after, o0, o1, o2, o3, mask, full):
    x = lax.axis_index("x")
    y = lax.axis_index("y")
    e = 2 * lax.axis_index("z") + lax.axis_index("core")
    qi = lax.broadcasted_iota(jnp.int32, (ROW_TOK, ROW_TOK), 0)
    ki = lax.broadcasted_iota(jnp.int32, (ROW_TOK, ROW_TOK), 1)
    starts = [offsets[e, 4 * y + k] * 64 for k in range(4)]
    start = jnp.where(
        qi < 128,
        jnp.where(qi < 64, starts[0], starts[1]),
        jnp.where(qi < 192, starts[2], starts[3]),
    )
    for j in range(4):
        key = ki + lax.rem(y + j, 4) * ROW_TOK
        ok = (key >= start) & (key <= qi + y * ROW_TOK)
        mask[:, j * ROW_TOK : (j + 1) * ROW_TOK] = jnp.where(ok, 0.0, NEG)

    for h in range(4):
        left = (x == 1) if h == 2 else ((x == 1) | (x == 3))
        pick = jnp.where(left, 1, 0) if h < 3 else 0
        qh = q[:, h * HEAD : (h + 1) * HEAD]
        parts = []
        vals = []
        for j, (pa, pb) in enumerate(((a0, b0), (a1, b1), (a2, b2), (a3, b3))):
            kv = jnp.where(pick == 1, pb[...], pa[...]) if h < 3 else pa[...]
            s = lax.dot_general(
                qh, kv[:, :HEAD], (((1,), (1,)), ((), ())), preferred_element_type=jnp.float32
            )
            parts.append(s * (HEAD**-0.5) + mask[:, j * ROW_TOK : (j + 1) * ROW_TOK])
            vals.append(kv[:, HEAD:])
        top = functools.reduce(jnp.maximum, [jnp.max(s, axis=1, keepdims=True) for s in parts])
        mass = jnp.zeros((ROW_TOK, 1), jnp.float32)
        acc = jnp.zeros((ROW_TOK, HEAD), jnp.float32)
        for s, v in zip(parts, vals):
            p = jnp.exp(s - top)
            mass += jnp.sum(p, axis=1, keepdims=True)
            acc += jnp.dot(p.astype(jnp.bfloat16), v, preferred_element_type=jnp.float32)
        full[:, h * HEAD : (h + 1) * HEAD] = (acc / mass).astype(jnp.bfloat16)
    for j, o in enumerate((o0, o1, o2, o3)):
        o[...] = full[pl.ds(pl.multiple_of(lax.rem(x + j, 4) * 64, 64), 64), :]


def cache_rows(a0, a1, a2, a3, after1, after2, after3, t0, t1, t2, t3):
    x = lax.axis_index("x")
    y = lax.axis_index("y")
    i = lax.broadcasted_iota(jnp.int32, (64, ROW_TOK), 0)
    t = lax.broadcasted_iota(jnp.int32, (64, ROW_TOK), 1)
    want = 16 * lax.rem(i, 16) + 4 * y + lax.rem(x + lax.div(i, 16), 4)
    select = jnp.where(t == want, 1.0, 0.0).astype(jnp.bfloat16)
    for j, a in enumerate((a0, a1, a2, a3)):
        got = jnp.dot(select, a[...], preferred_element_type=jnp.float32).astype(jnp.bfloat16)
        rows = pl.ds(pl.multiple_of(lax.rem(y + j, 4) * 16, 16), 16)
        for k, out in enumerate((t0, t1, t2, t3)):
            out[rows, :] = got[16 * k : 16 * k + 16]


def cache_heads(t0, t1, t2, t3, out, buf):
    x = lax.axis_index("x")
    for j, t in enumerate((t0, t1, t2, t3)):
        buf[lax.rem(x + 4 - j, 4)] = t[...]
    for k, src in enumerate((0, 1, 3)):
        out[:, k * HEAD : (k + 1) * HEAD] = buf[src, :, :HEAD]
        out[:, (3 + k) * HEAD : (4 + k) * HEAD] = buf[src, :, HEAD:]


def cache_join(c0, c1, c2, c3, after, out):
    for n, c in enumerate((c0, c1, c2, c3)):
        out[n] = c[...]


def finish(plan, own, other, r0, r1, r2, r3, attended, cache):
    x = lax.axis_index("x")
    for j, r in enumerate((r0, r1, r2, r3)):
        low = pl.multiple_of(lax.rem(x + 4 - j, 4) * 512, 512)
        attended[:, pl.ds(low, 512)] = r[...]
    z = lax.axis_index("z")
    core = lax.axis_index("core")
    group = 2 * z + core
    for ref, t in ((own, core), (other, 1 - core)):
        for j in range(4):
            e = 2 * lax.rem(z + j, 4) + t
            rows = pl.ds(pl.multiple_of(e * 64, 64), 64)
            v = ref[j]
            cache[0, 0, rows, :] = jnp.where(plan[e, 0] == group, v, jnp.zeros_like(v))


def per_device(tokens, gain, q_weight, key_value_weight, q_bias, kv_bias, plan, home_offsets):
    bf = jnp.bfloat16
    f32 = jnp.float32
    blocks = call(
        cut,
        [((28, COLS), bf)] * 4,
        (q_weight, key_value_weight),
        [ANY] * 2,
        [
            pltpu.VMEM((28, 2048), bf),
            pltpu.VMEM((28, 768), bf),
            pltpu.SemaphoreType.DMA((2,)),
        ],
        grant=60,
    )
    got = [blocks[0]] + [send(blocks[j], along_x(j)) for j in (1, 2, 3)]
    (w0,) = call(place, [((112, COLS), bf)], got, scratch=[pltpu.VMEM((4, 28, COLS), f32)])
    (n0,) = call(norm, [((64, 3584), bf)], (tokens, gain, w0), [VM, VM, ANY])
    (s0,) = call(
        stage,
        [((4, 112, COLS), bf)],
        (w0, *[send(w0, along_first(-j)) for j in (1, 2, 3)], n0),
        [VM] * 4 + [ANY],
    )
    n1 = send(n0, along_x(-1))
    n3 = send(n0, along_x(1))
    s1 = send(s0, along_second(-1))
    s3 = send(s0, along_second(1))
    own1, r1, r3, low, high = call(
        relay,
        [((12, 112, COLS), bf)] + [((2, 112, COLS), bf)] * 2 + [((32, 3584), bf)] * 2,
        (s0, s1, s3, n1, n3),
    )
    n2a = send(low, along_x(-1))
    n2b = send(high, along_x(1))
    s2a = send(r1, along_second(-1))
    s2b = send(r3, along_second(1))
    other1 = send(own1, other_core)
    (own2,) = call(
        join2, [((4, 112, COLS), bf)], (s2a, s2b, n2a, n2b), [VM] * 2 + [ANY] * 2
    )
    other2 = send(own2, other_core)
    w, x_all, cs, qb, kvb = call(
        gather,
        [
            ((32, 112, COLS), bf),
            ((ROW_TOK, 3584), bf),
            ((ROW_TOK, HEAD), f32),
            ((512,), f32),
            ((2, HEAD), f32),
        ],
        (
            home_offsets, own1, own2, other1, n0, n1, n2a, n2b, n3,
            jnp.asarray(rotary_table()), q_bias, kv_bias,
        ),
        [SM] + [VM] * 8 + [ANY] * 3,
        [pltpu.SemaphoreType.DMA((7,))],
    )
    w, kv = call(
        kv_project,
        [((32, 112, COLS), bf), ((ROW_TOK, 256), bf)],
        (w, other2, x_all, cs, kvb),
        input_output_aliases={0: 0},
    )
    (q,) = call(q_project, [((ROW_TOK, 512), bf)], (w, x_all, cs, qb))

    a = [kv] + [send(kv, along_y(-j)) for j in (1, 2, 3)]
    b = [send(v, pair_x) for v in a]
    rows = call(cache_rows, [((64, 256), bf)] * 4, (*a, q, b[0], b[1]), [VM] * 4 + [ANY] * 3)
    (mine,) = call(
        cache_heads,
        [((64, 768), bf)],
        (rows[0], *[send(rows[j], along_x(j)) for j in (1, 2, 3)]),
        scratch=[pltpu.VMEM((4, 64, 256), bf)],
    )
    outs = call(
        attend,
        [((64, 512), bf)] * 4,
        (home_offsets, q, *a, *b, mine),
        [SM] + [VM] * 9 + [ANY],
        [pltpu.VMEM((ROW_TOK, 1024), f32), pltpu.VMEM((ROW_TOK, 512), bf)],
    )
    (cached,) = call(
        cache_join,
        [((4, 64, 768), bf)],
        (mine, *[send(mine, along_z(-j)) for j in (1, 2, 3)], outs[0]),
        [VM] * 4 + [ANY],
    )
    attended, cache = call(
        finish,
        [((64, 2048), bf), ((1, 1, 512, 768), bf)],
        (
            plan,
            cached,
            send(cached, other_core),
            outs[0],
            *[send(outs[j], along_x(j)) for j in (1, 2, 3)],
        ),
        [SM] + [VM] * 6,
    )
    return attended, cache


def solution(mesh):
    fine = Mesh(mesh.devices.reshape(SIZES), EVERY)
    in_specs = (P(EVERY, None), P(), P(EVERY, None), P(EVERY, None), P(), P(), P(), P())
    out_specs = (P(EVERY, None), P(("z", "core"), ("y", "x"), None, None))
    return jax.shard_map(
        per_device, mesh=fine, in_specs=in_specs, out_specs=out_specs, check_vma=False
    )
```

```python
import functools

import jax
import jax.numpy as jnp
import numpy as np
from jax import lax
from jax.experimental import pallas as pl
from jax.experimental.pallas import tpu as pltpu
from jax.sharding import Mesh
from jax.sharding import PartitionSpec as P

HEAD = 128
NEG = -1e30
ROW_TOK = 256
COLS = 768

EVERY = ("z", "core", "y", "x")
SIZES = (4, 2, 4, 4)
VM = pl.BlockSpec(memory_space=pltpu.VMEM)
SM = pl.BlockSpec(memory_space=pltpu.SMEM)
ANY = pl.BlockSpec(memory_space=pl.ANY)


def rotary_table():
    angles = np.arange(1024)[:, None] * 1000000.0 ** (-np.arange(64) * 2.0 / HEAD)[None, :]
    return np.concatenate([np.cos(angles), np.sin(angles)], axis=1).astype(np.float32)


def flat(z, c, y, x):
    return ((z % 4 * 2 + c % 2) * 4 + y % 4) * 4 + x % 4


PLACES = [(z, c, y, x) for z in range(4) for c in range(2) for y in range(4) for x in range(4)]


def send(v, move):
    return lax.ppermute(v, EVERY, [(flat(*p), flat(*move(*p))) for p in PLACES])


def along_x(j):
    return lambda z, c, y, x: (z, c, y, x + j)


def along_z(j):
    return lambda z, c, y, x: (z + j, c, y, x)


def along_first(j):
    return lambda z, c, y, x: (z + j, c, y, x) if c == 0 else (z, c, y + j, x)


def along_second(j):
    return lambda z, c, y, x: (z, c, y + j, x) if c == 0 else (z + j, c, y, x)


def other_core(z, c, y, x):
    return (z, 1 - c, y, x)


def along_y(j):
    return lambda z, c, y, x: (z, c, y + j, x)


def pair_x(z, c, y, x):
    return (z, c, y, x ^ 1)


def call(kernel, outs, operands, in_specs=None, scratch=(), grant=20, **more):
    outs = tuple(jax.ShapeDtypeStruct(s, d) for s, d in outs)
    return pl.pallas_call(
        kernel,
        out_shape=outs,
        in_specs=[VM] * len(operands) if in_specs is None else in_specs,
        out_specs=(VM,) * len(outs),
        scratch_shapes=list(scratch),
        compiler_params=pltpu.CompilerParams(vmem_limit_bytes=grant * 1024 * 1024),
        name=kernel.__name__,
        **more,
    )(*operands)


def cut(wq, wkv, b0, b1, b2, b3, q_buf, kv_buf, sem):
    copies = [
        pltpu.make_async_copy(wq, q_buf, sem.at[0]),
        pltpu.make_async_copy(wkv, kv_buf, sem.at[1]),
    ]
    for copy in copies:
        copy.start()
    for copy in copies:
        copy.wait()
    x = lax.axis_index("x")
    for j, block in enumerate((b0, b1, b2, b3)):
        to = lax.rem(x + j, 4)
        slot = lax.div(to + 1, 2)
        for n in range(2):
            low = pl.multiple_of((slot + 3 * n) * HEAD, HEAD)
            block[:, n * HEAD : (n + 1) * HEAD] = kv_buf[:, pl.ds(low, HEAD)]
        block[:, 256:] = q_buf[:, pl.ds(pl.multiple_of(to * 512, 512), 512)]


def norm(tokens, gain, after, out):
    floats = tokens[...].astype(jnp.float32)
    mean = jnp.mean(floats * floats, axis=1, keepdims=True)
    out[...] = (floats * lax.rsqrt(mean + 1e-06) * gain[...][None, :]).astype(jnp.bfloat16)


def keep(v, out, sem):
    copy = pltpu.make_async_copy(v, out, sem)
    copy.start()
    copy.wait()


def pair(u, v, out):
    out[0] = u[...]
    out[1] = v[...]


def place(p0, p1, p2, p3, out, buf):
    x = lax.axis_index("x")
    for j, p in enumerate((p0, p1, p2, p3)):
        buf[lax.rem(x + 4 - j, 4)] = p[...].astype(jnp.float32)
    out[...] = jnp.concatenate([buf[k] for k in range(4)], axis=0).astype(jnp.bfloat16)


def stage(s0, s1, s2, s3, after, block):
    for i, s in enumerate((s0, s1, s2, s3)):
        block[i] = s[...]


def relay(s0, s1, s3, n1, n3, joined, r1, r3, low, high):
    for n, s in enumerate((s0, s1, s3)):
        joined[4 * n : 4 * n + 4] = s[...]
    r1[...] = s1[:2]
    r3[...] = s3[2:]
    low[...] = n1[:32, :]
    high[...] = n3[32:, :]


def join2(a, b, after1, after2, out):
    out[:2] = a[...]
    out[2:] = b[...]


def load_weights(ref, t, places, buf):
    y = lax.axis_index("y")
    z = lax.axis_index("z")
    for n, (j, i) in enumerate(places):
        zz = lax.rem(z + jnp.where(t == 0, i, j), 4)
        yy = lax.rem(y + jnp.where(t == 0, j, i), 4)
        buf[(2 * zz + t) * 4 + yy] = ref[n]


FIRST = [(j, i) for j in (0, 1, 3) for i in range(4)]
LAST = [(2, i) for i in range(4)]


def gather(
    offsets, own1, own2, other1, n0, n1, n2a, n2b, n3, table, qb, kvb, w, x_out, cs, qb_out, kvb_out, sem
):
    e = 2 * lax.axis_index("z") + lax.axis_index("core")
    y = lax.axis_index("y")
    x = lax.axis_index("x")
    core = lax.axis_index("core")
    copies = []
    for k in range(4):
        s = 4 * y + k
        row = pl.multiple_of((s - offsets[e, s]) * 64, 64)
        copies.append(
            pltpu.make_async_copy(
                table.at[pl.ds(row, 64), :], cs.at[k * 64 : (k + 1) * 64, :], sem.at[k]
            )
        )
    copies.append(
        pltpu.make_async_copy(qb.at[pl.ds(pl.multiple_of(x * 512, 512), 512)], qb_out, sem.at[4])
    )
    slot = lax.div(x + 1, 2)
    for n in range(2):
        low = pl.multiple_of((slot + 3 * n) * HEAD, HEAD)
        copies.append(
            pltpu.make_async_copy(kvb.at[pl.ds(low, HEAD)], kvb_out.at[n], sem.at[5 + n])
        )
    for copy in copies:
        copy.start()
    for ref, j, low, size in (
        (n0, 0, 0, 64),
        (n1, 1, 0, 64),
        (n2a, 2, 0, 32),
        (n2b, 2, 32, 32),
        (n3, 3, 0, 64),
    ):
        row = pl.multiple_of(lax.rem(x + j, 4) * 64 + low, 32)
        x_out[pl.ds(row, size), :] = ref[...]
    load_weights(own1, core, FIRST, w)
    load_weights(own2, core, LAST, w)
    load_weights(other1, 1 - core, FIRST, w)
    for copy in copies:
        copy.wait()


def rotate(v, cos, sin):
    a = v[:, :64]
    b = v[:, 64:]
    return jnp.concatenate([a * cos - b * sin, b * cos + a * sin], axis=1).astype(jnp.bfloat16)


def kv_project(w_in, other2, x_in, cs, kvb, w, kv):
    del w_in
    load_weights(other2, 1 - lax.axis_index("core"), LAST, w)
    acc = jnp.dot(
        x_in[...], w[:, :, :256].reshape(3584, 256), preferred_element_type=jnp.float32
    )
    kv[:, :HEAD] = rotate(acc[:, :HEAD] + kvb[0][None, :], cs[:, :64], cs[:, 64:])
    kv[:, HEAD:] = (acc[:, HEAD:] + kvb[1][None, :]).astype(jnp.bfloat16)


def q_project(w, x_in, cs, qb, q):
    for g in range(2):
        part = slice((g + 1) * 256, (g + 2) * 256)
        acc = jnp.dot(
            x_in[...], w[:, :, part].reshape(3584, 256), preferred_element_type=jnp.float32
        )
        for h in range(2):
            low = (2 * g + h) * HEAD
            head = acc[:, h * HEAD : (h + 1) * HEAD] + qb[low : low + HEAD][None, :]
            q[:, low : low + HEAD] = rotate(head, cs[:, :64], cs[:, 64:])


def attend(offsets, q, a0, a1, a2, a3, b01, b23, after, o0, o1, o2, o3, mask, full):
    x = lax.axis_index("x")
    y = lax.axis_index("y")
    e = 2 * lax.axis_index("z") + lax.axis_index("core")
    qi = lax.broadcasted_iota(jnp.int32, (ROW_TOK, ROW_TOK), 0)
    ki = lax.broadcasted_iota(jnp.int32, (ROW_TOK, ROW_TOK), 1)
    starts = [offsets[e, 4 * y + k] * 64 for k in range(4)]
    start = jnp.where(
        qi < 128,
        jnp.where(qi < 64, starts[0], starts[1]),
        jnp.where(qi < 192, starts[2], starts[3]),
    )
    for j in range(4):
        key = ki + lax.rem(y + j, 4) * ROW_TOK
        ok = (key >= start) & (key <= qi + y * ROW_TOK)
        mask[:, j * ROW_TOK : (j + 1) * ROW_TOK] = jnp.where(ok, 0.0, NEG)

    for h in range(4):
        left = (x == 1) if h == 2 else ((x == 1) | (x == 3))
        pick = jnp.where(left, 1, 0) if h < 3 else 0
        qh = q[:, h * HEAD : (h + 1) * HEAD]
        parts = []
        vals = []
        for j, pa in enumerate((a0, a1, a2, a3)):
            pb = b01 if j < 2 else b23
            kv = jnp.where(pick == 1, pb[j % 2], pa[...]) if h < 3 else pa[...]
            s = lax.dot_general(
                qh, kv[:, :HEAD], (((1,), (1,)), ((), ())), preferred_element_type=jnp.float32
            )
            parts.append(s * (HEAD**-0.5) + mask[:, j * ROW_TOK : (j + 1) * ROW_TOK])
            vals.append(kv[:, HEAD:])
        top = functools.reduce(jnp.maximum, [jnp.max(s, axis=1, keepdims=True) for s in parts])
        mass = jnp.zeros((ROW_TOK, 1), jnp.float32)
        acc = jnp.zeros((ROW_TOK, HEAD), jnp.float32)
        for s, v in zip(parts, vals):
            p = jnp.exp(s - top)
            mass += jnp.sum(p, axis=1, keepdims=True)
            acc += jnp.dot(p.astype(jnp.bfloat16), v, preferred_element_type=jnp.float32)
        full[:, h * HEAD : (h + 1) * HEAD] = (acc / mass).astype(jnp.bfloat16)
    for j, o in enumerate((o0, o1, o2, o3)):
        o[...] = full[pl.ds(pl.multiple_of(lax.rem(x + j, 4) * 64, 64), 64), :]


def cache_rows(a0, a1, a2, a3, after, t0, t1, t2, t3):
    x = lax.axis_index("x")
    y = lax.axis_index("y")
    i = lax.broadcasted_iota(jnp.int32, (64, ROW_TOK), 0)
    t = lax.broadcasted_iota(jnp.int32, (64, ROW_TOK), 1)
    want = 16 * lax.rem(i, 16) + 4 * y + lax.rem(x + lax.div(i, 16), 4)
    select = jnp.where(t == want, 1.0, 0.0).astype(jnp.bfloat16)
    for j, a in enumerate((a0, a1, a2, a3)):
        got = jnp.dot(select, a[...], preferred_element_type=jnp.float32).astype(jnp.bfloat16)
        rows = pl.ds(pl.multiple_of(lax.rem(y + j, 4) * 16, 16), 16)
        for k, out in enumerate((t0, t1, t2, t3)):
            out[rows, :] = got[16 * k : 16 * k + 16]


def cache_heads(t0, t1, t2, t3, out, buf):
    x = lax.axis_index("x")
    for j, t in enumerate((t0, t1, t2, t3)):
        buf[lax.rem(x + 4 - j, 4)] = t[...]
    for k, src in enumerate((0, 1, 3)):
        out[:, k * HEAD : (k + 1) * HEAD] = buf[src, :, :HEAD]
        out[:, (3 + k) * HEAD : (4 + k) * HEAD] = buf[src, :, HEAD:]


def cache_join(c0, c1, c2, c3, after, out):
    for n, c in enumerate((c0, c1, c2, c3)):
        out[n] = c[...]


def finish(plan, own, other, r0, r1, r2, r3, attended, cache):
    x = lax.axis_index("x")
    for j, r in enumerate((r0, r1, r2, r3)):
        low = pl.multiple_of(lax.rem(x + 4 - j, 4) * 512, 512)
        attended[:, pl.ds(low, 512)] = r[...]
    z = lax.axis_index("z")
    core = lax.axis_index("core")
    group = 2 * z + core
    for ref, t in ((own, core), (other, 1 - core)):
        for j in range(4):
            e = 2 * lax.rem(z + j, 4) + t
            rows = pl.ds(pl.multiple_of(e * 64, 64), 64)
            v = ref[j]
            cache[0, 0, rows, :] = jnp.where(plan[e, 0] == group, v, jnp.zeros_like(v))


def per_device(tokens, gain, q_weight, key_value_weight, q_bias, kv_bias, plan, home_offsets):
    bf = jnp.bfloat16
    f32 = jnp.float32
    blocks = call(
        cut,
        [((28, COLS), bf)] * 4,
        (q_weight, key_value_weight),
        [ANY] * 2,
        [
            pltpu.VMEM((28, 2048), bf),
            pltpu.VMEM((28, 768), bf),
            pltpu.SemaphoreType.DMA((2,)),
        ],
        grant=60,
    )
    (kept,) = call(keep, [((28, COLS), bf)], (blocks[0],), [ANY], [pltpu.SemaphoreType.DMA])
    got = [kept] + [send(blocks[j], along_x(j)) for j in (1, 2, 3)]
    (w0,) = call(place, [((112, COLS), bf)], got, scratch=[pltpu.VMEM((4, 28, COLS), f32)])
    (n0,) = call(norm, [((64, 3584), bf)], (tokens, gain, w0), [VM, VM, ANY])
    (s0,) = call(
        stage,
        [((4, 112, COLS), bf)],
        (w0, *[send(w0, along_first(-j)) for j in (1, 2, 3)], n0),
        [VM] * 4 + [ANY],
    )
    n1 = send(n0, along_x(-1))
    n3 = send(n0, along_x(1))
    s1 = send(s0, along_second(-1))
    s3 = send(s0, along_second(1))
    own1, r1, r3, low, high = call(
        relay,
        [((12, 112, COLS), bf)] + [((2, 112, COLS), bf)] * 2 + [((32, 3584), bf)] * 2,
        (s0, s1, s3, n1, n3),
    )
    n2a = send(low, along_x(-1))
    n2b = send(high, along_x(1))
    s2a = send(r1, along_second(-1))
    s2b = send(r3, along_second(1))
    other1 = send(own1, other_core)
    (own2,) = call(
        join2, [((4, 112, COLS), bf)], (s2a, s2b, n2a, n2b), [VM] * 2 + [ANY] * 2
    )
    other2 = send(own2, other_core)
    w, x_all, cs, qb, kvb = call(
        gather,
        [
            ((32, 112, COLS), bf),
            ((ROW_TOK, 3584), bf),
            ((ROW_TOK, HEAD), f32),
            ((512,), f32),
            ((2, HEAD), f32),
        ],
        (
            home_offsets, own1, own2, other1, n0, n1, n2a, n2b, n3,
            jnp.asarray(rotary_table()), q_bias, kv_bias,
        ),
        [SM] + [VM] * 8 + [ANY] * 3,
        [pltpu.SemaphoreType.DMA((7,))],
    )
    w, kv = call(
        kv_project,
        [((32, 112, COLS), bf), ((ROW_TOK, 256), bf)],
        (w, other2, x_all, cs, kvb),
        input_output_aliases={0: 0},
    )
    (q,) = call(q_project, [((ROW_TOK, 512), bf)], (w, x_all, cs, qb))

    a = [kv] + [send(kv, along_y(-j)) for j in (1, 2, 3)]
    b = [
        send(call(pair, [((2, ROW_TOK, 256), bf)], (a[n], a[n + 1]))[0], pair_x) for n in (0, 2)
    ]
    rows = call(cache_rows, [((64, 256), bf)] * 4, (*a, q), [VM] * 4 + [ANY])
    (mine,) = call(
        cache_heads,
        [((64, 768), bf)],
        (rows[0], *[send(rows[j], along_x(j)) for j in (1, 2, 3)]),
        scratch=[pltpu.VMEM((4, 64, 256), bf)],
    )
    outs = call(
        attend,
        [((64, 512), bf)] * 4,
        (home_offsets, q, *a, *b, mine),
        [SM] + [VM] * 7 + [ANY],
        [pltpu.VMEM((ROW_TOK, 1024), f32), pltpu.VMEM((ROW_TOK, 512), bf)],
    )
    (cached,) = call(
        cache_join,
        [((4, 64, 768), bf)],
        (mine, *[send(mine, along_z(-j)) for j in (1, 2, 3)], outs[0]),
        [VM] * 4 + [ANY],
    )
    attended, cache = call(
        finish,
        [((64, 2048), bf), ((1, 1, 512, 768), bf)],
        (
            plan,
            cached,
            send(cached, other_core),
            outs[0],
            *[send(outs[j], along_x(j)) for j in (1, 2, 3)],
        ),
        [SM] + [VM] * 6,
    )
    return attended, cache


def solution(mesh):
    fine = Mesh(mesh.devices.reshape(SIZES), EVERY)
    in_specs = (P(EVERY, None), P(), P(EVERY, None), P(EVERY, None), P(), P(), P(), P())
    out_specs = (P(EVERY, None), P(("z", "core"), ("y", "x"), None, None))
    return jax.shard_map(
        per_device, mesh=fine, in_specs=in_specs, out_specs=out_specs, check_vma=False
    )
```

```python
import functools

import jax
import jax.numpy as jnp
import numpy as np
from jax import lax
from jax.experimental import pallas as pl
from jax.experimental.pallas import tpu as pltpu
from jax.sharding import Mesh
from jax.sharding import PartitionSpec as P

HEAD = 128
NEG = -1e30
ROW_TOK = 256
COLS = 768

EVERY = ("z", "core", "y", "x")
SIZES = (4, 2, 4, 4)
VM = pl.BlockSpec(memory_space=pltpu.VMEM)
SM = pl.BlockSpec(memory_space=pltpu.SMEM)
ANY = pl.BlockSpec(memory_space=pl.ANY)


def rotary_table():
    angles = np.arange(1024)[:, None] * 1000000.0 ** (-np.arange(64) * 2.0 / HEAD)[None, :]
    return np.concatenate([np.cos(angles), np.sin(angles)], axis=1).astype(np.float32)


def flat(z, c, y, x):
    return ((z % 4 * 2 + c % 2) * 4 + y % 4) * 4 + x % 4


PLACES = [(z, c, y, x) for z in range(4) for c in range(2) for y in range(4) for x in range(4)]


def send(v, move):
    return lax.ppermute(v, EVERY, [(flat(*p), flat(*move(*p))) for p in PLACES])


def spread(one):
    sent = {j: one(j) for j in (2, 1, 3)}
    return [sent[j] for j in (1, 2, 3)]


def along_x(j):
    return lambda z, c, y, x: (z, c, y, x + j)


def along_z(j):
    return lambda z, c, y, x: (z + j, c, y, x)


def along_first(j):
    return lambda z, c, y, x: (z + j, c, y, x) if c == 0 else (z, c, y + j, x)


def along_second(j):
    return lambda z, c, y, x: (z, c, y + j, x) if c == 0 else (z + j, c, y, x)


def other_core(z, c, y, x):
    return (z, 1 - c, y, x)


def along_y(j):
    return lambda z, c, y, x: (z, c, y + j, x)


def pair_x(z, c, y, x):
    return (z, c, y, x ^ 1)


def call(kernel, outs, operands, in_specs=None, scratch=(), grant=20, **more):
    outs = tuple(jax.ShapeDtypeStruct(s, d) for s, d in outs)
    return pl.pallas_call(
        kernel,
        out_shape=outs,
        in_specs=[VM] * len(operands) if in_specs is None else in_specs,
        out_specs=(VM,) * len(outs),
        scratch_shapes=list(scratch),
        compiler_params=pltpu.CompilerParams(vmem_limit_bytes=grant * 1024 * 1024),
        name=kernel.__name__,
        **more,
    )(*operands)


def cut(wq, wkv, b0, b1, b2, b3, q_buf, kv_buf, sem):
    copies = [
        pltpu.make_async_copy(wq, q_buf, sem.at[0]),
        pltpu.make_async_copy(wkv, kv_buf, sem.at[1]),
    ]
    for copy in copies:
        copy.start()
    for copy in copies:
        copy.wait()
    x = lax.axis_index("x")
    for j, block in enumerate((b0, b1, b2, b3)):
        to = lax.rem(x + j, 4)
        slot = lax.div(to + 1, 2)
        for n in range(2):
            low = pl.multiple_of((slot + 3 * n) * HEAD, HEAD)
            block[:, n * HEAD : (n + 1) * HEAD] = kv_buf[:, pl.ds(low, HEAD)]
        block[:, 256:] = q_buf[:, pl.ds(pl.multiple_of(to * 512, 512), 512)]


def norm(tokens, gain, after, out):
    floats = tokens[...].astype(jnp.float32)
    mean = jnp.mean(floats * floats, axis=1, keepdims=True)
    out[...] = (floats * lax.rsqrt(mean + 1e-06) * gain[...][None, :]).astype(jnp.bfloat16)


def keep(v, out, sem):
    copy = pltpu.make_async_copy(v, out, sem)
    copy.start()
    copy.wait()


def place(p0, p1, p2, p3, out, buf):
    x = lax.axis_index("x")
    for j, p in enumerate((p0, p1, p2, p3)):
        buf[lax.rem(x + 4 - j, 4)] = p[...].astype(jnp.float32)
    out[...] = jnp.concatenate([buf[k] for k in range(4)], axis=0).astype(jnp.bfloat16)


def stage(s0, s1, s2, s3, after, block):
    for i, s in enumerate((s0, s1, s2, s3)):
        block[i] = s[...]


def relay(s0, s1, s3, n1, n3, joined, r1, r3, low, high):
    for n, s in enumerate((s0, s1, s3)):
        joined[4 * n : 4 * n + 4] = s[...]
    r1[...] = s1[:2]
    r3[...] = s3[2:]
    low[...] = n1[:32, :]
    high[...] = n3[32:, :]


def join2(a, b, after1, after2, out):
    out[:2] = a[...]
    out[2:] = b[...]


def load_weights(ref, t, places, buf):
    y = lax.axis_index("y")
    z = lax.axis_index("z")
    for n, (j, i) in enumerate(places):
        zz = lax.rem(z + jnp.where(t == 0, i, j), 4)
        yy = lax.rem(y + jnp.where(t == 0, j, i), 4)
        buf[(2 * zz + t) * 4 + yy] = ref[n]


FIRST = [(j, i) for j in (0, 1, 3) for i in range(4)]
LAST = [(2, i) for i in range(4)]


def gather(
    offsets, own1, own2, other1, n0, n1, n2a, n2b, n3, table, qb, kvb, w, x_out, cs, qb_out, kvb_out, sem
):
    e = 2 * lax.axis_index("z") + lax.axis_index("core")
    y = lax.axis_index("y")
    x = lax.axis_index("x")
    core = lax.axis_index("core")
    copies = []
    for k in range(4):
        s = 4 * y + k
        row = pl.multiple_of((s - offsets[e, s]) * 64, 64)
        copies.append(
            pltpu.make_async_copy(
                table.at[pl.ds(row, 64), :], cs.at[k * 64 : (k + 1) * 64, :], sem.at[k]
            )
        )
    copies.append(
        pltpu.make_async_copy(qb.at[pl.ds(pl.multiple_of(x * 512, 512), 512)], qb_out, sem.at[4])
    )
    slot = lax.div(x + 1, 2)
    for n in range(2):
        low = pl.multiple_of((slot + 3 * n) * HEAD, HEAD)
        copies.append(
            pltpu.make_async_copy(kvb.at[pl.ds(low, HEAD)], kvb_out.at[n], sem.at[5 + n])
        )
    for copy in copies:
        copy.start()
    for ref, j, low, size in (
        (n0, 0, 0, 64),
        (n1, 1, 0, 64),
        (n2a, 2, 0, 32),
        (n2b, 2, 32, 32),
        (n3, 3, 0, 64),
    ):
        row = pl.multiple_of(lax.rem(x + j, 4) * 64 + low, 32)
        x_out[pl.ds(row, size), :] = ref[...]
    load_weights(own1, core, FIRST, w)
    load_weights(own2, core, LAST, w)
    load_weights(other1, 1 - core, FIRST, w)
    for copy in copies:
        copy.wait()


def rotate(v, cos, sin):
    a = v[:, :64]
    b = v[:, 64:]
    return jnp.concatenate([a * cos - b * sin, b * cos + a * sin], axis=1).astype(jnp.bfloat16)


def kv_project(w_in, other2, x_in, cs, kvb, w, kv):
    del w_in
    load_weights(other2, 1 - lax.axis_index("core"), LAST, w)
    acc = jnp.dot(
        x_in[...], w[:, :, :256].reshape(3584, 256), preferred_element_type=jnp.float32
    )
    kv[:, :HEAD] = rotate(acc[:, :HEAD] + kvb[0][None, :], cs[:, :64], cs[:, 64:])
    kv[:, HEAD:] = (acc[:, HEAD:] + kvb[1][None, :]).astype(jnp.bfloat16)


def q_project(w, x_in, cs, qb, q):
    for g in range(2):
        part = slice((g + 1) * 256, (g + 2) * 256)
        acc = jnp.dot(
            x_in[...], w[:, :, part].reshape(3584, 256), preferred_element_type=jnp.float32
        )
        for h in range(2):
            low = (2 * g + h) * HEAD
            head = acc[:, h * HEAD : (h + 1) * HEAD] + qb[low : low + HEAD][None, :]
            q[:, low : low + HEAD] = rotate(head, cs[:, :64], cs[:, 64:])


def attend(offsets, q, a0, a1, a2, a3, b0, b1, b2, b3, after, o0, o1, o2, o3, mask, full):
    x = lax.axis_index("x")
    y = lax.axis_index("y")
    e = 2 * lax.axis_index("z") + lax.axis_index("core")
    qi = lax.broadcasted_iota(jnp.int32, (ROW_TOK, ROW_TOK), 0)
    ki = lax.broadcasted_iota(jnp.int32, (ROW_TOK, ROW_TOK), 1)
    starts = [offsets[e, 4 * y + k] * 64 for k in range(4)]
    start = jnp.where(
        qi < 128,
        jnp.where(qi < 64, starts[0], starts[1]),
        jnp.where(qi < 192, starts[2], starts[3]),
    )
    for j in range(4):
        key = ki + lax.rem(y + j, 4) * ROW_TOK
        ok = (key >= start) & (key <= qi + y * ROW_TOK)
        mask[:, j * ROW_TOK : (j + 1) * ROW_TOK] = jnp.where(ok, 0.0, NEG)

    for h in range(4):
        left = (x == 1) if h == 2 else ((x == 1) | (x == 3))
        pick = jnp.where(left, 1, 0) if h < 3 else 0
        qh = q[:, h * HEAD : (h + 1) * HEAD]
        parts = []
        vals = []
        for j, (pa, pb) in enumerate(((a0, b0), (a1, b1), (a2, b2), (a3, b3))):
            kv = jnp.where(pick == 1, pb[...], pa[...]) if h < 3 else pa[...]
            s = lax.dot_general(
                qh, kv[:, :HEAD], (((1,), (1,)), ((), ())), preferred_element_type=jnp.float32
            )
            parts.append(s * (HEAD**-0.5) + mask[:, j * ROW_TOK : (j + 1) * ROW_TOK])
            vals.append(kv[:, HEAD:])
        top = functools.reduce(jnp.maximum, [jnp.max(s, axis=1, keepdims=True) for s in parts])
        mass = jnp.zeros((ROW_TOK, 1), jnp.float32)
        acc = jnp.zeros((ROW_TOK, HEAD), jnp.float32)
        for s, v in zip(parts, vals):
            p = jnp.exp(s - top)
            mass += jnp.sum(p, axis=1, keepdims=True)
            acc += jnp.dot(p.astype(jnp.bfloat16), v, preferred_element_type=jnp.float32)
        full[:, h * HEAD : (h + 1) * HEAD] = (acc / mass).astype(jnp.bfloat16)
    for j, o in enumerate((o0, o1, o2, o3)):
        o[...] = full[pl.ds(pl.multiple_of(lax.rem(x + j, 4) * 64, 64), 64), :]


def cache_rows(a0, a1, a2, a3, after1, after2, after3, t0, t1, t2, t3):
    x = lax.axis_index("x")
    y = lax.axis_index("y")
    i = lax.broadcasted_iota(jnp.int32, (64, ROW_TOK), 0)
    t = lax.broadcasted_iota(jnp.int32, (64, ROW_TOK), 1)
    want = 16 * lax.rem(i, 16) + 4 * y + lax.rem(x + lax.div(i, 16), 4)
    select = jnp.where(t == want, 1.0, 0.0).astype(jnp.bfloat16)
    for j, a in enumerate((a0, a1, a2, a3)):
        got = jnp.dot(select, a[...], preferred_element_type=jnp.float32).astype(jnp.bfloat16)
        rows = pl.ds(pl.multiple_of(lax.rem(y + j, 4) * 16, 16), 16)
        for k, out in enumerate((t0, t1, t2, t3)):
            out[rows, :] = got[16 * k : 16 * k + 16]


def cache_heads(t0, t1, t2, t3, out, buf):
    x = lax.axis_index("x")
    for j, t in enumerate((t0, t1, t2, t3)):
        buf[lax.rem(x + 4 - j, 4)] = t[...]
    for k, src in enumerate((0, 1, 3)):
        out[:, k * HEAD : (k + 1) * HEAD] = buf[src, :, :HEAD]
        out[:, (3 + k) * HEAD : (4 + k) * HEAD] = buf[src, :, HEAD:]


def cache_join(c0, c1, c2, c3, after, out):
    for n, c in enumerate((c0, c1, c2, c3)):
        out[n] = c[...]


def finish(plan, own, other, r0, r1, r2, r3, attended, cache):
    x = lax.axis_index("x")
    for j, r in enumerate((r0, r1, r2, r3)):
        low = pl.multiple_of(lax.rem(x + 4 - j, 4) * 512, 512)
        attended[:, pl.ds(low, 512)] = r[...]
    z = lax.axis_index("z")
    core = lax.axis_index("core")
    group = 2 * z + core
    for ref, t in ((own, core), (other, 1 - core)):
        for j in range(4):
            e = 2 * lax.rem(z + j, 4) + t
            rows = pl.ds(pl.multiple_of(e * 64, 64), 64)
            v = ref[j]
            cache[0, 0, rows, :] = jnp.where(plan[e, 0] == group, v, jnp.zeros_like(v))


def per_device(tokens, gain, q_weight, key_value_weight, q_bias, kv_bias, plan, home_offsets):
    bf = jnp.bfloat16
    f32 = jnp.float32
    blocks = call(
        cut,
        [((28, COLS), bf)] * 4,
        (q_weight, key_value_weight),
        [ANY] * 2,
        [
            pltpu.VMEM((28, 2048), bf),
            pltpu.VMEM((28, 768), bf),
            pltpu.SemaphoreType.DMA((2,)),
        ],
        grant=60,
    )
    (kept,) = call(keep, [((28, COLS), bf)], (blocks[0],), [ANY], [pltpu.SemaphoreType.DMA])
    got = [kept] + spread(lambda j: send(blocks[j], along_x(j)))
    (w0,) = call(place, [((112, COLS), bf)], got, scratch=[pltpu.VMEM((4, 28, COLS), f32)])
    (n0,) = call(norm, [((64, 3584), bf)], (tokens, gain, w0), [VM, VM, ANY])
    (s0,) = call(
        stage,
        [((4, 112, COLS), bf)],
        (w0, *spread(lambda j: send(w0, along_first(-j))), n0),
        [VM] * 4 + [ANY],
    )
    n1 = send(n0, along_x(-1))
    n3 = send(n0, along_x(1))
    s1 = send(s0, along_second(-1))
    s3 = send(s0, along_second(1))
    own1, r1, r3, low, high = call(
        relay,
        [((12, 112, COLS), bf)] + [((2, 112, COLS), bf)] * 2 + [((32, 3584), bf)] * 2,
        (s0, s1, s3, n1, n3),
    )
    n2a = send(low, along_x(-1))
    n2b = send(high, along_x(1))
    s2a = send(r1, along_second(-1))
    s2b = send(r3, along_second(1))
    other1 = send(own1, other_core)
    (own2,) = call(
        join2, [((4, 112, COLS), bf)], (s2a, s2b, n2a, n2b), [VM] * 2 + [ANY] * 2
    )
    other2 = send(own2, other_core)
    w, x_all, cs, qb, kvb = call(
        gather,
        [
            ((32, 112, COLS), bf),
            ((ROW_TOK, 3584), bf),
            ((ROW_TOK, HEAD), f32),
            ((512,), f32),
            ((2, HEAD), f32),
        ],
        (
            home_offsets, own1, own2, other1, n0, n1, n2a, n2b, n3,
            jnp.asarray(rotary_table()), q_bias, kv_bias,
        ),
        [SM] + [VM] * 8 + [ANY] * 3,
        [pltpu.SemaphoreType.DMA((7,))],
    )
    w, kv = call(
        kv_project,
        [((32, 112, COLS), bf), ((ROW_TOK, 256), bf)],
        (w, other2, x_all, cs, kvb),
        input_output_aliases={0: 0},
    )
    (q,) = call(q_project, [((ROW_TOK, 512), bf)], (w, x_all, cs, qb))

    a = [kv] + spread(lambda j: send(kv, along_y(-j)))
    b = [send(v, pair_x) for v in a]
    rows = call(cache_rows, [((64, 256), bf)] * 4, (*a, q, b[0], b[1]), [VM] * 4 + [ANY] * 3)
    (mine,) = call(
        cache_heads,
        [((64, 768), bf)],
        (rows[0], *spread(lambda j: send(rows[j], along_x(j)))),
        scratch=[pltpu.VMEM((4, 64, 256), bf)],
    )
    outs = call(
        attend,
        [((64, 512), bf)] * 4,
        (home_offsets, q, *a, *b, mine),
        [SM] + [VM] * 9 + [ANY],
        [pltpu.VMEM((ROW_TOK, 1024), f32), pltpu.VMEM((ROW_TOK, 512), bf)],
    )
    (cached,) = call(
        cache_join,
        [((4, 64, 768), bf)],
        (mine, *spread(lambda j: send(mine, along_z(-j))), outs[0]),
        [VM] * 4 + [ANY],
    )
    attended, cache = call(
        finish,
        [((64, 2048), bf), ((1, 1, 512, 768), bf)],
        (
            plan,
            cached,
            send(cached, other_core),
            outs[0],
            *spread(lambda j: send(outs[j], along_x(j))),
        ),
        [SM] + [VM] * 6,
    )
    return attended, cache


def solution(mesh):
    fine = Mesh(mesh.devices.reshape(SIZES), EVERY)
    in_specs = (P(EVERY, None), P(), P(EVERY, None), P(EVERY, None), P(), P(), P(), P())
    out_specs = (P(EVERY, None), P(("z", "core"), ("y", "x"), None, None))
    return jax.shard_map(
        per_device, mesh=fine, in_specs=in_specs, out_specs=out_specs, check_vma=False
    )
```

```python
import functools

import jax
import jax.numpy as jnp
import numpy as np
from jax import lax
from jax.experimental import pallas as pl
from jax.experimental.pallas import tpu as pltpu
from jax.sharding import Mesh
from jax.sharding import PartitionSpec as P

HEAD = 128
NEG = -1e30
ROW_TOK = 256
COLS = 768

EVERY = ("z", "core", "y", "x")
SIZES = (4, 2, 4, 4)
VM = pl.BlockSpec(memory_space=pltpu.VMEM)
SM = pl.BlockSpec(memory_space=pltpu.SMEM)
ANY = pl.BlockSpec(memory_space=pl.ANY)


def rotary_table():
    angles = np.arange(1024)[:, None] * 1000000.0 ** (-np.arange(64) * 2.0 / HEAD)[None, :]
    return np.concatenate([np.cos(angles), np.sin(angles)], axis=1).astype(np.float32)


def flat(z, c, y, x):
    return ((z % 4 * 2 + c % 2) * 4 + y % 4) * 4 + x % 4


PLACES = [(z, c, y, x) for z in range(4) for c in range(2) for y in range(4) for x in range(4)]


def send(v, move):
    return lax.ppermute(v, EVERY, [(flat(*p), flat(*move(*p))) for p in PLACES])


def spread(one):
    return [one(j) for j in (2, 1, 3)]


HOPS = (0, 2, 1, 3)


def along_x(j):
    return lambda z, c, y, x: (z, c, y, x + j)


def along_z(j):
    return lambda z, c, y, x: (z + j, c, y, x)


def along_first(j):
    return lambda z, c, y, x: (z + j, c, y, x) if c == 0 else (z, c, y + j, x)


def along_second(j):
    return lambda z, c, y, x: (z, c, y + j, x) if c == 0 else (z + j, c, y, x)


def other_core(z, c, y, x):
    return (z, 1 - c, y, x)


def along_y(j):
    return lambda z, c, y, x: (z, c, y + j, x)


def pair_x(z, c, y, x):
    return (z, c, y, x ^ 1)


def call(kernel, outs, operands, in_specs=None, scratch=(), grant=20, **more):
    outs = tuple(jax.ShapeDtypeStruct(s, d) for s, d in outs)
    return pl.pallas_call(
        kernel,
        out_shape=outs,
        in_specs=[VM] * len(operands) if in_specs is None else in_specs,
        out_specs=(VM,) * len(outs),
        scratch_shapes=list(scratch),
        compiler_params=pltpu.CompilerParams(vmem_limit_bytes=grant * 1024 * 1024),
        name=kernel.__name__,
        **more,
    )(*operands)


def cut(wq, wkv, b0, b1, b2, b3, q_buf, kv_buf, sem):
    copies = [
        pltpu.make_async_copy(wq, q_buf, sem.at[0]),
        pltpu.make_async_copy(wkv, kv_buf, sem.at[1]),
    ]
    for copy in copies:
        copy.start()
    for copy in copies:
        copy.wait()
    x = lax.axis_index("x")
    for j, block in enumerate((b0, b1, b2, b3)):
        to = lax.rem(x + j, 4)
        slot = lax.div(to + 1, 2)
        for n in range(2):
            low = pl.multiple_of((slot + 3 * n) * HEAD, HEAD)
            block[:, n * HEAD : (n + 1) * HEAD] = kv_buf[:, pl.ds(low, HEAD)]
        block[:, 256:] = q_buf[:, pl.ds(pl.multiple_of(to * 512, 512), 512)]


def norm(tokens, gain, after, out):
    floats = tokens[...].astype(jnp.float32)
    mean = jnp.mean(floats * floats, axis=1, keepdims=True)
    out[...] = (floats * lax.rsqrt(mean + 1e-06) * gain[...][None, :]).astype(jnp.bfloat16)


def keep(v, out, sem):
    copy = pltpu.make_async_copy(v, out, sem)
    copy.start()
    copy.wait()


def place(p0, p2, p1, p3, out, buf):
    x = lax.axis_index("x")
    for j, p in zip(HOPS, (p0, p2, p1, p3)):
        buf[lax.rem(x + 4 - j, 4)] = p[...].astype(jnp.float32)
    out[...] = jnp.concatenate([buf[k] for k in range(4)], axis=0).astype(jnp.bfloat16)


def stage(s0, s2, s1, s3, after, block):
    for i, s in enumerate((s0, s1, s2, s3)):
        block[i] = s[...]


def relay(s0, s1, s3, n1, n3, joined, r1, r3, low, high):
    for n, s in enumerate((s0, s1, s3)):
        joined[4 * n : 4 * n + 4] = s[...]
    r1[...] = s1[:2]
    r3[...] = s3[2:]
    low[...] = n1[:32, :]
    high[...] = n3[32:, :]


def join2(a, b, after1, after2, out):
    out[:2] = a[...]
    out[2:] = b[...]


def load_weights(ref, t, places, buf):
    y = lax.axis_index("y")
    z = lax.axis_index("z")
    for n, (j, i) in enumerate(places):
        zz = lax.rem(z + jnp.where(t == 0, i, j), 4)
        yy = lax.rem(y + jnp.where(t == 0, j, i), 4)
        buf[(2 * zz + t) * 4 + yy] = ref[n]


FIRST = [(j, i) for j in (0, 1, 3) for i in range(4)]
LAST = [(2, i) for i in range(4)]


def gather(
    offsets, own1, own2, other1, n0, n1, n2a, n2b, n3, table, qb, kvb, w, x_out, cs, qb_out, kvb_out, sem
):
    e = 2 * lax.axis_index("z") + lax.axis_index("core")
    y = lax.axis_index("y")
    x = lax.axis_index("x")
    core = lax.axis_index("core")
    copies = []
    for k in range(4):
        s = 4 * y + k
        row = pl.multiple_of((s - offsets[e, s]) * 64, 64)
        copies.append(
            pltpu.make_async_copy(
                table.at[pl.ds(row, 64), :], cs.at[k * 64 : (k + 1) * 64, :], sem.at[k]
            )
        )
    copies.append(
        pltpu.make_async_copy(qb.at[pl.ds(pl.multiple_of(x * 512, 512), 512)], qb_out, sem.at[4])
    )
    slot = lax.div(x + 1, 2)
    for n in range(2):
        low = pl.multiple_of((slot + 3 * n) * HEAD, HEAD)
        copies.append(
            pltpu.make_async_copy(kvb.at[pl.ds(low, HEAD)], kvb_out.at[n], sem.at[5 + n])
        )
    for copy in copies:
        copy.start()
    for ref, j, low, size in (
        (n0, 0, 0, 64),
        (n1, 1, 0, 64),
        (n2a, 2, 0, 32),
        (n2b, 2, 32, 32),
        (n3, 3, 0, 64),
    ):
        row = pl.multiple_of(lax.rem(x + j, 4) * 64 + low, 32)
        x_out[pl.ds(row, size), :] = ref[...]
    load_weights(own1, core, FIRST, w)
    load_weights(own2, core, LAST, w)
    load_weights(other1, 1 - core, FIRST, w)
    for copy in copies:
        copy.wait()


def rotate(v, cos, sin):
    a = v[:, :64]
    b = v[:, 64:]
    return jnp.concatenate([a * cos - b * sin, b * cos + a * sin], axis=1).astype(jnp.bfloat16)


def kv_project(w_in, other2, x_in, cs, kvb, w, kv):
    del w_in
    load_weights(other2, 1 - lax.axis_index("core"), LAST, w)
    acc = jnp.dot(
        x_in[...], w[:, :, :256].reshape(3584, 256), preferred_element_type=jnp.float32
    )
    kv[:, :HEAD] = rotate(acc[:, :HEAD] + kvb[0][None, :], cs[:, :64], cs[:, 64:])
    kv[:, HEAD:] = (acc[:, HEAD:] + kvb[1][None, :]).astype(jnp.bfloat16)


def q_project(w, x_in, cs, qb, q):
    for g in range(2):
        part = slice((g + 1) * 256, (g + 2) * 256)
        acc = jnp.dot(
            x_in[...], w[:, :, part].reshape(3584, 256), preferred_element_type=jnp.float32
        )
        for h in range(2):
            low = (2 * g + h) * HEAD
            head = acc[:, h * HEAD : (h + 1) * HEAD] + qb[low : low + HEAD][None, :]
            q[:, low : low + HEAD] = rotate(head, cs[:, :64], cs[:, 64:])


def attend(offsets, q, a0, a1, a2, a3, b0, b1, b2, b3, after, o0, o1, o2, o3, mask, full):
    x = lax.axis_index("x")
    y = lax.axis_index("y")
    e = 2 * lax.axis_index("z") + lax.axis_index("core")
    qi = lax.broadcasted_iota(jnp.int32, (ROW_TOK, ROW_TOK), 0)
    ki = lax.broadcasted_iota(jnp.int32, (ROW_TOK, ROW_TOK), 1)
    starts = [offsets[e, 4 * y + k] * 64 for k in range(4)]
    start = jnp.where(
        qi < 128,
        jnp.where(qi < 64, starts[0], starts[1]),
        jnp.where(qi < 192, starts[2], starts[3]),
    )
    for j in range(4):
        key = ki + lax.rem(y + j, 4) * ROW_TOK
        ok = (key >= start) & (key <= qi + y * ROW_TOK)
        mask[:, j * ROW_TOK : (j + 1) * ROW_TOK] = jnp.where(ok, 0.0, NEG)

    for h in range(4):
        left = (x == 1) if h == 2 else ((x == 1) | (x == 3))
        pick = jnp.where(left, 1, 0) if h < 3 else 0
        qh = q[:, h * HEAD : (h + 1) * HEAD]
        parts = []
        vals = []
        for j, (pa, pb) in enumerate(((a0, b0), (a1, b1), (a2, b2), (a3, b3))):
            kv = jnp.where(pick == 1, pb[...], pa[...]) if h < 3 else pa[...]
            s = lax.dot_general(
                qh, kv[:, :HEAD], (((1,), (1,)), ((), ())), preferred_element_type=jnp.float32
            )
            parts.append(s * (HEAD**-0.5) + mask[:, j * ROW_TOK : (j + 1) * ROW_TOK])
            vals.append(kv[:, HEAD:])
        top = functools.reduce(jnp.maximum, [jnp.max(s, axis=1, keepdims=True) for s in parts])
        mass = jnp.zeros((ROW_TOK, 1), jnp.float32)
        acc = jnp.zeros((ROW_TOK, HEAD), jnp.float32)
        for s, v in zip(parts, vals):
            p = jnp.exp(s - top)
            mass += jnp.sum(p, axis=1, keepdims=True)
            acc += jnp.dot(p.astype(jnp.bfloat16), v, preferred_element_type=jnp.float32)
        full[:, h * HEAD : (h + 1) * HEAD] = (acc / mass).astype(jnp.bfloat16)
    for j, o in enumerate((o0, o1, o2, o3)):
        o[...] = full[pl.ds(pl.multiple_of(lax.rem(x + j, 4) * 64, 64), 64), :]


def cache_rows(a0, a2, a1, a3, after1, after2, after3, t0, t1, t2, t3):
    x = lax.axis_index("x")
    y = lax.axis_index("y")
    i = lax.broadcasted_iota(jnp.int32, (64, ROW_TOK), 0)
    t = lax.broadcasted_iota(jnp.int32, (64, ROW_TOK), 1)
    want = 16 * lax.rem(i, 16) + 4 * y + lax.rem(x + lax.div(i, 16), 4)
    select = jnp.where(t == want, 1.0, 0.0).astype(jnp.bfloat16)
    for j, a in zip(HOPS, (a0, a2, a1, a3)):
        got = jnp.dot(select, a[...], preferred_element_type=jnp.float32).astype(jnp.bfloat16)
        rows = pl.ds(pl.multiple_of(lax.rem(y + j, 4) * 16, 16), 16)
        for k, out in enumerate((t0, t1, t2, t3)):
            out[rows, :] = got[16 * k : 16 * k + 16]


def cache_heads(t0, t2, t1, t3, out, buf):
    x = lax.axis_index("x")
    for j, t in zip(HOPS, (t0, t2, t1, t3)):
        buf[lax.rem(x + 4 - j, 4)] = t[...]
    for k, src in enumerate((0, 1, 3)):
        out[:, k * HEAD : (k + 1) * HEAD] = buf[src, :, :HEAD]
        out[:, (3 + k) * HEAD : (4 + k) * HEAD] = buf[src, :, HEAD:]


def cache_join(c0, c2, c1, c3, after, out):
    for n, c in zip(HOPS, (c0, c2, c1, c3)):
        out[n] = c[...]


def finish(plan, own, other, r0, r2, r1, r3, attended, cache):
    x = lax.axis_index("x")
    for j, r in zip(HOPS, (r0, r2, r1, r3)):
        low = pl.multiple_of(lax.rem(x + 4 - j, 4) * 512, 512)
        attended[:, pl.ds(low, 512)] = r[...]
    z = lax.axis_index("z")
    core = lax.axis_index("core")
    group = 2 * z + core
    for ref, t in ((own, core), (other, 1 - core)):
        for j in range(4):
            e = 2 * lax.rem(z + j, 4) + t
            rows = pl.ds(pl.multiple_of(e * 64, 64), 64)
            v = ref[j]
            cache[0, 0, rows, :] = jnp.where(plan[e, 0] == group, v, jnp.zeros_like(v))


def per_device(tokens, gain, q_weight, key_value_weight, q_bias, kv_bias, plan, home_offsets):
    bf = jnp.bfloat16
    f32 = jnp.float32
    blocks = call(
        cut,
        [((28, COLS), bf)] * 4,
        (q_weight, key_value_weight),
        [ANY] * 2,
        [
            pltpu.VMEM((28, 2048), bf),
            pltpu.VMEM((28, 768), bf),
            pltpu.SemaphoreType.DMA((2,)),
        ],
        grant=60,
    )
    (kept,) = call(keep, [((28, COLS), bf)], (blocks[0],), [ANY], [pltpu.SemaphoreType.DMA])
    got = [kept] + spread(lambda j: send(blocks[j], along_x(j)))
    (w0,) = call(place, [((112, COLS), bf)], got, scratch=[pltpu.VMEM((4, 28, COLS), f32)])
    (n0,) = call(norm, [((64, 3584), bf)], (tokens, gain, w0), [VM, VM, ANY])
    (s0,) = call(
        stage,
        [((4, 112, COLS), bf)],
        (w0, *spread(lambda j: send(w0, along_first(-j))), n0),
        [VM] * 4 + [ANY],
    )
    n1 = send(n0, along_x(-1))
    n3 = send(n0, along_x(1))
    s1 = send(s0, along_second(-1))
    s3 = send(s0, along_second(1))
    own1, r1, r3, low, high = call(
        relay,
        [((12, 112, COLS), bf)] + [((2, 112, COLS), bf)] * 2 + [((32, 3584), bf)] * 2,
        (s0, s1, s3, n1, n3),
    )
    n2a = send(low, along_x(-1))
    n2b = send(high, along_x(1))
    s2a = send(r1, along_second(-1))
    s2b = send(r3, along_second(1))
    other1 = send(own1, other_core)
    (own2,) = call(
        join2, [((4, 112, COLS), bf)], (s2a, s2b, n2a, n2b), [VM] * 2 + [ANY] * 2
    )
    other2 = send(own2, other_core)
    w, x_all, cs, qb, kvb = call(
        gather,
        [
            ((32, 112, COLS), bf),
            ((ROW_TOK, 3584), bf),
            ((ROW_TOK, HEAD), f32),
            ((512,), f32),
            ((2, HEAD), f32),
        ],
        (
            home_offsets, own1, own2, other1, n0, n1, n2a, n2b, n3,
            jnp.asarray(rotary_table()), q_bias, kv_bias,
        ),
        [SM] + [VM] * 8 + [ANY] * 3,
        [pltpu.SemaphoreType.DMA((7,))],
    )
    w, kv = call(
        kv_project,
        [((32, 112, COLS), bf), ((ROW_TOK, 256), bf)],
        (w, other2, x_all, cs, kvb),
        input_output_aliases={0: 0},
    )
    (q,) = call(q_project, [((ROW_TOK, 512), bf)], (w, x_all, cs, qb))

    a2, a1, a3 = spread(lambda j: send(kv, along_y(-j)))
    a = [kv, a1, a2, a3]
    b = [send(v, pair_x) for v in a]
    rows = call(cache_rows, [((64, 256), bf)] * 4, (kv, a2, a1, a3, q, b[0], b[1]), [VM] * 4 + [ANY] * 3)
    (mine,) = call(
        cache_heads,
        [((64, 768), bf)],
        (rows[0], *spread(lambda j: send(rows[j], along_x(j)))),
        scratch=[pltpu.VMEM((4, 64, 256), bf)],
    )
    outs = call(
        attend,
        [((64, 512), bf)] * 4,
        (home_offsets, q, *a, *b, mine),
        [SM] + [VM] * 9 + [ANY],
        [pltpu.VMEM((ROW_TOK, 1024), f32), pltpu.VMEM((ROW_TOK, 512), bf)],
    )
    (cached,) = call(
        cache_join,
        [((4, 64, 768), bf)],
        (mine, *spread(lambda j: send(mine, along_z(-j))), outs[0]),
        [VM] * 4 + [ANY],
    )
    attended, cache = call(
        finish,
        [((64, 2048), bf), ((1, 1, 512, 768), bf)],
        (
            plan,
            cached,
            send(cached, other_core),
            outs[0],
            *spread(lambda j: send(outs[j], along_x(j))),
        ),
        [SM] + [VM] * 6,
    )
    return attended, cache


def solution(mesh):
    fine = Mesh(mesh.devices.reshape(SIZES), EVERY)
    in_specs = (P(EVERY, None), P(), P(EVERY, None), P(EVERY, None), P(), P(), P(), P())
    out_specs = (P(EVERY, None), P(("z", "core"), ("y", "x"), None, None))
    return jax.shard_map(
        per_device, mesh=fine, in_specs=in_specs, out_specs=out_specs, check_vma=False
    )
```

```python
import functools

import jax
import jax.numpy as jnp
import numpy as np
from jax import lax
from jax.experimental import pallas as pl
from jax.experimental.pallas import tpu as pltpu
from jax.sharding import Mesh
from jax.sharding import PartitionSpec as P

HEAD = 128
NEG = -1e30
ROW_TOK = 256
COLS = 768

EVERY = ("z", "core", "y", "x")
SIZES = (4, 2, 4, 4)
VM = pl.BlockSpec(memory_space=pltpu.VMEM)
SM = pl.BlockSpec(memory_space=pltpu.SMEM)
ANY = pl.BlockSpec(memory_space=pl.ANY)


def rotary_table():
    angles = np.arange(1024)[:, None] * 1000000.0 ** (-np.arange(64) * 2.0 / HEAD)[None, :]
    return np.concatenate([np.cos(angles), np.sin(angles)], axis=1).astype(np.float32)


def flat(z, c, y, x):
    return ((z % 4 * 2 + c % 2) * 4 + y % 4) * 4 + x % 4


PLACES = [(z, c, y, x) for z in range(4) for c in range(2) for y in range(4) for x in range(4)]


def send(v, move):
    return lax.ppermute(v, EVERY, [(flat(*p), flat(*move(*p))) for p in PLACES])


def spread(one):
    return [one(j) for j in (2, 1, 3)]


HOPS = (0, 2, 1, 3)


def along_x(j):
    return lambda z, c, y, x: (z, c, y, x + j)


def along_z(j):
    return lambda z, c, y, x: (z + j, c, y, x)


def along_first(j):
    return lambda z, c, y, x: (z + j, c, y, x) if c == 0 else (z, c, y + j, x)


def along_second(j):
    return lambda z, c, y, x: (z, c, y + j, x) if c == 0 else (z + j, c, y, x)


def other_core(z, c, y, x):
    return (z, 1 - c, y, x)


def along_y(j):
    return lambda z, c, y, x: (z, c, y + j, x)


def pair_x(z, c, y, x):
    return (z, c, y, x ^ 1)


def call(kernel, outs, operands, in_specs=None, scratch=(), grant=20, **more):
    outs = tuple(jax.ShapeDtypeStruct(s, d) for s, d in outs)
    return pl.pallas_call(
        kernel,
        out_shape=outs,
        in_specs=[VM] * len(operands) if in_specs is None else in_specs,
        out_specs=(VM,) * len(outs),
        scratch_shapes=list(scratch),
        compiler_params=pltpu.CompilerParams(vmem_limit_bytes=grant * 1024 * 1024),
        name=kernel.__name__,
        **more,
    )(*operands)


def cut(wq, wkv, b0, b1, b2, b3, q_buf, kv_buf, sem):
    copies = [
        pltpu.make_async_copy(wq, q_buf, sem.at[0]),
        pltpu.make_async_copy(wkv, kv_buf, sem.at[1]),
    ]
    for copy in copies:
        copy.start()
    for copy in copies:
        copy.wait()
    x = lax.axis_index("x")
    for j, block in enumerate((b0, b1, b2, b3)):
        to = lax.rem(x + j, 4)
        slot = lax.div(to + 1, 2)
        for n in range(2):
            low = pl.multiple_of((slot + 3 * n) * HEAD, HEAD)
            block[:, n * HEAD : (n + 1) * HEAD] = kv_buf[:, pl.ds(low, HEAD)]
        block[:, 256:] = q_buf[:, pl.ds(pl.multiple_of(to * 512, 512), 512)]


def norm(tokens, gain, after, out, low16, low48, high16, high48):
    floats = tokens[...].astype(jnp.float32)
    mean = jnp.mean(floats * floats, axis=1, keepdims=True)
    rows = (floats * lax.rsqrt(mean + 1e-06) * gain[...][None, :]).astype(jnp.bfloat16)
    out[...] = rows
    low16[...] = rows[:16]
    low48[...] = rows[:48]
    high16[...] = rows[48:]
    high48[...] = rows[16:]


def keep(v, out, sem):
    copy = pltpu.make_async_copy(v, out, sem)
    copy.start()
    copy.wait()


def place(p0, p2, p1, p3, out, buf):
    x = lax.axis_index("x")
    for j, p in zip(HOPS, (p0, p2, p1, p3)):
        buf[lax.rem(x + 4 - j, 4)] = p[...].astype(jnp.float32)
    out[...] = jnp.concatenate([buf[k] for k in range(4)], axis=0).astype(jnp.bfloat16)


def stage(s0, s2, s1, s3, after1, after2, block):
    for i, s in enumerate((s0, s1, s2, s3)):
        block[i] = s[...]


def relay(s0, s1, s3, n1a, n1b, n3a, n3b, joined, r1, r3, low, high):
    for n, s in enumerate((s0, s1, s3)):
        joined[4 * n : 4 * n + 4] = s[...]
    r1[...] = s1[:2]
    r3[...] = s3[2:]
    low[:16, :] = n1a[...]
    low[16:, :] = n1b[:16, :]
    high[:16, :] = n3b[32:, :]
    high[16:, :] = n3a[...]


def join2(after1, after2, a, b, out):
    out[:2] = a[...]
    out[2:] = b[...]


def load_weights(ref, t, places, buf):
    y = lax.axis_index("y")
    z = lax.axis_index("z")
    for n, (j, i) in enumerate(places):
        zz = lax.rem(z + jnp.where(t == 0, i, j), 4)
        yy = lax.rem(y + jnp.where(t == 0, j, i), 4)
        buf[(2 * zz + t) * 4 + yy] = ref[n]


FIRST = [(j, i) for j in (0, 1, 3) for i in range(4)]
LAST = [(2, i) for i in range(4)]


def gather(
    offsets,
    own1,
    own2,
    other1,
    n0,
    n1a,
    n1b,
    n2a,
    n2b,
    n3a,
    n3b,
    table,
    qb,
    kvb,
    w,
    x_out,
    cs,
    qb_out,
    kvb_out,
    sem,
):
    e = 2 * lax.axis_index("z") + lax.axis_index("core")
    y = lax.axis_index("y")
    x = lax.axis_index("x")
    core = lax.axis_index("core")
    copies = []
    for k in range(4):
        s = 4 * y + k
        row = pl.multiple_of((s - offsets[e, s]) * 64, 64)
        copies.append(
            pltpu.make_async_copy(
                table.at[pl.ds(row, 64), :], cs.at[k * 64 : (k + 1) * 64, :], sem.at[k]
            )
        )
    copies.append(
        pltpu.make_async_copy(qb.at[pl.ds(pl.multiple_of(x * 512, 512), 512)], qb_out, sem.at[4])
    )
    slot = lax.div(x + 1, 2)
    for n in range(2):
        low = pl.multiple_of((slot + 3 * n) * HEAD, HEAD)
        copies.append(
            pltpu.make_async_copy(kvb.at[pl.ds(low, HEAD)], kvb_out.at[n], sem.at[5 + n])
        )
    for copy in copies:
        copy.start()
    for ref, j, low, size in (
        (n0, 0, 0, 64),
        (n1a, 1, 0, 16),
        (n1b, 1, 16, 48),
        (n2a, 2, 0, 32),
        (n2b, 2, 32, 32),
        (n3b, 3, 0, 48),
        (n3a, 3, 48, 16),
    ):
        row = pl.multiple_of(lax.rem(x + j, 4) * 64 + low, 16)
        x_out[pl.ds(row, size), :] = ref[...]
    load_weights(own1, core, FIRST, w)
    load_weights(own2, core, LAST, w)
    load_weights(other1, 1 - core, FIRST, w)
    for copy in copies:
        copy.wait()


def rotate(v, cos, sin):
    a = v[:, :64]
    b = v[:, 64:]
    return jnp.concatenate([a * cos - b * sin, b * cos + a * sin], axis=1).astype(jnp.bfloat16)


def kv_project(w_in, other2, x_in, cs, kvb, w, kv):
    del w_in
    load_weights(other2, 1 - lax.axis_index("core"), LAST, w)
    acc = jnp.dot(
        x_in[...], w[:, :, :256].reshape(3584, 256), preferred_element_type=jnp.float32
    )
    kv[:, :HEAD] = rotate(acc[:, :HEAD] + kvb[0][None, :], cs[:, :64], cs[:, 64:])
    kv[:, HEAD:] = (acc[:, HEAD:] + kvb[1][None, :]).astype(jnp.bfloat16)


def q_project(w, x_in, cs, qb, q):
    for g in range(2):
        part = slice((g + 1) * 256, (g + 2) * 256)
        acc = jnp.dot(
            x_in[...], w[:, :, part].reshape(3584, 256), preferred_element_type=jnp.float32
        )
        for h in range(2):
            low = (2 * g + h) * HEAD
            head = acc[:, h * HEAD : (h + 1) * HEAD] + qb[low : low + HEAD][None, :]
            q[:, low : low + HEAD] = rotate(head, cs[:, :64], cs[:, 64:])


def attend(offsets, q, a0, a1, a2, a3, b0, b1, b2, b3, after, o0, o1, o2, o3, mask, full):
    x = lax.axis_index("x")
    y = lax.axis_index("y")
    e = 2 * lax.axis_index("z") + lax.axis_index("core")
    qi = lax.broadcasted_iota(jnp.int32, (ROW_TOK, ROW_TOK), 0)
    ki = lax.broadcasted_iota(jnp.int32, (ROW_TOK, ROW_TOK), 1)
    starts = [offsets[e, 4 * y + k] * 64 for k in range(4)]
    start = jnp.where(
        qi < 128,
        jnp.where(qi < 64, starts[0], starts[1]),
        jnp.where(qi < 192, starts[2], starts[3]),
    )
    for j in range(4):
        key = ki + lax.rem(y + j, 4) * ROW_TOK
        ok = (key >= start) & (key <= qi + y * ROW_TOK)
        mask[:, j * ROW_TOK : (j + 1) * ROW_TOK] = jnp.where(ok, 0.0, NEG)

    for h in range(4):
        left = (x == 1) if h == 2 else ((x == 1) | (x == 3))
        pick = jnp.where(left, 1, 0) if h < 3 else 0
        qh = q[:, h * HEAD : (h + 1) * HEAD]
        parts = []
        vals = []
        for j, (pa, pb) in enumerate(((a0, b0), (a1, b1), (a2, b2), (a3, b3))):
            kv = jnp.where(pick == 1, pb[...], pa[...]) if h < 3 else pa[...]
            s = lax.dot_general(
                qh, kv[:, :HEAD], (((1,), (1,)), ((), ())), preferred_element_type=jnp.float32
            )
            parts.append(s * (HEAD**-0.5) + mask[:, j * ROW_TOK : (j + 1) * ROW_TOK])
            vals.append(kv[:, HEAD:])
        top = functools.reduce(jnp.maximum, [jnp.max(s, axis=1, keepdims=True) for s in parts])
        mass = jnp.zeros((ROW_TOK, 1), jnp.float32)
        acc = jnp.zeros((ROW_TOK, HEAD), jnp.float32)
        for s, v in zip(parts, vals):
            p = jnp.exp(s - top)
            mass += jnp.sum(p, axis=1, keepdims=True)
            acc += jnp.dot(p.astype(jnp.bfloat16), v, preferred_element_type=jnp.float32)
        full[:, h * HEAD : (h + 1) * HEAD] = (acc / mass).astype(jnp.bfloat16)
    for j, o in enumerate((o0, o1, o2, o3)):
        o[...] = full[pl.ds(pl.multiple_of(lax.rem(x + j, 4) * 64, 64), 64), :]


def cache_rows(a0, a2, a1, a3, after1, after2, after3, t0, t1, t2, t3):
    x = lax.axis_index("x")
    y = lax.axis_index("y")
    i = lax.broadcasted_iota(jnp.int32, (64, ROW_TOK), 0)
    t = lax.broadcasted_iota(jnp.int32, (64, ROW_TOK), 1)
    want = 16 * lax.rem(i, 16) + 4 * y + lax.rem(x + lax.div(i, 16), 4)
    select = jnp.where(t == want, 1.0, 0.0).astype(jnp.bfloat16)
    for j, a in zip(HOPS, (a0, a2, a1, a3)):
        got = jnp.dot(select, a[...], preferred_element_type=jnp.float32).astype(jnp.bfloat16)
        rows = pl.ds(pl.multiple_of(lax.rem(y + j, 4) * 16, 16), 16)
        for k, out in enumerate((t0, t1, t2, t3)):
            out[rows, :] = got[16 * k : 16 * k + 16]


def cache_heads(t0, t2, t1, t3, out, buf):
    x = lax.axis_index("x")
    for j, t in zip(HOPS, (t0, t2, t1, t3)):
        buf[lax.rem(x + 4 - j, 4)] = t[...]
    for k, src in enumerate((0, 1, 3)):
        out[:, k * HEAD : (k + 1) * HEAD] = buf[src, :, :HEAD]
        out[:, (3 + k) * HEAD : (4 + k) * HEAD] = buf[src, :, HEAD:]


def cache_join(c0, c2, c1, c3, after, out):
    for n, c in zip(HOPS, (c0, c2, c1, c3)):
        out[n] = c[...]


def finish(plan, own, other, r0, r2, r1, r3, attended, cache):
    x = lax.axis_index("x")
    for j, r in zip(HOPS, (r0, r2, r1, r3)):
        low = pl.multiple_of(lax.rem(x + 4 - j, 4) * 512, 512)
        attended[:, pl.ds(low, 512)] = r[...]
    z = lax.axis_index("z")
    core = lax.axis_index("core")
    group = 2 * z + core
    for ref, t in ((own, core), (other, 1 - core)):
        for j in range(4):
            e = 2 * lax.rem(z + j, 4) + t
            rows = pl.ds(pl.multiple_of(e * 64, 64), 64)
            v = ref[j]
            cache[0, 0, rows, :] = jnp.where(plan[e, 0] == group, v, jnp.zeros_like(v))


def per_device(tokens, gain, q_weight, key_value_weight, q_bias, kv_bias, plan, home_offsets):
    bf = jnp.bfloat16
    f32 = jnp.float32
    blocks = call(
        cut,
        [((28, COLS), bf)] * 4,
        (q_weight, key_value_weight),
        [ANY] * 2,
        [
            pltpu.VMEM((28, 2048), bf),
            pltpu.VMEM((28, 768), bf),
            pltpu.SemaphoreType.DMA((2,)),
        ],
        grant=60,
    )
    (kept,) = call(keep, [((28, COLS), bf)], (blocks[0],), [ANY], [pltpu.SemaphoreType.DMA])
    got = [kept] + spread(lambda j: send(blocks[j], along_x(j)))
    (w0,) = call(place, [((112, COLS), bf)], got, scratch=[pltpu.VMEM((4, 28, COLS), f32)])
    n0, low16, low48, high16, high48 = call(
        norm,
        [((n, 3584), bf) for n in (64, 16, 48, 16, 48)],
        (tokens, gain, kept),
        [VM, VM, ANY],
    )
    n1a = send(low16, along_x(-1))
    n3a = send(high16, along_x(1))
    (s0,) = call(
        stage,
        [((4, 112, COLS), bf)],
        (w0, *spread(lambda j: send(w0, along_first(-j))), n1a, n3a),
        [VM] * 4 + [ANY] * 2,
    )
    n1b = send(high48, along_x(-1))
    n3b = send(low48, along_x(1))
    s1 = send(s0, along_second(-1))
    s3 = send(s0, along_second(1))
    own1, r1, r3, low, high = call(
        relay,
        [((12, 112, COLS), bf)] + [((2, 112, COLS), bf)] * 2 + [((32, 3584), bf)] * 2,
        (s0, s1, s3, n1a, n1b, n3a, n3b),
    )
    n2a = send(low, along_x(-1))
    n2b = send(high, along_x(1))
    s2a = send(r1, along_second(-1))
    s2b = send(r3, along_second(1))
    other1 = send(own1, other_core)
    (own2,) = call(
        join2, [((4, 112, COLS), bf)], (n2a, n2b, s2a, s2b), [ANY] * 2 + [VM] * 2
    )
    other2 = send(own2, other_core)
    w, x_all, cs, qb, kvb = call(
        gather,
        [
            ((32, 112, COLS), bf),
            ((ROW_TOK, 3584), bf),
            ((ROW_TOK, HEAD), f32),
            ((512,), f32),
            ((2, HEAD), f32),
        ],
        (
            home_offsets, own1, own2, other1, n0, n1a, n1b, n2a, n2b, n3a, n3b,
            jnp.asarray(rotary_table()), q_bias, kv_bias,
        ),
        [SM] + [VM] * 10 + [ANY] * 3,
        [pltpu.SemaphoreType.DMA((7,))],
    )
    w, kv = call(
        kv_project,
        [((32, 112, COLS), bf), ((ROW_TOK, 256), bf)],
        (w, other2, x_all, cs, kvb),
        input_output_aliases={0: 0},
    )
    (q,) = call(q_project, [((ROW_TOK, 512), bf)], (w, x_all, cs, qb))

    a2, a1, a3 = spread(lambda j: send(kv, along_y(-j)))
    a = [kv, a1, a2, a3]
    b = [send(v, pair_x) for v in a]
    rows = call(cache_rows, [((64, 256), bf)] * 4, (kv, a2, a1, a3, q, b[0], b[1]), [VM] * 4 + [ANY] * 3)
    (mine,) = call(
        cache_heads,
        [((64, 768), bf)],
        (rows[0], *spread(lambda j: send(rows[j], along_x(j)))),
        scratch=[pltpu.VMEM((4, 64, 256), bf)],
    )
    outs = call(
        attend,
        [((64, 512), bf)] * 4,
        (home_offsets, q, *a, *b, mine),
        [SM] + [VM] * 9 + [ANY],
        [pltpu.VMEM((ROW_TOK, 1024), f32), pltpu.VMEM((ROW_TOK, 512), bf)],
    )
    (cached,) = call(
        cache_join,
        [((4, 64, 768), bf)],
        (mine, *spread(lambda j: send(mine, along_z(-j))), outs[0]),
        [VM] * 4 + [ANY],
    )
    attended, cache = call(
        finish,
        [((64, 2048), bf), ((1, 1, 512, 768), bf)],
        (
            plan,
            cached,
            send(cached, other_core),
            outs[0],
            *spread(lambda j: send(outs[j], along_x(j))),
        ),
        [SM] + [VM] * 6,
    )
    return attended, cache


def solution(mesh):
    fine = Mesh(mesh.devices.reshape(SIZES), EVERY)
    in_specs = (P(EVERY, None), P(), P(EVERY, None), P(EVERY, None), P(), P(), P(), P())
    out_specs = (P(EVERY, None), P(("z", "core"), ("y", "x"), None, None))
    return jax.shard_map(
        per_device, mesh=fine, in_specs=in_specs, out_specs=out_specs, check_vma=False
    )
```

```python
import functools

import jax
import jax.numpy as jnp
import numpy as np
from jax import lax
from jax.experimental import pallas as pl
from jax.experimental.pallas import tpu as pltpu
from jax.sharding import Mesh
from jax.sharding import PartitionSpec as P

HEAD = 128
NEG = -1e30
ROW_TOK = 256
COLS = 768

EVERY = ("z", "core", "y", "x")
SIZES = (4, 2, 4, 4)
VM = pl.BlockSpec(memory_space=pltpu.VMEM)
SM = pl.BlockSpec(memory_space=pltpu.SMEM)
ANY = pl.BlockSpec(memory_space=pl.ANY)


def rotary_table():
    angles = np.arange(1024)[:, None] * 1000000.0 ** (-np.arange(64) * 2.0 / HEAD)[None, :]
    return np.concatenate([np.cos(angles), np.sin(angles)], axis=1).astype(np.float32)


def flat(z, c, y, x):
    return ((z % 4 * 2 + c % 2) * 4 + y % 4) * 4 + x % 4


PLACES = [(z, c, y, x) for z in range(4) for c in range(2) for y in range(4) for x in range(4)]


def send(v, move):
    return lax.ppermute(v, EVERY, [(flat(*p), flat(*move(*p))) for p in PLACES])


def spread(one):
    return [one(j) for j in (2, 1, 3)]


HOPS = (0, 2, 1, 3)


def along_x(j):
    return lambda z, c, y, x: (z, c, y, x + j)


def along_z(j):
    return lambda z, c, y, x: (z + j, c, y, x)


def along_first(j):
    return lambda z, c, y, x: (z + j, c, y, x) if c == 0 else (z, c, y + j, x)


def along_second(j):
    return lambda z, c, y, x: (z, c, y + j, x) if c == 0 else (z + j, c, y, x)


def other_core(z, c, y, x):
    return (z, 1 - c, y, x)


def along_y(j):
    return lambda z, c, y, x: (z, c, y + j, x)


def pair_x(z, c, y, x):
    return (z, c, y, x ^ 1)


def call(kernel, outs, operands, in_specs=None, scratch=(), grant=20, **more):
    outs = tuple(jax.ShapeDtypeStruct(s, d) for s, d in outs)
    return pl.pallas_call(
        kernel,
        out_shape=outs,
        in_specs=[VM] * len(operands) if in_specs is None else in_specs,
        out_specs=(VM,) * len(outs),
        scratch_shapes=list(scratch),
        compiler_params=pltpu.CompilerParams(vmem_limit_bytes=grant * 1024 * 1024),
        name=kernel.__name__,
        **more,
    )(*operands)


def cut(wq, wkv, b0, b1, b2, b3, q_buf, kv_buf, sem):
    copies = [
        pltpu.make_async_copy(wq, q_buf, sem.at[0]),
        pltpu.make_async_copy(wkv, kv_buf, sem.at[1]),
    ]
    for copy in copies:
        copy.start()
    for copy in copies:
        copy.wait()
    x = lax.axis_index("x")
    for j, block in enumerate((b0, b1, b2, b3)):
        to = lax.rem(x + j, 4)
        slot = lax.div(to + 1, 2)
        for n in range(2):
            low = pl.multiple_of((slot + 3 * n) * HEAD, HEAD)
            block[:, n * HEAD : (n + 1) * HEAD] = kv_buf[:, pl.ds(low, HEAD)]
        block[:, 256:] = q_buf[:, pl.ds(pl.multiple_of(to * 512, 512), 512)]


def norm(tokens, gain, after, out):
    floats = tokens[...].astype(jnp.float32)
    mean = jnp.mean(floats * floats, axis=1, keepdims=True)
    out[...] = (floats * lax.rsqrt(mean + 1e-06) * gain[...][None, :]).astype(jnp.bfloat16)


def keep(v, out, sem):
    copy = pltpu.make_async_copy(v, out, sem)
    copy.start()
    copy.wait()


def place(p0, p2, p1, p3, out, buf):
    x = lax.axis_index("x")
    for j, p in zip(HOPS, (p0, p2, p1, p3)):
        buf[lax.rem(x + 4 - j, 4)] = p[...].astype(jnp.float32)
    out[...] = jnp.concatenate([buf[k] for k in range(4)], axis=0).astype(jnp.bfloat16)


def stage(s0, s2, s1, s3, after, block):
    for i, s in enumerate((s0, s1, s2, s3)):
        block[i] = s[...]


def relay(n1, n3, s0, s1, s3, joined, r1, r3, low, high):
    for n, s in enumerate((s0, s1, s3)):
        joined[4 * n : 4 * n + 4] = s[...]
    r1[...] = s1[:2]
    r3[...] = s3[2:]
    low[...] = n1[:32, :]
    high[...] = n3[32:, :]


def join2(after1, after2, a, b, out):
    out[:2] = a[...]
    out[2:] = b[...]


def load_weights(ref, t, places, buf):
    y = lax.axis_index("y")
    z = lax.axis_index("z")
    for n, (j, i) in enumerate(places):
        zz = lax.rem(z + jnp.where(t == 0, i, j), 4)
        yy = lax.rem(y + jnp.where(t == 0, j, i), 4)
        buf[(2 * zz + t) * 4 + yy] = ref[n]


FIRST = [(j, i) for j in (0, 1, 3) for i in range(4)]
LAST = [(2, i) for i in range(4)]


def gather(
    offsets, own1, own2, other1, n0, n1, n2a, n2b, n3, table, qb, kvb, w, x_out, cs, qb_out, kvb_out, sem
):
    e = 2 * lax.axis_index("z") + lax.axis_index("core")
    y = lax.axis_index("y")
    x = lax.axis_index("x")
    core = lax.axis_index("core")
    copies = []
    for k in range(4):
        s = 4 * y + k
        row = pl.multiple_of((s - offsets[e, s]) * 64, 64)
        copies.append(
            pltpu.make_async_copy(
                table.at[pl.ds(row, 64), :], cs.at[k * 64 : (k + 1) * 64, :], sem.at[k]
            )
        )
    copies.append(
        pltpu.make_async_copy(qb.at[pl.ds(pl.multiple_of(x * 512, 512), 512)], qb_out, sem.at[4])
    )
    slot = lax.div(x + 1, 2)
    for n in range(2):
        low = pl.multiple_of((slot + 3 * n) * HEAD, HEAD)
        copies.append(
            pltpu.make_async_copy(kvb.at[pl.ds(low, HEAD)], kvb_out.at[n], sem.at[5 + n])
        )
    for copy in copies:
        copy.start()
    for ref, j, low, size in (
        (n0, 0, 0, 64),
        (n1, 1, 0, 64),
        (n2a, 2, 0, 32),
        (n2b, 2, 32, 32),
        (n3, 3, 0, 64),
    ):
        row = pl.multiple_of(lax.rem(x + j, 4) * 64 + low, 32)
        x_out[pl.ds(row, size), :] = ref[...]
    load_weights(own1, core, FIRST, w)
    load_weights(own2, core, LAST, w)
    load_weights(other1, 1 - core, FIRST, w)
    for copy in copies:
        copy.wait()


def rotate(v, cos, sin):
    a = v[:, :64]
    b = v[:, 64:]
    return jnp.concatenate([a * cos - b * sin, b * cos + a * sin], axis=1).astype(jnp.bfloat16)


def kv_project(w_in, other2, x_in, cs, kvb, w, kv):
    del w_in
    load_weights(other2, 1 - lax.axis_index("core"), LAST, w)
    acc = jnp.dot(
        x_in[...], w[:, :, :256].reshape(3584, 256), preferred_element_type=jnp.float32
    )
    kv[:, :HEAD] = rotate(acc[:, :HEAD] + kvb[0][None, :], cs[:, :64], cs[:, 64:])
    kv[:, HEAD:] = (acc[:, HEAD:] + kvb[1][None, :]).astype(jnp.bfloat16)


def q_project(w, x_in, cs, qb, q):
    for g in range(2):
        part = slice((g + 1) * 256, (g + 2) * 256)
        acc = jnp.dot(
            x_in[...], w[:, :, part].reshape(3584, 256), preferred_element_type=jnp.float32
        )
        for h in range(2):
            low = (2 * g + h) * HEAD
            head = acc[:, h * HEAD : (h + 1) * HEAD] + qb[low : low + HEAD][None, :]
            q[:, low : low + HEAD] = rotate(head, cs[:, :64], cs[:, 64:])


def attend(offsets, q, a0, a1, a2, a3, b0, b1, b2, b3, after, o0, o1, o2, o3, mask, full):
    x = lax.axis_index("x")
    y = lax.axis_index("y")
    e = 2 * lax.axis_index("z") + lax.axis_index("core")
    qi = lax.broadcasted_iota(jnp.int32, (ROW_TOK, ROW_TOK), 0)
    ki = lax.broadcasted_iota(jnp.int32, (ROW_TOK, ROW_TOK), 1)
    starts = [offsets[e, 4 * y + k] * 64 for k in range(4)]
    start = jnp.where(
        qi < 128,
        jnp.where(qi < 64, starts[0], starts[1]),
        jnp.where(qi < 192, starts[2], starts[3]),
    )
    for j in range(4):
        key = ki + lax.rem(y + j, 4) * ROW_TOK
        ok = (key >= start) & (key <= qi + y * ROW_TOK)
        mask[:, j * ROW_TOK : (j + 1) * ROW_TOK] = jnp.where(ok, 0.0, NEG)

    for h in range(4):
        left = (x == 1) if h == 2 else ((x == 1) | (x == 3))
        pick = jnp.where(left, 1, 0) if h < 3 else 0
        qh = q[:, h * HEAD : (h + 1) * HEAD]
        parts = []
        vals = []
        for j, (pa, pb) in enumerate(((a0, b0), (a1, b1), (a2, b2), (a3, b3))):
            kv = jnp.where(pick == 1, pb[...], pa[...]) if h < 3 else pa[...]
            s = lax.dot_general(
                qh, kv[:, :HEAD], (((1,), (1,)), ((), ())), preferred_element_type=jnp.float32
            )
            parts.append(s * (HEAD**-0.5) + mask[:, j * ROW_TOK : (j + 1) * ROW_TOK])
            vals.append(kv[:, HEAD:])
        top = functools.reduce(jnp.maximum, [jnp.max(s, axis=1, keepdims=True) for s in parts])
        mass = jnp.zeros((ROW_TOK, 1), jnp.float32)
        acc = jnp.zeros((ROW_TOK, HEAD), jnp.float32)
        for s, v in zip(parts, vals):
            p = jnp.exp(s - top)
            mass += jnp.sum(p, axis=1, keepdims=True)
            acc += jnp.dot(p.astype(jnp.bfloat16), v, preferred_element_type=jnp.float32)
        full[:, h * HEAD : (h + 1) * HEAD] = (acc / mass).astype(jnp.bfloat16)
    for j, o in enumerate((o0, o1, o2, o3)):
        o[...] = full[pl.ds(pl.multiple_of(lax.rem(x + j, 4) * 64, 64), 64), :]


def cache_rows(a0, a2, a1, a3, after1, after2, after3, t0, t1, t2, t3):
    x = lax.axis_index("x")
    y = lax.axis_index("y")
    i = lax.broadcasted_iota(jnp.int32, (64, ROW_TOK), 0)
    t = lax.broadcasted_iota(jnp.int32, (64, ROW_TOK), 1)
    want = 16 * lax.rem(i, 16) + 4 * y + lax.rem(x + lax.div(i, 16), 4)
    select = jnp.where(t == want, 1.0, 0.0).astype(jnp.bfloat16)
    for j, a in zip(HOPS, (a0, a2, a1, a3)):
        got = jnp.dot(select, a[...], preferred_element_type=jnp.float32).astype(jnp.bfloat16)
        rows = pl.ds(pl.multiple_of(lax.rem(y + j, 4) * 16, 16), 16)
        for k, out in enumerate((t0, t1, t2, t3)):
            out[rows, :] = got[16 * k : 16 * k + 16]


def cache_heads(t0, t2, t1, t3, out, buf):
    x = lax.axis_index("x")
    for j, t in zip(HOPS, (t0, t2, t1, t3)):
        buf[lax.rem(x + 4 - j, 4)] = t[...]
    for k, src in enumerate((0, 1, 3)):
        out[:, k * HEAD : (k + 1) * HEAD] = buf[src, :, :HEAD]
        out[:, (3 + k) * HEAD : (4 + k) * HEAD] = buf[src, :, HEAD:]


def cache_join(c0, c2, c1, c3, after, out):
    for n, c in zip(HOPS, (c0, c2, c1, c3)):
        out[n] = c[...]


def finish(plan, own, other, r0, r2, r1, r3, attended, cache):
    x = lax.axis_index("x")
    for j, r in zip(HOPS, (r0, r2, r1, r3)):
        low = pl.multiple_of(lax.rem(x + 4 - j, 4) * 512, 512)
        attended[:, pl.ds(low, 512)] = r[...]
    z = lax.axis_index("z")
    core = lax.axis_index("core")
    group = 2 * z + core
    for ref, t in ((own, core), (other, 1 - core)):
        for j in range(4):
            e = 2 * lax.rem(z + j, 4) + t
            rows = pl.ds(pl.multiple_of(e * 64, 64), 64)
            v = ref[j]
            cache[0, 0, rows, :] = jnp.where(plan[e, 0] == group, v, jnp.zeros_like(v))


def per_device(tokens, gain, q_weight, key_value_weight, q_bias, kv_bias, plan, home_offsets):
    bf = jnp.bfloat16
    f32 = jnp.float32
    blocks = call(
        cut,
        [((28, COLS), bf)] * 4,
        (q_weight, key_value_weight),
        [ANY] * 2,
        [
            pltpu.VMEM((28, 2048), bf),
            pltpu.VMEM((28, 768), bf),
            pltpu.SemaphoreType.DMA((2,)),
        ],
        grant=60,
    )
    (kept,) = call(keep, [((28, COLS), bf)], (blocks[0],), [ANY], [pltpu.SemaphoreType.DMA])
    got = [kept] + spread(lambda j: send(blocks[j], along_x(j)))
    (w0,) = call(place, [((112, COLS), bf)], got, scratch=[pltpu.VMEM((4, 28, COLS), f32)])
    (n0,) = call(norm, [((64, 3584), bf)], (tokens, gain, w0), [VM, VM, ANY])
    (s0,) = call(
        stage,
        [((4, 112, COLS), bf)],
        (w0, *spread(lambda j: send(w0, along_first(-j))), n0),
        [VM] * 4 + [ANY],
    )
    n1 = send(n0, along_x(-1))
    n3 = send(n0, along_x(1))
    s1 = send(s0, along_second(-1))
    s3 = send(s0, along_second(1))
    own1, r1, r3, low, high = call(
        relay,
        [((12, 112, COLS), bf)] + [((2, 112, COLS), bf)] * 2 + [((32, 3584), bf)] * 2,
        (n1, n3, s0, s1, s3),
    )
    n2a = send(low, along_x(-1))
    n2b = send(high, along_x(1))
    s2a = send(r1, along_second(-1))
    s2b = send(r3, along_second(1))
    other1 = send(own1, other_core)
    (own2,) = call(
        join2, [((4, 112, COLS), bf)], (n2a, n2b, s2a, s2b), [ANY] * 2 + [VM] * 2
    )
    other2 = send(own2, other_core)
    w, x_all, cs, qb, kvb = call(
        gather,
        [
            ((32, 112, COLS), bf),
            ((ROW_TOK, 3584), bf),
            ((ROW_TOK, HEAD), f32),
            ((512,), f32),
            ((2, HEAD), f32),
        ],
        (
            home_offsets, own1, own2, other1, n0, n1, n2a, n2b, n3,
            jnp.asarray(rotary_table()), q_bias, kv_bias,
        ),
        [SM] + [VM] * 8 + [ANY] * 3,
        [pltpu.SemaphoreType.DMA((7,))],
    )
    w, kv = call(
        kv_project,
        [((32, 112, COLS), bf), ((ROW_TOK, 256), bf)],
        (w, other2, x_all, cs, kvb),
        input_output_aliases={0: 0},
    )
    (q,) = call(q_project, [((ROW_TOK, 512), bf)], (w, x_all, cs, qb))

    a2, a1, a3 = spread(lambda j: send(kv, along_y(-j)))
    a = [kv, a1, a2, a3]
    b = [send(v, pair_x) for v in a]
    rows = call(cache_rows, [((64, 256), bf)] * 4, (kv, a2, a1, a3, q, b[0], b[1]), [VM] * 4 + [ANY] * 3)
    (mine,) = call(
        cache_heads,
        [((64, 768), bf)],
        (rows[0], *spread(lambda j: send(rows[j], along_x(j)))),
        scratch=[pltpu.VMEM((4, 64, 256), bf)],
    )
    outs = call(
        attend,
        [((64, 512), bf)] * 4,
        (home_offsets, q, *a, *b, mine),
        [SM] + [VM] * 9 + [ANY],
        [pltpu.VMEM((ROW_TOK, 1024), f32), pltpu.VMEM((ROW_TOK, 512), bf)],
    )
    (cached,) = call(
        cache_join,
        [((4, 64, 768), bf)],
        (mine, *spread(lambda j: send(mine, along_z(-j))), outs[0]),
        [VM] * 4 + [ANY],
    )
    attended, cache = call(
        finish,
        [((64, 2048), bf), ((1, 1, 512, 768), bf)],
        (
            plan,
            cached,
            send(cached, other_core),
            outs[0],
            *spread(lambda j: send(outs[j], along_x(j))),
        ),
        [SM] + [VM] * 6,
    )
    return attended, cache


def solution(mesh):
    fine = Mesh(mesh.devices.reshape(SIZES), EVERY)
    in_specs = (P(EVERY, None), P(), P(EVERY, None), P(EVERY, None), P(), P(), P(), P())
    out_specs = (P(EVERY, None), P(("z", "core"), ("y", "x"), None, None))
    return jax.shard_map(
        per_device, mesh=fine, in_specs=in_specs, out_specs=out_specs, check_vma=False
    )
```

```python
import functools

import jax
import jax.numpy as jnp
import numpy as np
from jax import lax
from jax.experimental import pallas as pl
from jax.experimental.pallas import tpu as pltpu
from jax.sharding import Mesh
from jax.sharding import PartitionSpec as P

HEAD = 128
NEG = -1e30
ROW_TOK = 256
COLS = 768

EVERY = ("z", "core", "y", "x")
SIZES = (4, 2, 4, 4)
VM = pl.BlockSpec(memory_space=pltpu.VMEM)
SM = pl.BlockSpec(memory_space=pltpu.SMEM)
ANY = pl.BlockSpec(memory_space=pl.ANY)


def rotary_table():
    angles = np.arange(1024)[:, None] * 1000000.0 ** (-np.arange(64) * 2.0 / HEAD)[None, :]
    return np.concatenate([np.cos(angles), np.sin(angles)], axis=1).astype(np.float32)


def flat(z, c, y, x):
    return ((z % 4 * 2 + c % 2) * 4 + y % 4) * 4 + x % 4


PLACES = [(z, c, y, x) for z in range(4) for c in range(2) for y in range(4) for x in range(4)]


def send(v, move):
    return lax.ppermute(v, EVERY, [(flat(*p), flat(*move(*p))) for p in PLACES])


def spread(one):
    return [one(j) for j in (2, 1, 3)]


HOPS = (0, 2, 1, 3)


def along_x(j):
    return lambda z, c, y, x: (z, c, y, x + j)


def along_z(j):
    return lambda z, c, y, x: (z + j, c, y, x)


def along_first(j):
    return lambda z, c, y, x: (z + j, c, y, x) if c == 0 else (z, c, y + j, x)


def along_second(j):
    return lambda z, c, y, x: (z, c, y + j, x) if c == 0 else (z + j, c, y, x)


def other_core(z, c, y, x):
    return (z, 1 - c, y, x)


def along_y(j):
    return lambda z, c, y, x: (z, c, y + j, x)


def pair_x(z, c, y, x):
    return (z, c, y, x ^ 1)


def call(kernel, outs, operands, in_specs=None, scratch=(), grant=20, **more):
    outs = tuple(jax.ShapeDtypeStruct(s, d) for s, d in outs)
    return pl.pallas_call(
        kernel,
        out_shape=outs,
        in_specs=[VM] * len(operands) if in_specs is None else in_specs,
        out_specs=(VM,) * len(outs),
        scratch_shapes=list(scratch),
        compiler_params=pltpu.CompilerParams(vmem_limit_bytes=grant * 1024 * 1024),
        name=kernel.__name__,
        **more,
    )(*operands)


def cut(wq, wkv, b0, b1, b2, b3, q_buf, kv_buf, sem):
    copies = [
        pltpu.make_async_copy(wq, q_buf, sem.at[0]),
        pltpu.make_async_copy(wkv, kv_buf, sem.at[1]),
    ]
    for copy in copies:
        copy.start()
    for copy in copies:
        copy.wait()
    x = lax.axis_index("x")
    for j, block in enumerate((b0, b1, b2, b3)):
        to = lax.rem(x + j, 4)
        slot = lax.div(to + 1, 2)
        for n in range(2):
            low = pl.multiple_of((slot + 3 * n) * HEAD, HEAD)
            block[:, n * HEAD : (n + 1) * HEAD] = kv_buf[:, pl.ds(low, HEAD)]
        block[:, 256:] = q_buf[:, pl.ds(pl.multiple_of(to * 512, 512), 512)]


def norm(tokens, gain, after, out):
    floats = tokens[...].astype(jnp.float32)
    mean = jnp.mean(floats * floats, axis=1, keepdims=True)
    out[...] = (floats * lax.rsqrt(mean + 1e-06) * gain[...][None, :]).astype(jnp.bfloat16)


def keep(v, out, sem):
    copy = pltpu.make_async_copy(v, out, sem)
    copy.start()
    copy.wait()


def place(p0, p2, p1, p3, out, buf):
    x = lax.axis_index("x")
    for j, p in zip(HOPS, (p0, p2, p1, p3)):
        buf[lax.rem(x + 4 - j, 4)] = p[...].astype(jnp.float32)
    out[...] = jnp.concatenate([buf[k] for k in range(4)], axis=0).astype(jnp.bfloat16)


def stage(s0, s2, s1, s3, after, block):
    for i, s in enumerate((s0, s1, s2, s3)):
        block[i] = s[...]


def relay(n1, n3, s0, s1, s3, joined, low, high):
    for n, s in enumerate((s0, s1, s3)):
        joined[4 * n : 4 * n + 4] = s[...]
    low[...] = n1[:32, :]
    high[...] = n3[32:, :]


def hand_on(after1, after2, v, out):
    out[...] = v[...]


def load_weights(ref, t, places, buf):
    y = lax.axis_index("y")
    z = lax.axis_index("z")
    for n, (j, i) in enumerate(places):
        zz = lax.rem(z + jnp.where(t == 0, i, j), 4)
        yy = lax.rem(y + jnp.where(t == 0, j, i), 4)
        buf[(2 * zz + t) * 4 + yy] = ref[n]


FIRST = [(j, i) for j in (0, 1, 3) for i in range(4)]
LAST = [(2, i) for i in range(4)]


def gather(
    offsets, own1, own2, other1, n0, n1, n2a, n2b, n3, table, qb, kvb, w, x_out, cs, qb_out, kvb_out, sem
):
    e = 2 * lax.axis_index("z") + lax.axis_index("core")
    y = lax.axis_index("y")
    x = lax.axis_index("x")
    core = lax.axis_index("core")
    copies = []
    for k in range(4):
        s = 4 * y + k
        row = pl.multiple_of((s - offsets[e, s]) * 64, 64)
        copies.append(
            pltpu.make_async_copy(
                table.at[pl.ds(row, 64), :], cs.at[k * 64 : (k + 1) * 64, :], sem.at[k]
            )
        )
    copies.append(
        pltpu.make_async_copy(qb.at[pl.ds(pl.multiple_of(x * 512, 512), 512)], qb_out, sem.at[4])
    )
    slot = lax.div(x + 1, 2)
    for n in range(2):
        low = pl.multiple_of((slot + 3 * n) * HEAD, HEAD)
        copies.append(
            pltpu.make_async_copy(kvb.at[pl.ds(low, HEAD)], kvb_out.at[n], sem.at[5 + n])
        )
    for copy in copies:
        copy.start()
    for ref, j, low, size in (
        (n0, 0, 0, 64),
        (n1, 1, 0, 64),
        (n2a, 2, 0, 32),
        (n2b, 2, 32, 32),
        (n3, 3, 0, 64),
    ):
        row = pl.multiple_of(lax.rem(x + j, 4) * 64 + low, 32)
        x_out[pl.ds(row, size), :] = ref[...]
    load_weights(own1, core, FIRST, w)
    load_weights(own2, core, LAST, w)
    load_weights(other1, 1 - core, FIRST, w)
    for copy in copies:
        copy.wait()


def rotate(v, cos, sin):
    a = v[:, :64]
    b = v[:, 64:]
    return jnp.concatenate([a * cos - b * sin, b * cos + a * sin], axis=1).astype(jnp.bfloat16)


def kv_project(w_in, other2, x_in, cs, kvb, w, kv):
    del w_in
    load_weights(other2, 1 - lax.axis_index("core"), LAST, w)
    acc = jnp.dot(
        x_in[...], w[:, :, :256].reshape(3584, 256), preferred_element_type=jnp.float32
    )
    kv[:, :HEAD] = rotate(acc[:, :HEAD] + kvb[0][None, :], cs[:, :64], cs[:, 64:])
    kv[:, HEAD:] = (acc[:, HEAD:] + kvb[1][None, :]).astype(jnp.bfloat16)


def q_project(w, x_in, cs, qb, q):
    for g in range(2):
        part = slice((g + 1) * 256, (g + 2) * 256)
        acc = jnp.dot(
            x_in[...], w[:, :, part].reshape(3584, 256), preferred_element_type=jnp.float32
        )
        for h in range(2):
            low = (2 * g + h) * HEAD
            head = acc[:, h * HEAD : (h + 1) * HEAD] + qb[low : low + HEAD][None, :]
            q[:, low : low + HEAD] = rotate(head, cs[:, :64], cs[:, 64:])


def attend(offsets, q, a0, a1, a2, a3, b0, b1, b2, b3, after, o0, o1, o2, o3, mask, full):
    x = lax.axis_index("x")
    y = lax.axis_index("y")
    e = 2 * lax.axis_index("z") + lax.axis_index("core")
    qi = lax.broadcasted_iota(jnp.int32, (ROW_TOK, ROW_TOK), 0)
    ki = lax.broadcasted_iota(jnp.int32, (ROW_TOK, ROW_TOK), 1)
    starts = [offsets[e, 4 * y + k] * 64 for k in range(4)]
    start = jnp.where(
        qi < 128,
        jnp.where(qi < 64, starts[0], starts[1]),
        jnp.where(qi < 192, starts[2], starts[3]),
    )
    for j in range(4):
        key = ki + lax.rem(y + j, 4) * ROW_TOK
        ok = (key >= start) & (key <= qi + y * ROW_TOK)
        mask[:, j * ROW_TOK : (j + 1) * ROW_TOK] = jnp.where(ok, 0.0, NEG)

    for h in range(4):
        left = (x == 1) if h == 2 else ((x == 1) | (x == 3))
        pick = jnp.where(left, 1, 0) if h < 3 else 0
        qh = q[:, h * HEAD : (h + 1) * HEAD]
        parts = []
        vals = []
        for j, (pa, pb) in enumerate(((a0, b0), (a1, b1), (a2, b2), (a3, b3))):
            kv = jnp.where(pick == 1, pb[...], pa[...]) if h < 3 else pa[...]
            s = lax.dot_general(
                qh, kv[:, :HEAD], (((1,), (1,)), ((), ())), preferred_element_type=jnp.float32
            )
            parts.append(s * (HEAD**-0.5) + mask[:, j * ROW_TOK : (j + 1) * ROW_TOK])
            vals.append(kv[:, HEAD:])
        top = functools.reduce(jnp.maximum, [jnp.max(s, axis=1, keepdims=True) for s in parts])
        mass = jnp.zeros((ROW_TOK, 1), jnp.float32)
        acc = jnp.zeros((ROW_TOK, HEAD), jnp.float32)
        for s, v in zip(parts, vals):
            p = jnp.exp(s - top)
            mass += jnp.sum(p, axis=1, keepdims=True)
            acc += jnp.dot(p.astype(jnp.bfloat16), v, preferred_element_type=jnp.float32)
        full[:, h * HEAD : (h + 1) * HEAD] = (acc / mass).astype(jnp.bfloat16)
    for j, o in enumerate((o0, o1, o2, o3)):
        o[...] = full[pl.ds(pl.multiple_of(lax.rem(x + j, 4) * 64, 64), 64), :]


def cache_rows(a0, a2, a1, a3, after1, after2, after3, t0, t1, t2, t3):
    x = lax.axis_index("x")
    y = lax.axis_index("y")
    i = lax.broadcasted_iota(jnp.int32, (64, ROW_TOK), 0)
    t = lax.broadcasted_iota(jnp.int32, (64, ROW_TOK), 1)
    want = 16 * lax.rem(i, 16) + 4 * y + lax.rem(x + lax.div(i, 16), 4)
    select = jnp.where(t == want, 1.0, 0.0).astype(jnp.bfloat16)
    for j, a in zip(HOPS, (a0, a2, a1, a3)):
        got = jnp.dot(select, a[...], preferred_element_type=jnp.float32).astype(jnp.bfloat16)
        rows = pl.ds(pl.multiple_of(lax.rem(y + j, 4) * 16, 16), 16)
        for k, out in enumerate((t0, t1, t2, t3)):
            out[rows, :] = got[16 * k : 16 * k + 16]


def cache_heads(t0, t2, t1, t3, out, buf):
    x = lax.axis_index("x")
    for j, t in zip(HOPS, (t0, t2, t1, t3)):
        buf[lax.rem(x + 4 - j, 4)] = t[...]
    for k, src in enumerate((0, 1, 3)):
        out[:, k * HEAD : (k + 1) * HEAD] = buf[src, :, :HEAD]
        out[:, (3 + k) * HEAD : (4 + k) * HEAD] = buf[src, :, HEAD:]


def cache_join(c0, c2, c1, c3, after, out):
    for n, c in zip(HOPS, (c0, c2, c1, c3)):
        out[n] = c[...]


def finish(plan, own, other, r0, r2, r1, r3, attended, cache):
    x = lax.axis_index("x")
    for j, r in zip(HOPS, (r0, r2, r1, r3)):
        low = pl.multiple_of(lax.rem(x + 4 - j, 4) * 512, 512)
        attended[:, pl.ds(low, 512)] = r[...]
    z = lax.axis_index("z")
    core = lax.axis_index("core")
    group = 2 * z + core
    for ref, t in ((own, core), (other, 1 - core)):
        for j in range(4):
            e = 2 * lax.rem(z + j, 4) + t
            rows = pl.ds(pl.multiple_of(e * 64, 64), 64)
            v = ref[j]
            cache[0, 0, rows, :] = jnp.where(plan[e, 0] == group, v, jnp.zeros_like(v))


def per_device(tokens, gain, q_weight, key_value_weight, q_bias, kv_bias, plan, home_offsets):
    bf = jnp.bfloat16
    f32 = jnp.float32
    blocks = call(
        cut,
        [((28, COLS), bf)] * 4,
        (q_weight, key_value_weight),
        [ANY] * 2,
        [
            pltpu.VMEM((28, 2048), bf),
            pltpu.VMEM((28, 768), bf),
            pltpu.SemaphoreType.DMA((2,)),
        ],
        grant=60,
    )
    (kept,) = call(keep, [((28, COLS), bf)], (blocks[0],), [ANY], [pltpu.SemaphoreType.DMA])
    got = [kept] + spread(lambda j: send(blocks[j], along_x(j)))
    (w0,) = call(place, [((112, COLS), bf)], got, scratch=[pltpu.VMEM((4, 28, COLS), f32)])
    (n0,) = call(norm, [((64, 3584), bf)], (tokens, gain, w0), [VM, VM, ANY])
    (s0,) = call(
        stage,
        [((4, 112, COLS), bf)],
        (w0, *spread(lambda j: send(w0, along_first(-j))), n0),
        [VM] * 4 + [ANY],
    )
    n1 = send(n0, along_x(-1))
    n3 = send(n0, along_x(1))
    s2, s1, s3 = spread(lambda j: send(s0, along_second(-j)))
    own1, low, high = call(
        relay, [((12, 112, COLS), bf)] + [((32, 3584), bf)] * 2, (n1, n3, s0, s1, s3)
    )
    n2a = send(low, along_x(-1))
    n2b = send(high, along_x(1))
    other1 = send(own1, other_core)
    (own2,) = call(
        hand_on, [((4, 112, COLS), bf)], (n2a, n2b, s2), [ANY] * 2 + [VM]
    )
    other2 = send(own2, other_core)
    w, x_all, cs, qb, kvb = call(
        gather,
        [
            ((32, 112, COLS), bf),
            ((ROW_TOK, 3584), bf),
            ((ROW_TOK, HEAD), f32),
            ((512,), f32),
            ((2, HEAD), f32),
        ],
        (
            home_offsets, own1, own2, other1, n0, n1, n2a, n2b, n3,
            jnp.asarray(rotary_table()), q_bias, kv_bias,
        ),
        [SM] + [VM] * 8 + [ANY] * 3,
        [pltpu.SemaphoreType.DMA((7,))],
    )
    w, kv = call(
        kv_project,
        [((32, 112, COLS), bf), ((ROW_TOK, 256), bf)],
        (w, other2, x_all, cs, kvb),
        input_output_aliases={0: 0},
    )
    (q,) = call(q_project, [((ROW_TOK, 512), bf)], (w, x_all, cs, qb))

    a2, a1, a3 = spread(lambda j: send(kv, along_y(-j)))
    a = [kv, a1, a2, a3]
    b = [send(v, pair_x) for v in a]
    rows = call(cache_rows, [((64, 256), bf)] * 4, (kv, a2, a1, a3, q, b[0], b[1]), [VM] * 4 + [ANY] * 3)
    (mine,) = call(
        cache_heads,
        [((64, 768), bf)],
        (rows[0], *spread(lambda j: send(rows[j], along_x(j)))),
        scratch=[pltpu.VMEM((4, 64, 256), bf)],
    )
    outs = call(
        attend,
        [((64, 512), bf)] * 4,
        (home_offsets, q, *a, *b, mine),
        [SM] + [VM] * 9 + [ANY],
        [pltpu.VMEM((ROW_TOK, 1024), f32), pltpu.VMEM((ROW_TOK, 512), bf)],
    )
    (cached,) = call(
        cache_join,
        [((4, 64, 768), bf)],
        (mine, *spread(lambda j: send(mine, along_z(-j))), outs[0]),
        [VM] * 4 + [ANY],
    )
    attended, cache = call(
        finish,
        [((64, 2048), bf), ((1, 1, 512, 768), bf)],
        (
            plan,
            cached,
            send(cached, other_core),
            outs[0],
            *spread(lambda j: send(outs[j], along_x(j))),
        ),
        [SM] + [VM] * 6,
    )
    return attended, cache


def solution(mesh):
    fine = Mesh(mesh.devices.reshape(SIZES), EVERY)
    in_specs = (P(EVERY, None), P(), P(EVERY, None), P(EVERY, None), P(), P(), P(), P())
    out_specs = (P(EVERY, None), P(("z", "core"), ("y", "x"), None, None))
    return jax.shard_map(
        per_device, mesh=fine, in_specs=in_specs, out_specs=out_specs, check_vma=False
    )
```

```python
import functools

import jax
import jax.numpy as jnp
import numpy as np
from jax import lax
from jax.experimental import pallas as pl
from jax.experimental.pallas import tpu as pltpu
from jax.sharding import Mesh
from jax.sharding import PartitionSpec as P

HEAD = 128
NEG = -1e30
ROW_TOK = 256
COLS = 768

EVERY = ("z", "core", "y", "x")
SIZES = (4, 2, 4, 4)
VM = pl.BlockSpec(memory_space=pltpu.VMEM)
SM = pl.BlockSpec(memory_space=pltpu.SMEM)
ANY = pl.BlockSpec(memory_space=pl.ANY)


def rotary_table():
    angles = np.arange(1024)[:, None] * 1000000.0 ** (-np.arange(64) * 2.0 / HEAD)[None, :]
    return np.concatenate([np.cos(angles), np.sin(angles)], axis=1).astype(np.float32)


def flat(z, c, y, x):
    return ((z % 4 * 2 + c % 2) * 4 + y % 4) * 4 + x % 4


PLACES = [(z, c, y, x) for z in range(4) for c in range(2) for y in range(4) for x in range(4)]


def send(v, move):
    return lax.ppermute(v, EVERY, [(flat(*p), flat(*move(*p))) for p in PLACES])


def spread(one):
    return [one(j) for j in (2, 1, 3)]


HOPS = (0, 2, 1, 3)


def along_x(j):
    return lambda z, c, y, x: (z, c, y, x + j)


def along_z(j):
    return lambda z, c, y, x: (z + j, c, y, x)


def along_first(j):
    return lambda z, c, y, x: (z + j, c, y, x) if c == 0 else (z, c, y + j, x)


def along_second(j):
    return lambda z, c, y, x: (z, c, y + j, x) if c == 0 else (z + j, c, y, x)


def other_core(z, c, y, x):
    return (z, 1 - c, y, x)


def along_y(j):
    return lambda z, c, y, x: (z, c, y + j, x)


def pair_x(z, c, y, x):
    return (z, c, y, x ^ 1)


def call(kernel, outs, operands, in_specs=None, scratch=(), grant=20, **more):
    outs = tuple(jax.ShapeDtypeStruct(s, d) for s, d in outs)
    return pl.pallas_call(
        kernel,
        out_shape=outs,
        in_specs=[VM] * len(operands) if in_specs is None else in_specs,
        out_specs=(VM,) * len(outs),
        scratch_shapes=list(scratch),
        compiler_params=pltpu.CompilerParams(vmem_limit_bytes=grant * 1024 * 1024),
        name=kernel.__name__,
        **more,
    )(*operands)


def cut(wq, wkv, b0, b1, b2, b3, q_buf, kv_buf, sem):
    copies = [
        pltpu.make_async_copy(wq, q_buf, sem.at[0]),
        pltpu.make_async_copy(wkv, kv_buf, sem.at[1]),
    ]
    for copy in copies:
        copy.start()
    for copy in copies:
        copy.wait()
    x = lax.axis_index("x")
    for j, block in enumerate((b0, b1, b2, b3)):
        to = lax.rem(x + j, 4)
        slot = lax.div(to + 1, 2)
        for n in range(2):
            low = pl.multiple_of((slot + 3 * n) * HEAD, HEAD)
            block[:, n * HEAD : (n + 1) * HEAD] = kv_buf[:, pl.ds(low, HEAD)]
        block[:, 256:] = q_buf[:, pl.ds(pl.multiple_of(to * 512, 512), 512)]


def norm(tokens, gain, after, out):
    floats = tokens[...].astype(jnp.float32)
    mean = jnp.mean(floats * floats, axis=1, keepdims=True)
    out[...] = (floats * lax.rsqrt(mean + 1e-06) * gain[...][None, :]).astype(jnp.bfloat16)


def keep(v, out, sem):
    copy = pltpu.make_async_copy(v, out, sem)
    copy.start()
    copy.wait()


def place(p0, p2, p1, p3, out, buf):
    x = lax.axis_index("x")
    for j, p in zip(HOPS, (p0, p2, p1, p3)):
        buf[lax.rem(x + 4 - j, 4)] = p[...].astype(jnp.float32)
    out[...] = jnp.concatenate([buf[k] for k in range(4)], axis=0).astype(jnp.bfloat16)


def stage(s0, s2, s1, s3, after, block):
    for i, s in enumerate((s0, s1, s2, s3)):
        block[i] = s[...]


def relay(n1, n3, s0, s1, s3, joined, r1, r3, low, high):
    for n, s in enumerate((s0, s1, s3)):
        joined[4 * n : 4 * n + 4] = s[...]
    r1[...] = s1[:2]
    r3[...] = s3[2:]
    low[...] = n1[:32, :]
    high[...] = n3[32:, :]


def join2(after1, after2, a, b, out):
    out[:2] = a[...]
    out[2:] = b[...]


def load_weights(ref, t, places, buf):
    y = lax.axis_index("y")
    z = lax.axis_index("z")
    for n, (j, i) in enumerate(places):
        zz = lax.rem(z + jnp.where(t == 0, i, j), 4)
        yy = lax.rem(y + jnp.where(t == 0, j, i), 4)
        buf[(2 * zz + t) * 4 + yy] = ref[n]


FIRST = [(j, i) for j in (0, 1, 3) for i in range(4)]
LAST = [(2, i) for i in range(4)]


def gather(
    offsets, own1, own2, other1, n0, n1, n2a, n2b, n3, table, qb, kvb, w, x_out, cs, qb_out, kvb_out, sem
):
    e = 2 * lax.axis_index("z") + lax.axis_index("core")
    y = lax.axis_index("y")
    x = lax.axis_index("x")
    core = lax.axis_index("core")
    copies = []
    for k in range(4):
        s = 4 * y + k
        row = pl.multiple_of((s - offsets[e, s]) * 64, 64)
        copies.append(
            pltpu.make_async_copy(
                table.at[pl.ds(row, 64), :], cs.at[k * 64 : (k + 1) * 64, :], sem.at[k]
            )
        )
    copies.append(
        pltpu.make_async_copy(qb.at[pl.ds(pl.multiple_of(x * 512, 512), 512)], qb_out, sem.at[4])
    )
    slot = lax.div(x + 1, 2)
    for n in range(2):
        low = pl.multiple_of((slot + 3 * n) * HEAD, HEAD)
        copies.append(
            pltpu.make_async_copy(kvb.at[pl.ds(low, HEAD)], kvb_out.at[n], sem.at[5 + n])
        )
    for copy in copies:
        copy.start()
    for ref, j, low, size in (
        (n0, 0, 0, 64),
        (n1, 1, 0, 64),
        (n2a, 2, 0, 32),
        (n2b, 2, 32, 32),
        (n3, 3, 0, 64),
    ):
        row = pl.multiple_of(lax.rem(x + j, 4) * 64 + low, 32)
        x_out[pl.ds(row, size), :] = ref[...]
    load_weights(own1, core, FIRST, w)
    load_weights(own2, core, LAST, w)
    load_weights(other1, 1 - core, FIRST, w)
    for copy in copies:
        copy.wait()


def rotate(v, cos, sin):
    a = v[:, :64]
    b = v[:, 64:]
    return jnp.concatenate([a * cos - b * sin, b * cos + a * sin], axis=1).astype(jnp.bfloat16)


def kv_project(w_in, other2, x_in, cs, kvb, w, kv):
    del w_in
    load_weights(other2, 1 - lax.axis_index("core"), LAST, w)
    acc = jnp.dot(
        x_in[...], w[:, :, :256].reshape(3584, 256), preferred_element_type=jnp.float32
    )
    kv[:, :HEAD] = rotate(acc[:, :HEAD] + kvb[0][None, :], cs[:, :64], cs[:, 64:])
    kv[:, HEAD:] = (acc[:, HEAD:] + kvb[1][None, :]).astype(jnp.bfloat16)


def q_project(w, x_in, cs, qb, q):
    for g in range(2):
        part = slice((g + 1) * 256, (g + 2) * 256)
        acc = jnp.dot(
            x_in[...], w[:, :, part].reshape(3584, 256), preferred_element_type=jnp.float32
        )
        for h in range(2):
            low = (2 * g + h) * HEAD
            head = acc[:, h * HEAD : (h + 1) * HEAD] + qb[low : low + HEAD][None, :]
            q[:, low : low + HEAD] = rotate(head, cs[:, :64], cs[:, 64:])


def one_head(qh, blocks, mask):
    parts = []
    for j, kv in enumerate(blocks):
        s = lax.dot_general(
            qh, kv[:, :HEAD], (((1,), (1,)), ((), ())), preferred_element_type=jnp.float32
        )
        parts.append(s * (HEAD**-0.5) + mask[:, j * ROW_TOK : (j + 1) * ROW_TOK])
    top = functools.reduce(jnp.maximum, [jnp.max(s, axis=1, keepdims=True) for s in parts])
    mass = jnp.zeros((ROW_TOK, 1), jnp.float32)
    acc = jnp.zeros((ROW_TOK, HEAD), jnp.float32)
    for s, kv in zip(parts, blocks):
        p = jnp.exp(s - top)
        mass += jnp.sum(p, axis=1, keepdims=True)
        acc += jnp.dot(p.astype(jnp.bfloat16), kv[:, HEAD:], preferred_element_type=jnp.float32)
    return (acc / mass).astype(jnp.bfloat16)


def attend_own(offsets, q, a0, a1, a2, a3, after, mask, last):
    y = lax.axis_index("y")
    e = 2 * lax.axis_index("z") + lax.axis_index("core")
    qi = lax.broadcasted_iota(jnp.int32, (ROW_TOK, ROW_TOK), 0)
    ki = lax.broadcasted_iota(jnp.int32, (ROW_TOK, ROW_TOK), 1)
    starts = [offsets[e, 4 * y + k] * 64 for k in range(4)]
    start = jnp.where(
        qi < 128,
        jnp.where(qi < 64, starts[0], starts[1]),
        jnp.where(qi < 192, starts[2], starts[3]),
    )
    for j in range(4):
        key = ki + lax.rem(y + j, 4) * ROW_TOK
        ok = (key >= start) & (key <= qi + y * ROW_TOK)
        mask[:, j * ROW_TOK : (j + 1) * ROW_TOK] = jnp.where(ok, 0.0, NEG)
    last[...] = one_head(q[:, 3 * HEAD :], [a[...] for a in (a0, a1, a2, a3)], mask)


def attend(mask, last, q, a0, a1, a2, a3, b0, b1, b2, b3, o0, o1, o2, o3, full):
    x = lax.axis_index("x")
    for h in range(3):
        left = (x == 1) if h == 2 else ((x == 1) | (x == 3))
        pick = jnp.where(left, 1, 0)
        blocks = [
            jnp.where(pick == 1, b[...], a[...])
            for a, b in ((a0, b0), (a1, b1), (a2, b2), (a3, b3))
        ]
        part = slice(h * HEAD, (h + 1) * HEAD)
        full[:, part] = one_head(q[:, part], blocks, mask)
    full[:, 3 * HEAD :] = last[...]
    for j, o in enumerate((o0, o1, o2, o3)):
        o[...] = full[pl.ds(pl.multiple_of(lax.rem(x + j, 4) * 64, 64), 64), :]


def cache_rows(a0, a2, a1, a3, after1, after2, t0, t1, t2, t3):
    x = lax.axis_index("x")
    y = lax.axis_index("y")
    i = lax.broadcasted_iota(jnp.int32, (64, ROW_TOK), 0)
    t = lax.broadcasted_iota(jnp.int32, (64, ROW_TOK), 1)
    want = 16 * lax.rem(i, 16) + 4 * y + lax.rem(x + lax.div(i, 16), 4)
    select = jnp.where(t == want, 1.0, 0.0).astype(jnp.bfloat16)
    for j, a in zip(HOPS, (a0, a2, a1, a3)):
        got = jnp.dot(select, a[...], preferred_element_type=jnp.float32).astype(jnp.bfloat16)
        rows = pl.ds(pl.multiple_of(lax.rem(y + j, 4) * 16, 16), 16)
        for k, out in enumerate((t0, t1, t2, t3)):
            out[rows, :] = got[16 * k : 16 * k + 16]


def cache_heads(t0, t2, t1, t3, out, buf):
    x = lax.axis_index("x")
    for j, t in zip(HOPS, (t0, t2, t1, t3)):
        buf[lax.rem(x + 4 - j, 4)] = t[...]
    for k, src in enumerate((0, 1, 3)):
        out[:, k * HEAD : (k + 1) * HEAD] = buf[src, :, :HEAD]
        out[:, (3 + k) * HEAD : (4 + k) * HEAD] = buf[src, :, HEAD:]


def cache_join(c0, c2, c1, c3, after, out):
    for n, c in zip(HOPS, (c0, c2, c1, c3)):
        out[n] = c[...]


def finish(plan, own, other, r0, r2, r1, r3, attended, cache):
    x = lax.axis_index("x")
    for j, r in zip(HOPS, (r0, r2, r1, r3)):
        low = pl.multiple_of(lax.rem(x + 4 - j, 4) * 512, 512)
        attended[:, pl.ds(low, 512)] = r[...]
    z = lax.axis_index("z")
    core = lax.axis_index("core")
    group = 2 * z + core
    for ref, t in ((own, core), (other, 1 - core)):
        for j in range(4):
            e = 2 * lax.rem(z + j, 4) + t
            rows = pl.ds(pl.multiple_of(e * 64, 64), 64)
            v = ref[j]
            cache[0, 0, rows, :] = jnp.where(plan[e, 0] == group, v, jnp.zeros_like(v))


def per_device(tokens, gain, q_weight, key_value_weight, q_bias, kv_bias, plan, home_offsets):
    bf = jnp.bfloat16
    f32 = jnp.float32
    blocks = call(
        cut,
        [((28, COLS), bf)] * 4,
        (q_weight, key_value_weight),
        [ANY] * 2,
        [
            pltpu.VMEM((28, 2048), bf),
            pltpu.VMEM((28, 768), bf),
            pltpu.SemaphoreType.DMA((2,)),
        ],
        grant=60,
    )
    (kept,) = call(keep, [((28, COLS), bf)], (blocks[0],), [ANY], [pltpu.SemaphoreType.DMA])
    got = [kept] + spread(lambda j: send(blocks[j], along_x(j)))
    (w0,) = call(place, [((112, COLS), bf)], got, scratch=[pltpu.VMEM((4, 28, COLS), f32)])
    (n0,) = call(norm, [((64, 3584), bf)], (tokens, gain, w0), [VM, VM, ANY])
    (s0,) = call(
        stage,
        [((4, 112, COLS), bf)],
        (w0, *spread(lambda j: send(w0, along_first(-j))), n0),
        [VM] * 4 + [ANY],
    )
    n1 = send(n0, along_x(-1))
    n3 = send(n0, along_x(1))
    s1 = send(s0, along_second(-1))
    s3 = send(s0, along_second(1))
    own1, r1, r3, low, high = call(
        relay,
        [((12, 112, COLS), bf)] + [((2, 112, COLS), bf)] * 2 + [((32, 3584), bf)] * 2,
        (n1, n3, s0, s1, s3),
    )
    n2a = send(low, along_x(-1))
    n2b = send(high, along_x(1))
    s2a = send(r1, along_second(-1))
    s2b = send(r3, along_second(1))
    other1 = send(own1, other_core)
    (own2,) = call(
        join2, [((4, 112, COLS), bf)], (n2a, n2b, s2a, s2b), [ANY] * 2 + [VM] * 2
    )
    other2 = send(own2, other_core)
    w, x_all, cs, qb, kvb = call(
        gather,
        [
            ((32, 112, COLS), bf),
            ((ROW_TOK, 3584), bf),
            ((ROW_TOK, HEAD), f32),
            ((512,), f32),
            ((2, HEAD), f32),
        ],
        (
            home_offsets, own1, own2, other1, n0, n1, n2a, n2b, n3,
            jnp.asarray(rotary_table()), q_bias, kv_bias,
        ),
        [SM] + [VM] * 8 + [ANY] * 3,
        [pltpu.SemaphoreType.DMA((7,))],
    )
    w, kv = call(
        kv_project,
        [((32, 112, COLS), bf), ((ROW_TOK, 256), bf)],
        (w, other2, x_all, cs, kvb),
        input_output_aliases={0: 0},
    )
    (q,) = call(q_project, [((ROW_TOK, 512), bf)], (w, x_all, cs, qb))

    a2, a1, a3 = spread(lambda j: send(kv, along_y(-j)))
    a = [kv, a1, a2, a3]
    b = [send(v, pair_x) for v in a]
    rows = call(cache_rows, [((64, 256), bf)] * 4, (kv, a2, a1, a3, q, b[0]), [VM] * 4 + [ANY] * 2)
    (mine,) = call(
        cache_heads,
        [((64, 768), bf)],
        (rows[0], *spread(lambda j: send(rows[j], along_x(j)))),
        scratch=[pltpu.VMEM((4, 64, 256), bf)],
    )
    mask, last = call(
        attend_own,
        [((ROW_TOK, 1024), f32), ((ROW_TOK, HEAD), bf)],
        (home_offsets, q, *a, mine),
        [SM] + [VM] * 5 + [ANY],
    )
    outs = call(
        attend,
        [((64, 512), bf)] * 4,
        (mask, last, q, *a, *b),
        scratch=[pltpu.VMEM((ROW_TOK, 512), bf)],
    )
    (cached,) = call(
        cache_join,
        [((4, 64, 768), bf)],
        (mine, *spread(lambda j: send(mine, along_z(-j))), outs[0]),
        [VM] * 4 + [ANY],
    )
    attended, cache = call(
        finish,
        [((64, 2048), bf), ((1, 1, 512, 768), bf)],
        (
            plan,
            cached,
            send(cached, other_core),
            outs[0],
            *spread(lambda j: send(outs[j], along_x(j))),
        ),
        [SM] + [VM] * 6,
    )
    return attended, cache


def solution(mesh):
    fine = Mesh(mesh.devices.reshape(SIZES), EVERY)
    in_specs = (P(EVERY, None), P(), P(EVERY, None), P(EVERY, None), P(), P(), P(), P())
    out_specs = (P(EVERY, None), P(("z", "core"), ("y", "x"), None, None))
    return jax.shard_map(
        per_device, mesh=fine, in_specs=in_specs, out_specs=out_specs, check_vma=False
    )
```

```python
import functools

import jax
import jax.numpy as jnp
import numpy as np
from jax import lax
from jax.experimental import pallas as pl
from jax.experimental.pallas import tpu as pltpu
from jax.sharding import Mesh
from jax.sharding import PartitionSpec as P

HEAD = 128
NEG = -1e30
ROW_TOK = 256
COLS = 768

EVERY = ("z", "core", "y", "x")
SIZES = (4, 2, 4, 4)
VM = pl.BlockSpec(memory_space=pltpu.VMEM)
SM = pl.BlockSpec(memory_space=pltpu.SMEM)
ANY = pl.BlockSpec(memory_space=pl.ANY)


def rotary_table():
    angles = np.arange(1024)[:, None] * 1000000.0 ** (-np.arange(64) * 2.0 / HEAD)[None, :]
    return np.concatenate([np.cos(angles), np.sin(angles)], axis=1).astype(np.float32)


def flat(z, c, y, x):
    return ((z % 4 * 2 + c % 2) * 4 + y % 4) * 4 + x % 4


PLACES = [(z, c, y, x) for z in range(4) for c in range(2) for y in range(4) for x in range(4)]


def send(v, move):
    return lax.ppermute(v, EVERY, [(flat(*p), flat(*move(*p))) for p in PLACES])


def spread(one):
    return [one(j) for j in (2, 1, 3)]


def spread_down(one):
    return [one(j) for j in (2, 3, 1)]


HOPS = (0, 2, 1, 3)
DOWN = (0, 2, 3, 1)


def along_x(j):
    return lambda z, c, y, x: (z, c, y, x + j)


def along_z(j):
    return lambda z, c, y, x: (z + j, c, y, x)


def along_first(j):
    return lambda z, c, y, x: (z + j, c, y, x) if c == 0 else (z, c, y + j, x)


def along_second(j):
    return lambda z, c, y, x: (z, c, y + j, x) if c == 0 else (z + j, c, y, x)


def other_core(z, c, y, x):
    return (z, 1 - c, y, x)


def along_y(j):
    return lambda z, c, y, x: (z, c, y + j, x)


def pair_x(z, c, y, x):
    return (z, c, y, x ^ 1)


def call(kernel, outs, operands, in_specs=None, scratch=(), grant=20, **more):
    outs = tuple(jax.ShapeDtypeStruct(s, d) for s, d in outs)
    return pl.pallas_call(
        kernel,
        out_shape=outs,
        in_specs=[VM] * len(operands) if in_specs is None else in_specs,
        out_specs=(VM,) * len(outs),
        scratch_shapes=list(scratch),
        compiler_params=pltpu.CompilerParams(vmem_limit_bytes=grant * 1024 * 1024),
        name=kernel.__name__,
        **more,
    )(*operands)


def cut(wq, wkv, b0, b1, b2, b3, q_buf, kv_buf, sem):
    copies = [
        pltpu.make_async_copy(wq, q_buf, sem.at[0]),
        pltpu.make_async_copy(wkv, kv_buf, sem.at[1]),
    ]
    for copy in copies:
        copy.start()
    for copy in copies:
        copy.wait()
    x = lax.axis_index("x")
    for j, block in enumerate((b0, b1, b2, b3)):
        to = lax.rem(x + j, 4)
        slot = lax.div(to + 1, 2)
        for n in range(2):
            low = pl.multiple_of((slot + 3 * n) * HEAD, HEAD)
            block[:, n * HEAD : (n + 1) * HEAD] = kv_buf[:, pl.ds(low, HEAD)]
        block[:, 256:] = q_buf[:, pl.ds(pl.multiple_of(to * 512, 512), 512)]


def norm(tokens, gain, after, out):
    floats = tokens[...].astype(jnp.float32)
    mean = jnp.mean(floats * floats, axis=1, keepdims=True)
    out[...] = (floats * lax.rsqrt(mean + 1e-06) * gain[...][None, :]).astype(jnp.bfloat16)


def keep(v, out, sem):
    copy = pltpu.make_async_copy(v, out, sem)
    copy.start()
    copy.wait()


def place(p0, p2, p1, p3, out, buf):
    x = lax.axis_index("x")
    for j, p in zip(HOPS, (p0, p2, p1, p3)):
        buf[lax.rem(x + 4 - j, 4)] = p[...].astype(jnp.float32)
    out[...] = jnp.concatenate([buf[k] for k in range(4)], axis=0).astype(jnp.bfloat16)


def stage(s0, s2, s3, s1, after, block):
    for i, s in enumerate((s0, s1, s2, s3)):
        block[i] = s[...]


def relay(n1, n3, s0, s1, s3, joined, r1, r3, low, high):
    for n, s in enumerate((s0, s1, s3)):
        joined[4 * n : 4 * n + 4] = s[...]
    r1[...] = s1[:2]
    r3[...] = s3[2:]
    low[...] = n1[:32, :]
    high[...] = n3[32:, :]


def join2(after1, after2, a, b, out):
    out[:2] = a[...]
    out[2:] = b[...]


def load_weights(ref, t, places, buf):
    y = lax.axis_index("y")
    z = lax.axis_index("z")
    for n, (j, i) in enumerate(places):
        zz = lax.rem(z + jnp.where(t == 0, i, j), 4)
        yy = lax.rem(y + jnp.where(t == 0, j, i), 4)
        buf[(2 * zz + t) * 4 + yy] = ref[n]


FIRST = [(j, i) for j in (0, 1, 3) for i in range(4)]
LAST = [(2, i) for i in range(4)]


def gather(
    offsets, own1, own2, other1, n0, n1, n2a, n2b, n3, table, qb, kvb, w, x_out, cs, qb_out, kvb_out, sem
):
    e = 2 * lax.axis_index("z") + lax.axis_index("core")
    y = lax.axis_index("y")
    x = lax.axis_index("x")
    core = lax.axis_index("core")
    copies = []
    for k in range(4):
        s = 4 * y + k
        row = pl.multiple_of((s - offsets[e, s]) * 64, 64)
        copies.append(
            pltpu.make_async_copy(
                table.at[pl.ds(row, 64), :], cs.at[k * 64 : (k + 1) * 64, :], sem.at[k]
            )
        )
    copies.append(
        pltpu.make_async_copy(qb.at[pl.ds(pl.multiple_of(x * 512, 512), 512)], qb_out, sem.at[4])
    )
    slot = lax.div(x + 1, 2)
    for n in range(2):
        low = pl.multiple_of((slot + 3 * n) * HEAD, HEAD)
        copies.append(
            pltpu.make_async_copy(kvb.at[pl.ds(low, HEAD)], kvb_out.at[n], sem.at[5 + n])
        )
    for copy in copies:
        copy.start()
    for ref, j, low, size in (
        (n0, 0, 0, 64),
        (n1, 1, 0, 64),
        (n2a, 2, 0, 32),
        (n2b, 2, 32, 32),
        (n3, 3, 0, 64),
    ):
        row = pl.multiple_of(lax.rem(x + j, 4) * 64 + low, 32)
        x_out[pl.ds(row, size), :] = ref[...]
    load_weights(own1, core, FIRST, w)
    load_weights(own2, core, LAST, w)
    load_weights(other1, 1 - core, FIRST, w)
    for copy in copies:
        copy.wait()


def rotate(v, cos, sin):
    a = v[:, :64]
    b = v[:, 64:]
    return jnp.concatenate([a * cos - b * sin, b * cos + a * sin], axis=1).astype(jnp.bfloat16)


def kv_project(w_in, other2, x_in, cs, kvb, w, kv):
    del w_in
    load_weights(other2, 1 - lax.axis_index("core"), LAST, w)
    acc = jnp.dot(
        x_in[...], w[:, :, :256].reshape(3584, 256), preferred_element_type=jnp.float32
    )
    kv[:, :HEAD] = rotate(acc[:, :HEAD] + kvb[0][None, :], cs[:, :64], cs[:, 64:])
    kv[:, HEAD:] = (acc[:, HEAD:] + kvb[1][None, :]).astype(jnp.bfloat16)


def q_project(w, x_in, cs, qb, q):
    for g in range(2):
        part = slice((g + 1) * 256, (g + 2) * 256)
        acc = jnp.dot(
            x_in[...], w[:, :, part].reshape(3584, 256), preferred_element_type=jnp.float32
        )
        for h in range(2):
            low = (2 * g + h) * HEAD
            head = acc[:, h * HEAD : (h + 1) * HEAD] + qb[low : low + HEAD][None, :]
            q[:, low : low + HEAD] = rotate(head, cs[:, :64], cs[:, 64:])


def one_head(qh, blocks, mask):
    parts = []
    for j, kv in enumerate(blocks):
        s = lax.dot_general(
            qh, kv[:, :HEAD], (((1,), (1,)), ((), ())), preferred_element_type=jnp.float32
        )
        parts.append(s * (HEAD**-0.5) + mask[:, j * ROW_TOK : (j + 1) * ROW_TOK])
    top = functools.reduce(jnp.maximum, [jnp.max(s, axis=1, keepdims=True) for s in parts])
    mass = jnp.zeros((ROW_TOK, 1), jnp.float32)
    acc = jnp.zeros((ROW_TOK, HEAD), jnp.float32)
    for s, kv in zip(parts, blocks):
        p = jnp.exp(s - top)
        mass += jnp.sum(p, axis=1, keepdims=True)
        acc += jnp.dot(p.astype(jnp.bfloat16), kv[:, HEAD:], preferred_element_type=jnp.float32)
    return (acc / mass).astype(jnp.bfloat16)


def attend_own(offsets, q, a0, a1, a2, a3, after, mask, last):
    y = lax.axis_index("y")
    e = 2 * lax.axis_index("z") + lax.axis_index("core")
    qi = lax.broadcasted_iota(jnp.int32, (ROW_TOK, ROW_TOK), 0)
    ki = lax.broadcasted_iota(jnp.int32, (ROW_TOK, ROW_TOK), 1)
    starts = [offsets[e, 4 * y + k] * 64 for k in range(4)]
    start = jnp.where(
        qi < 128,
        jnp.where(qi < 64, starts[0], starts[1]),
        jnp.where(qi < 192, starts[2], starts[3]),
    )
    for j in range(4):
        key = ki + lax.rem(y + j, 4) * ROW_TOK
        ok = (key >= start) & (key <= qi + y * ROW_TOK)
        mask[:, j * ROW_TOK : (j + 1) * ROW_TOK] = jnp.where(ok, 0.0, NEG)
    last[...] = one_head(q[:, 3 * HEAD :], [a[...] for a in (a0, a1, a2, a3)], mask)


def attend(mask, last, q, a0, a1, a2, a3, b0, b3, b2, b1, o0, o1, o2, o3, full):
    x = lax.axis_index("x")
    for h in range(3):
        left = (x == 1) if h == 2 else ((x == 1) | (x == 3))
        pick = jnp.where(left, 1, 0)
        blocks = [
            jnp.where(pick == 1, b[...], a[...])
            for a, b in ((a0, b0), (a1, b1), (a2, b2), (a3, b3))
        ]
        part = slice(h * HEAD, (h + 1) * HEAD)
        full[:, part] = one_head(q[:, part], blocks, mask)
    full[:, 3 * HEAD :] = last[...]
    for j, o in enumerate((o0, o1, o2, o3)):
        o[...] = full[pl.ds(pl.multiple_of(lax.rem(x + j, 4) * 64, 64), 64), :]


def cache_rows(a0, a2, a3, a1, after1, after2, t0, t1, t2, t3):
    x = lax.axis_index("x")
    y = lax.axis_index("y")
    i = lax.broadcasted_iota(jnp.int32, (64, ROW_TOK), 0)
    t = lax.broadcasted_iota(jnp.int32, (64, ROW_TOK), 1)
    want = 16 * lax.rem(i, 16) + 4 * y + lax.rem(x + lax.div(i, 16), 4)
    select = jnp.where(t == want, 1.0, 0.0).astype(jnp.bfloat16)
    for j, a in zip(DOWN, (a0, a2, a3, a1)):
        got = jnp.dot(select, a[...], preferred_element_type=jnp.float32).astype(jnp.bfloat16)
        rows = pl.ds(pl.multiple_of(lax.rem(y + j, 4) * 16, 16), 16)
        for k, out in enumerate((t0, t1, t2, t3)):
            out[rows, :] = got[16 * k : 16 * k + 16]


def cache_heads(t0, t2, t1, t3, out, buf):
    x = lax.axis_index("x")
    for j, t in zip(HOPS, (t0, t2, t1, t3)):
        buf[lax.rem(x + 4 - j, 4)] = t[...]
    for k, src in enumerate((0, 1, 3)):
        out[:, k * HEAD : (k + 1) * HEAD] = buf[src, :, :HEAD]
        out[:, (3 + k) * HEAD : (4 + k) * HEAD] = buf[src, :, HEAD:]


def cache_join(c0, c2, c3, c1, after, out):
    for n, c in zip(DOWN, (c0, c2, c3, c1)):
        out[n] = c[...]


def finish(plan, own, other, r0, r2, r1, r3, attended, cache):
    x = lax.axis_index("x")
    for j, r in zip(HOPS, (r0, r2, r1, r3)):
        low = pl.multiple_of(lax.rem(x + 4 - j, 4) * 512, 512)
        attended[:, pl.ds(low, 512)] = r[...]
    z = lax.axis_index("z")
    core = lax.axis_index("core")
    group = 2 * z + core
    for ref, t in ((own, core), (other, 1 - core)):
        for j in range(4):
            e = 2 * lax.rem(z + j, 4) + t
            rows = pl.ds(pl.multiple_of(e * 64, 64), 64)
            v = ref[j]
            cache[0, 0, rows, :] = jnp.where(plan[e, 0] == group, v, jnp.zeros_like(v))


def per_device(tokens, gain, q_weight, key_value_weight, q_bias, kv_bias, plan, home_offsets):
    bf = jnp.bfloat16
    f32 = jnp.float32
    blocks = call(
        cut,
        [((28, COLS), bf)] * 4,
        (q_weight, key_value_weight),
        [ANY] * 2,
        [
            pltpu.VMEM((28, 2048), bf),
            pltpu.VMEM((28, 768), bf),
            pltpu.SemaphoreType.DMA((2,)),
        ],
        grant=60,
    )
    (kept,) = call(keep, [((28, COLS), bf)], (blocks[0],), [ANY], [pltpu.SemaphoreType.DMA])
    got = [kept] + spread(lambda j: send(blocks[j], along_x(j)))
    (w0,) = call(place, [((112, COLS), bf)], got, scratch=[pltpu.VMEM((4, 28, COLS), f32)])
    (n0,) = call(norm, [((64, 3584), bf)], (tokens, gain, w0), [VM, VM, ANY])
    (s0,) = call(
        stage,
        [((4, 112, COLS), bf)],
        (w0, *spread_down(lambda j: send(w0, along_first(-j))), n0),
        [VM] * 4 + [ANY],
    )
    n1 = send(n0, along_x(-1))
    n3 = send(n0, along_x(1))
    s1 = send(s0, along_second(-1))
    s3 = send(s0, along_second(1))
    own1, r1, r3, low, high = call(
        relay,
        [((12, 112, COLS), bf)] + [((2, 112, COLS), bf)] * 2 + [((32, 3584), bf)] * 2,
        (n1, n3, s0, s1, s3),
    )
    n2a = send(low, along_x(-1))
    n2b = send(high, along_x(1))
    s2a = send(r1, along_second(-1))
    s2b = send(r3, along_second(1))
    other1 = send(own1, other_core)
    (own2,) = call(
        join2, [((4, 112, COLS), bf)], (n2a, n2b, s2a, s2b), [ANY] * 2 + [VM] * 2
    )
    other2 = send(own2, other_core)
    w, x_all, cs, qb, kvb = call(
        gather,
        [
            ((32, 112, COLS), bf),
            ((ROW_TOK, 3584), bf),
            ((ROW_TOK, HEAD), f32),
            ((512,), f32),
            ((2, HEAD), f32),
        ],
        (
            home_offsets, own1, own2, other1, n0, n1, n2a, n2b, n3,
            jnp.asarray(rotary_table()), q_bias, kv_bias,
        ),
        [SM] + [VM] * 8 + [ANY] * 3,
        [pltpu.SemaphoreType.DMA((7,))],
    )
    w, kv = call(
        kv_project,
        [((32, 112, COLS), bf), ((ROW_TOK, 256), bf)],
        (w, other2, x_all, cs, kvb),
        input_output_aliases={0: 0},
    )
    (q,) = call(q_project, [((ROW_TOK, 512), bf)], (w, x_all, cs, qb))

    a2, a3, a1 = spread_down(lambda j: send(kv, along_y(-j)))
    a = [kv, a1, a2, a3]
    b = [send(v, pair_x) for v in a]
    rows = call(cache_rows, [((64, 256), bf)] * 4, (kv, a2, a3, a1, q, b[0]), [VM] * 4 + [ANY] * 2)
    (mine,) = call(
        cache_heads,
        [((64, 768), bf)],
        (rows[0], *spread(lambda j: send(rows[j], along_x(j)))),
        scratch=[pltpu.VMEM((4, 64, 256), bf)],
    )
    mask, last = call(
        attend_own,
        [((ROW_TOK, 1024), f32), ((ROW_TOK, HEAD), bf)],
        (home_offsets, q, *a, mine),
        [SM] + [VM] * 5 + [ANY],
    )
    outs = call(
        attend,
        [((64, 512), bf)] * 4,
        (mask, last, q, *a, b[0], b[3], b[2], b[1]),
        scratch=[pltpu.VMEM((ROW_TOK, 512), bf)],
    )
    (cached,) = call(
        cache_join,
        [((4, 64, 768), bf)],
        (mine, *spread_down(lambda j: send(mine, along_z(-j))), outs[0]),
        [VM] * 4 + [ANY],
    )
    attended, cache = call(
        finish,
        [((64, 2048), bf), ((1, 1, 512, 768), bf)],
        (
            plan,
            cached,
            send(cached, other_core),
            outs[0],
            *spread(lambda j: send(outs[j], along_x(j))),
        ),
        [SM] + [VM] * 6,
    )
    return attended, cache


def solution(mesh):
    fine = Mesh(mesh.devices.reshape(SIZES), EVERY)
    in_specs = (P(EVERY, None), P(), P(EVERY, None), P(EVERY, None), P(), P(), P(), P())
    out_specs = (P(EVERY, None), P(("z", "core"), ("y", "x"), None, None))
    return jax.shard_map(
        per_device, mesh=fine, in_specs=in_specs, out_specs=out_specs, check_vma=False
    )
```

```python
import functools

import jax
import jax.numpy as jnp
import numpy as np
from jax import lax
from jax.experimental import pallas as pl
from jax.experimental.pallas import tpu as pltpu
from jax.sharding import Mesh
from jax.sharding import PartitionSpec as P

HEAD = 128
NEG = -1e30
ROW_TOK = 256
COLS = 768

EVERY = ("z", "core", "y", "x")
SIZES = (4, 2, 4, 4)
VM = pl.BlockSpec(memory_space=pltpu.VMEM)
SM = pl.BlockSpec(memory_space=pltpu.SMEM)
ANY = pl.BlockSpec(memory_space=pl.ANY)


def rotary_table():
    angles = np.arange(1024)[:, None] * 1000000.0 ** (-np.arange(64) * 2.0 / HEAD)[None, :]
    return np.concatenate([np.cos(angles), np.sin(angles)], axis=1).astype(np.float32)


def flat(z, c, y, x):
    return ((z % 4 * 2 + c % 2) * 4 + y % 4) * 4 + x % 4


PLACES = [(z, c, y, x) for z in range(4) for c in range(2) for y in range(4) for x in range(4)]


def send(v, move):
    return lax.ppermute(v, EVERY, [(flat(*p), flat(*move(*p))) for p in PLACES])


def spread(one):
    return [one(j) for j in (2, 1, 3)]


HOPS = (0, 2, 1, 3)


def along_x(j):
    return lambda z, c, y, x: (z, c, y, x + j)


def along_z(j):
    return lambda z, c, y, x: (z + j, c, y, x)


def along_first(j):
    return lambda z, c, y, x: (z + j, c, y, x) if c == 0 else (z, c, y + j, x)


def along_second(j):
    return lambda z, c, y, x: (z, c, y + j, x) if c == 0 else (z + j, c, y, x)


def other_core(z, c, y, x):
    return (z, 1 - c, y, x)


def along_y(j):
    return lambda z, c, y, x: (z, c, y + j, x)


def pair_x(z, c, y, x):
    return (z, c, y, x ^ 1)


def call(kernel, outs, operands, in_specs=None, scratch=(), grant=20, **more):
    outs = tuple(jax.ShapeDtypeStruct(s, d) for s, d in outs)
    return pl.pallas_call(
        kernel,
        out_shape=outs,
        in_specs=[VM] * len(operands) if in_specs is None else in_specs,
        out_specs=(VM,) * len(outs),
        scratch_shapes=list(scratch),
        compiler_params=pltpu.CompilerParams(vmem_limit_bytes=grant * 1024 * 1024),
        name=kernel.__name__,
        **more,
    )(*operands)


def cut(wq, wkv, b0, b1, b2, b3, q_buf, kv_buf, sem):
    copies = [
        pltpu.make_async_copy(wq, q_buf, sem.at[0]),
        pltpu.make_async_copy(wkv, kv_buf, sem.at[1]),
    ]
    for copy in copies:
        copy.start()
    for copy in copies:
        copy.wait()
    x = lax.axis_index("x")
    for j, block in enumerate((b0, b1, b2, b3)):
        to = lax.rem(x + j, 4)
        slot = lax.div(to + 1, 2)
        for n in range(2):
            low = pl.multiple_of((slot + 3 * n) * HEAD, HEAD)
            block[:, n * HEAD : (n + 1) * HEAD] = kv_buf[:, pl.ds(low, HEAD)]
        block[:, 256:] = q_buf[:, pl.ds(pl.multiple_of(to * 512, 512), 512)]


def norm(tokens, gain, after, out):
    floats = tokens[...].astype(jnp.float32)
    mean = jnp.mean(floats * floats, axis=1, keepdims=True)
    out[...] = (floats * lax.rsqrt(mean + 1e-06) * gain[...][None, :]).astype(jnp.bfloat16)


def keep(v, out, sem):
    copy = pltpu.make_async_copy(v, out, sem)
    copy.start()
    copy.wait()


def place(p0, p2, p1, p3, out, buf):
    x = lax.axis_index("x")
    for j, p in zip(HOPS, (p0, p2, p1, p3)):
        buf[lax.rem(x + 4 - j, 4)] = p[...].astype(jnp.float32)
    out[...] = jnp.concatenate([buf[k] for k in range(4)], axis=0).astype(jnp.bfloat16)


def stage(s0, s2, s1, s3, after, block):
    for i, s in enumerate((s0, s1, s2, s3)):
        block[i] = s[...]


def relay(n1, n3, s0, s1, s3, joined, r1, r3, low, high):
    for n, s in enumerate((s0, s1, s3)):
        joined[4 * n : 4 * n + 4] = s[...]
    r1[...] = s1[:2]
    r3[...] = s3[2:]
    low[...] = n1[:32, :]
    high[...] = n3[32:, :]


def join2(after1, after2, a, b, out):
    out[:2] = a[...]
    out[2:] = b[...]


def load_weights(ref, t, places, buf):
    y = lax.axis_index("y")
    z = lax.axis_index("z")
    for n, (j, i) in enumerate(places):
        zz = lax.rem(z + jnp.where(t == 0, i, j), 4)
        yy = lax.rem(y + jnp.where(t == 0, j, i), 4)
        buf[(2 * zz + t) * 4 + yy] = ref[n]


FIRST = [(j, i) for j in (0, 1, 3) for i in range(4)]
LAST = [(2, i) for i in range(4)]


def gather(
    offsets, own1, own2, other1, n0, n1, n2a, n2b, n3, table, qb, kvb, w, x_out, cs, qb_out, kvb_out, sem
):
    e = 2 * lax.axis_index("z") + lax.axis_index("core")
    y = lax.axis_index("y")
    x = lax.axis_index("x")
    core = lax.axis_index("core")
    copies = []
    for k in range(4):
        s = 4 * y + k
        row = pl.multiple_of((s - offsets[e, s]) * 64, 64)
        copies.append(
            pltpu.make_async_copy(
                table.at[pl.ds(row, 64), :], cs.at[k * 64 : (k + 1) * 64, :], sem.at[k]
            )
        )
    copies.append(
        pltpu.make_async_copy(qb.at[pl.ds(pl.multiple_of(x * 512, 512), 512)], qb_out, sem.at[4])
    )
    slot = lax.div(x + 1, 2)
    for n in range(2):
        low = pl.multiple_of((slot + 3 * n) * HEAD, HEAD)
        copies.append(
            pltpu.make_async_copy(kvb.at[pl.ds(low, HEAD)], kvb_out.at[n], sem.at[5 + n])
        )
    for copy in copies:
        copy.start()
    for ref, j, low, size in (
        (n0, 0, 0, 64),
        (n1, 1, 0, 64),
        (n2a, 2, 0, 32),
        (n2b, 2, 32, 32),
        (n3, 3, 0, 64),
    ):
        row = pl.multiple_of(lax.rem(x + j, 4) * 64 + low, 32)
        x_out[pl.ds(row, size), :] = ref[...]
    load_weights(own1, core, FIRST, w)
    load_weights(own2, core, LAST, w)
    load_weights(other1, 1 - core, FIRST, w)
    for copy in copies:
        copy.wait()


def rotate(v, cos, sin):
    a = v[:, :64]
    b = v[:, 64:]
    return jnp.concatenate([a * cos - b * sin, b * cos + a * sin], axis=1).astype(jnp.bfloat16)


def kv_project(w_in, other2, x_in, cs, kvb, w, kv):
    del w_in
    load_weights(other2, 1 - lax.axis_index("core"), LAST, w)
    acc = jnp.dot(
        x_in[...], w[:, :, :256].reshape(3584, 256), preferred_element_type=jnp.float32
    )
    kv[:, :HEAD] = rotate(acc[:, :HEAD] + kvb[0][None, :], cs[:, :64], cs[:, 64:])
    kv[:, HEAD:] = (acc[:, HEAD:] + kvb[1][None, :]).astype(jnp.bfloat16)


def q_project(w, x_in, cs, qb, q):
    for g in range(2):
        part = slice((g + 1) * 256, (g + 2) * 256)
        acc = jnp.dot(
            x_in[...], w[:, :, part].reshape(3584, 256), preferred_element_type=jnp.float32
        )
        for h in range(2):
            low = (2 * g + h) * HEAD
            head = acc[:, h * HEAD : (h + 1) * HEAD] + qb[low : low + HEAD][None, :]
            q[:, low : low + HEAD] = rotate(head, cs[:, :64], cs[:, 64:])


def one_head(qh, blocks, mask):
    parts = []
    for j, kv in enumerate(blocks):
        s = lax.dot_general(
            qh, kv[:, :HEAD], (((1,), (1,)), ((), ())), preferred_element_type=jnp.float32
        )
        parts.append(s * (HEAD**-0.5) + mask[:, j * ROW_TOK : (j + 1) * ROW_TOK])
    top = functools.reduce(jnp.maximum, [jnp.max(s, axis=1, keepdims=True) for s in parts])
    mass = jnp.zeros((ROW_TOK, 1), jnp.float32)
    acc = jnp.zeros((ROW_TOK, HEAD), jnp.float32)
    for s, kv in zip(parts, blocks):
        p = jnp.exp(s - top)
        mass += jnp.sum(p, axis=1, keepdims=True)
        acc += jnp.dot(p.astype(jnp.bfloat16), kv[:, HEAD:], preferred_element_type=jnp.float32)
    return (acc / mass).astype(jnp.bfloat16)


def attend_own(offsets, q, a0, a1, a2, a3, after, mask, last):
    y = lax.axis_index("y")
    e = 2 * lax.axis_index("z") + lax.axis_index("core")
    qi = lax.broadcasted_iota(jnp.int32, (ROW_TOK, ROW_TOK), 0)
    ki = lax.broadcasted_iota(jnp.int32, (ROW_TOK, ROW_TOK), 1)
    starts = [offsets[e, 4 * y + k] * 64 for k in range(4)]
    start = jnp.where(
        qi < 128,
        jnp.where(qi < 64, starts[0], starts[1]),
        jnp.where(qi < 192, starts[2], starts[3]),
    )
    for j in range(4):
        key = ki + lax.rem(y + j, 4) * ROW_TOK
        ok = (key >= start) & (key <= qi + y * ROW_TOK)
        mask[:, j * ROW_TOK : (j + 1) * ROW_TOK] = jnp.where(ok, 0.0, NEG)
    last[...] = one_head(q[:, 3 * HEAD :], [a[...] for a in (a0, a1, a2, a3)], mask)


def attend(mask, last, q, a0, a1, a2, a3, b0, b1, b2, b3, o0, o1, o2, o3, full):
    x = lax.axis_index("x")
    for h in range(3):
        left = (x == 1) if h == 2 else ((x == 1) | (x == 3))
        pick = jnp.where(left, 1, 0)
        blocks = [
            jnp.where(pick == 1, b[...], a[...])
            for a, b in ((a0, b0), (a1, b1), (a2, b2), (a3, b3))
        ]
        part = slice(h * HEAD, (h + 1) * HEAD)
        full[:, part] = one_head(q[:, part], blocks, mask)
    full[:, 3 * HEAD :] = last[...]
    for j, o in enumerate((o0, o1, o2, o3)):
        o[...] = full[pl.ds(pl.multiple_of(lax.rem(x + j, 4) * 64, 64), 64), :]


def cache_rows(a0, a2, a1, a3, after1, after2, t0, t1, t2, t3):
    x = lax.axis_index("x")
    y = lax.axis_index("y")
    i = lax.broadcasted_iota(jnp.int32, (64, ROW_TOK), 0)
    t = lax.broadcasted_iota(jnp.int32, (64, ROW_TOK), 1)
    want = 16 * lax.rem(i, 16) + 4 * y + lax.rem(x + lax.div(i, 16), 4)
    select = jnp.where(t == want, 1.0, 0.0).astype(jnp.bfloat16)
    for j, a in zip(HOPS, (a0, a2, a1, a3)):
        got = jnp.dot(select, a[...], preferred_element_type=jnp.float32).astype(jnp.bfloat16)
        rows = pl.ds(pl.multiple_of(lax.rem(y + j, 4) * 16, 16), 16)
        for k, out in enumerate((t0, t1, t2, t3)):
            out[rows, :] = got[16 * k : 16 * k + 16]


def cache_heads(t0, t2, t1, t3, out, buf):
    x = lax.axis_index("x")
    for j, t in zip(HOPS, (t0, t2, t1, t3)):
        buf[lax.rem(x + 4 - j, 4)] = t[...]
    for k, src in enumerate((0, 1, 3)):
        out[:, k * HEAD : (k + 1) * HEAD] = buf[src, :, :HEAD]
        out[:, (3 + k) * HEAD : (4 + k) * HEAD] = buf[src, :, HEAD:]


def cache_join(c0, c2, c3, c1, after, out):
    for n, c in enumerate((c0, c1, c2, c3)):
        out[n] = c[...]


def finish(plan, own, other, r0, r2, r1, r3, attended, cache):
    x = lax.axis_index("x")
    for j, r in zip(HOPS, (r0, r2, r1, r3)):
        low = pl.multiple_of(lax.rem(x + 4 - j, 4) * 512, 512)
        attended[:, pl.ds(low, 512)] = r[...]
    z = lax.axis_index("z")
    core = lax.axis_index("core")
    group = 2 * z + core
    for ref, t in ((own, core), (other, 1 - core)):
        for j in range(4):
            e = 2 * lax.rem(z + j, 4) + t
            rows = pl.ds(pl.multiple_of(e * 64, 64), 64)
            v = ref[j]
            cache[0, 0, rows, :] = jnp.where(plan[e, 0] == group, v, jnp.zeros_like(v))


def per_device(tokens, gain, q_weight, key_value_weight, q_bias, kv_bias, plan, home_offsets):
    bf = jnp.bfloat16
    f32 = jnp.float32
    blocks = call(
        cut,
        [((28, COLS), bf)] * 4,
        (q_weight, key_value_weight),
        [ANY] * 2,
        [
            pltpu.VMEM((28, 2048), bf),
            pltpu.VMEM((28, 768), bf),
            pltpu.SemaphoreType.DMA((2,)),
        ],
        grant=60,
    )
    (kept,) = call(keep, [((28, COLS), bf)], (blocks[0],), [ANY], [pltpu.SemaphoreType.DMA])
    got = [kept] + spread(lambda j: send(blocks[j], along_x(j)))
    (w0,) = call(place, [((112, COLS), bf)], got, scratch=[pltpu.VMEM((4, 28, COLS), f32)])
    (n0,) = call(norm, [((64, 3584), bf)], (tokens, gain, w0), [VM, VM, ANY])
    (s0,) = call(
        stage,
        [((4, 112, COLS), bf)],
        (w0, *spread(lambda j: send(w0, along_first(-j))), n0),
        [VM] * 4 + [ANY],
    )
    n1 = send(n0, along_x(-1))
    n3 = send(n0, along_x(1))
    s1 = send(s0, along_second(-1))
    s3 = send(s0, along_second(1))
    own1, r1, r3, low, high = call(
        relay,
        [((12, 112, COLS), bf)] + [((2, 112, COLS), bf)] * 2 + [((32, 3584), bf)] * 2,
        (n1, n3, s0, s1, s3),
    )
    n2a = send(low, along_x(-1))
    n2b = send(high, along_x(1))
    s2a = send(r1, along_second(-1))
    s2b = send(r3, along_second(1))
    other1 = send(own1, other_core)
    (own2,) = call(
        join2, [((4, 112, COLS), bf)], (n2a, n2b, s2a, s2b), [ANY] * 2 + [VM] * 2
    )
    other2 = send(own2, other_core)
    w, x_all, cs, qb, kvb = call(
        gather,
        [
            ((32, 112, COLS), bf),
            ((ROW_TOK, 3584), bf),
            ((ROW_TOK, HEAD), f32),
            ((512,), f32),
            ((2, HEAD), f32),
        ],
        (
            home_offsets, own1, own2, other1, n0, n1, n2a, n2b, n3,
            jnp.asarray(rotary_table()), q_bias, kv_bias,
        ),
        [SM] + [VM] * 8 + [ANY] * 3,
        [pltpu.SemaphoreType.DMA((7,))],
    )
    w, kv = call(
        kv_project,
        [((32, 112, COLS), bf), ((ROW_TOK, 256), bf)],
        (w, other2, x_all, cs, kvb),
        input_output_aliases={0: 0},
    )
    (q,) = call(q_project, [((ROW_TOK, 512), bf)], (w, x_all, cs, qb))

    a2, a1, a3 = spread(lambda j: send(kv, along_y(-j)))
    a = [kv, a1, a2, a3]
    b = [send(v, pair_x) for v in a]
    rows = call(cache_rows, [((64, 256), bf)] * 4, (kv, a2, a1, a3, q, b[0]), [VM] * 4 + [ANY] * 2)
    (mine,) = call(
        cache_heads,
        [((64, 768), bf)],
        (rows[0], *spread(lambda j: send(rows[j], along_x(j)))),
        scratch=[pltpu.VMEM((4, 64, 256), bf)],
    )
    mask, last = call(
        attend_own,
        [((ROW_TOK, 1024), f32), ((ROW_TOK, HEAD), bf)],
        (home_offsets, q, *a, mine),
        [SM] + [VM] * 5 + [ANY],
    )
    outs = call(
        attend,
        [((64, 512), bf)] * 4,
        (mask, last, q, *a, *b),
        scratch=[pltpu.VMEM((ROW_TOK, 512), bf)],
    )
    (cached,) = call(
        cache_join,
        [((4, 64, 768), bf)],
        (mine, *[send(mine, along_z(-j)) for j in (2, 3, 1)], outs[0]),
        [VM] * 4 + [ANY],
    )
    attended, cache = call(
        finish,
        [((64, 2048), bf), ((1, 1, 512, 768), bf)],
        (
            plan,
            cached,
            send(cached, other_core),
            outs[0],
            *spread(lambda j: send(outs[j], along_x(j))),
        ),
        [SM] + [VM] * 6,
    )
    return attended, cache


def solution(mesh):
    fine = Mesh(mesh.devices.reshape(SIZES), EVERY)
    in_specs = (P(EVERY, None), P(), P(EVERY, None), P(EVERY, None), P(), P(), P(), P())
    out_specs = (P(EVERY, None), P(("z", "core"), ("y", "x"), None, None))
    return jax.shard_map(
        per_device, mesh=fine, in_specs=in_specs, out_specs=out_specs, check_vma=False
    )
```

```python
import functools

import jax
import jax.numpy as jnp
import numpy as np
from jax import lax
from jax.experimental import pallas as pl
from jax.experimental.pallas import tpu as pltpu
from jax.sharding import Mesh
from jax.sharding import PartitionSpec as P

HEAD = 128
NEG = -1e30
ROW_TOK = 256
COLS = 768

EVERY = ("z", "core", "y", "x")
SIZES = (4, 2, 4, 4)
VM = pl.BlockSpec(memory_space=pltpu.VMEM)
SM = pl.BlockSpec(memory_space=pltpu.SMEM)
ANY = pl.BlockSpec(memory_space=pl.ANY)


def rotary_table():
    angles = np.arange(1024)[:, None] * 1000000.0 ** (-np.arange(64) * 2.0 / HEAD)[None, :]
    return np.concatenate([np.cos(angles), np.sin(angles)], axis=1).astype(np.float32)


def flat(z, c, y, x):
    return ((z % 4 * 2 + c % 2) * 4 + y % 4) * 4 + x % 4


PLACES = [(z, c, y, x) for z in range(4) for c in range(2) for y in range(4) for x in range(4)]


def send(v, move):
    return lax.ppermute(v, EVERY, [(flat(*p), flat(*move(*p))) for p in PLACES])


def spread(one):
    return [one(j) for j in (2, 1, 3)]


HOPS = (0, 2, 1, 3)


def along_x(j):
    return lambda z, c, y, x: (z, c, y, x + j)


def along_z(j):
    return lambda z, c, y, x: (z + j, c, y, x)


def along_first(j):
    return lambda z, c, y, x: (z + j, c, y, x) if c == 0 else (z, c, y + j, x)


def along_second(j):
    return lambda z, c, y, x: (z, c, y + j, x) if c == 0 else (z + j, c, y, x)


def other_core(z, c, y, x):
    return (z, 1 - c, y, x)


def along_y(j):
    return lambda z, c, y, x: (z, c, y + j, x)


def pair_x(z, c, y, x):
    return (z, c, y, x ^ 1)


def call(kernel, outs, operands, in_specs=None, scratch=(), grant=20, **more):
    outs = tuple(jax.ShapeDtypeStruct(s, d) for s, d in outs)
    return pl.pallas_call(
        kernel,
        out_shape=outs,
        in_specs=[VM] * len(operands) if in_specs is None else in_specs,
        out_specs=(VM,) * len(outs),
        scratch_shapes=list(scratch),
        compiler_params=pltpu.CompilerParams(vmem_limit_bytes=grant * 1024 * 1024),
        name=kernel.__name__,
        **more,
    )(*operands)


def cut(wq, wkv, b0, b1, b2, b3, q_buf, kv_buf, sem):
    copies = [
        pltpu.make_async_copy(wq, q_buf, sem.at[0]),
        pltpu.make_async_copy(wkv, kv_buf, sem.at[1]),
    ]
    for copy in copies:
        copy.start()
    for copy in copies:
        copy.wait()
    x = lax.axis_index("x")
    for j, block in enumerate((b0, b1, b2, b3)):
        to = lax.rem(x + j, 4)
        slot = lax.div(to + 1, 2)
        for n in range(2):
            low = pl.multiple_of((slot + 3 * n) * HEAD, HEAD)
            block[:, n * HEAD : (n + 1) * HEAD] = kv_buf[:, pl.ds(low, HEAD)]
        block[:, 256:] = q_buf[:, pl.ds(pl.multiple_of(to * 512, 512), 512)]


def norm(tokens, gain, after, out):
    floats = tokens[...].astype(jnp.float32)
    mean = jnp.mean(floats * floats, axis=1, keepdims=True)
    out[...] = (floats * lax.rsqrt(mean + 1e-06) * gain[...][None, :]).astype(jnp.bfloat16)


def keep(v, out, sem):
    copy = pltpu.make_async_copy(v, out, sem)
    copy.start()
    copy.wait()


def place(p0, p2, p1, p3, out, buf):
    x = lax.axis_index("x")
    for j, p in zip(HOPS, (p0, p2, p1, p3)):
        buf[lax.rem(x + 4 - j, 4)] = p[...].astype(jnp.float32)
    out[...] = jnp.concatenate([buf[k] for k in range(4)], axis=0).astype(jnp.bfloat16)


def stage(s0, s2, s3, s1, after, block):
    for i, s in enumerate((s0, s1, s2, s3)):
        block[i] = s[...]


def relay(n1, n3, s0, s1, s3, joined, r1, r3, low, high):
    for n, s in enumerate((s0, s1, s3)):
        joined[4 * n : 4 * n + 4] = s[...]
    r1[...] = s1[:2]
    r3[...] = s3[2:]
    low[...] = n1[:32, :]
    high[...] = n3[32:, :]


def join2(after1, after2, a, b, out):
    out[:2] = a[...]
    out[2:] = b[...]


def load_weights(ref, t, places, buf):
    y = lax.axis_index("y")
    z = lax.axis_index("z")
    for n, (j, i) in enumerate(places):
        zz = lax.rem(z + jnp.where(t == 0, i, j), 4)
        yy = lax.rem(y + jnp.where(t == 0, j, i), 4)
        buf[(2 * zz + t) * 4 + yy] = ref[n]


FIRST = [(j, i) for j in (0, 1, 3) for i in range(4)]
LAST = [(2, i) for i in range(4)]


def gather(
    offsets, own1, own2, other1, n0, n1, n2a, n2b, n3, table, qb, kvb, w, x_out, cs, qb_out, kvb_out, sem
):
    e = 2 * lax.axis_index("z") + lax.axis_index("core")
    y = lax.axis_index("y")
    x = lax.axis_index("x")
    core = lax.axis_index("core")
    copies = []
    for k in range(4):
        s = 4 * y + k
        row = pl.multiple_of((s - offsets[e, s]) * 64, 64)
        copies.append(
            pltpu.make_async_copy(
                table.at[pl.ds(row, 64), :], cs.at[k * 64 : (k + 1) * 64, :], sem.at[k]
            )
        )
    copies.append(
        pltpu.make_async_copy(qb.at[pl.ds(pl.multiple_of(x * 512, 512), 512)], qb_out, sem.at[4])
    )
    slot = lax.div(x + 1, 2)
    for n in range(2):
        low = pl.multiple_of((slot + 3 * n) * HEAD, HEAD)
        copies.append(
            pltpu.make_async_copy(kvb.at[pl.ds(low, HEAD)], kvb_out.at[n], sem.at[5 + n])
        )
    for copy in copies:
        copy.start()
    for ref, j, low, size in (
        (n0, 0, 0, 64),
        (n1, 1, 0, 64),
        (n2a, 2, 0, 32),
        (n2b, 2, 32, 32),
        (n3, 3, 0, 64),
    ):
        row = pl.multiple_of(lax.rem(x + j, 4) * 64 + low, 32)
        x_out[pl.ds(row, size), :] = ref[...]
    load_weights(own1, core, FIRST, w)
    load_weights(own2, core, LAST, w)
    load_weights(other1, 1 - core, FIRST, w)
    for copy in copies:
        copy.wait()


def rotate(v, cos, sin):
    a = v[:, :64]
    b = v[:, 64:]
    return jnp.concatenate([a * cos - b * sin, b * cos + a * sin], axis=1).astype(jnp.bfloat16)


def kv_project(w_in, other2, x_in, cs, kvb, w, kv):
    del w_in
    load_weights(other2, 1 - lax.axis_index("core"), LAST, w)
    acc = jnp.dot(
        x_in[...], w[:, :, :256].reshape(3584, 256), preferred_element_type=jnp.float32
    )
    kv[:, :HEAD] = rotate(acc[:, :HEAD] + kvb[0][None, :], cs[:, :64], cs[:, 64:])
    kv[:, HEAD:] = (acc[:, HEAD:] + kvb[1][None, :]).astype(jnp.bfloat16)


def q_project(w, x_in, cs, qb, q):
    for g in range(2):
        part = slice((g + 1) * 256, (g + 2) * 256)
        acc = jnp.dot(
            x_in[...], w[:, :, part].reshape(3584, 256), preferred_element_type=jnp.float32
        )
        for h in range(2):
            low = (2 * g + h) * HEAD
            head = acc[:, h * HEAD : (h + 1) * HEAD] + qb[low : low + HEAD][None, :]
            q[:, low : low + HEAD] = rotate(head, cs[:, :64], cs[:, 64:])


def one_head(qh, blocks, mask):
    parts = []
    for j, kv in enumerate(blocks):
        s = lax.dot_general(
            qh, kv[:, :HEAD], (((1,), (1,)), ((), ())), preferred_element_type=jnp.float32
        )
        parts.append(s * (HEAD**-0.5) + mask[:, j * ROW_TOK : (j + 1) * ROW_TOK])
    top = functools.reduce(jnp.maximum, [jnp.max(s, axis=1, keepdims=True) for s in parts])
    mass = jnp.zeros((ROW_TOK, 1), jnp.float32)
    acc = jnp.zeros((ROW_TOK, HEAD), jnp.float32)
    for s, kv in zip(parts, blocks):
        p = jnp.exp(s - top)
        mass += jnp.sum(p, axis=1, keepdims=True)
        acc += jnp.dot(p.astype(jnp.bfloat16), kv[:, HEAD:], preferred_element_type=jnp.float32)
    return (acc / mass).astype(jnp.bfloat16)


def attend_own(offsets, q, a0, a1, a2, a3, after, mask, last):
    y = lax.axis_index("y")
    e = 2 * lax.axis_index("z") + lax.axis_index("core")
    qi = lax.broadcasted_iota(jnp.int32, (ROW_TOK, ROW_TOK), 0)
    ki = lax.broadcasted_iota(jnp.int32, (ROW_TOK, ROW_TOK), 1)
    starts = [offsets[e, 4 * y + k] * 64 for k in range(4)]
    start = jnp.where(
        qi < 128,
        jnp.where(qi < 64, starts[0], starts[1]),
        jnp.where(qi < 192, starts[2], starts[3]),
    )
    for j in range(4):
        key = ki + lax.rem(y + j, 4) * ROW_TOK
        ok = (key >= start) & (key <= qi + y * ROW_TOK)
        mask[:, j * ROW_TOK : (j + 1) * ROW_TOK] = jnp.where(ok, 0.0, NEG)
    last[...] = one_head(q[:, 3 * HEAD :], [a[...] for a in (a0, a1, a2, a3)], mask)


def attend(mask, last, q, a0, a1, a2, a3, b0, b1, b2, b3, o0, o1, o2, o3, full):
    x = lax.axis_index("x")
    for h in range(3):
        left = (x == 1) if h == 2 else ((x == 1) | (x == 3))
        pick = jnp.where(left, 1, 0)
        blocks = [
            jnp.where(pick == 1, b[...], a[...])
            for a, b in ((a0, b0), (a1, b1), (a2, b2), (a3, b3))
        ]
        part = slice(h * HEAD, (h + 1) * HEAD)
        full[:, part] = one_head(q[:, part], blocks, mask)
    full[:, 3 * HEAD :] = last[...]
    for j, o in enumerate((o0, o1, o2, o3)):
        o[...] = full[pl.ds(pl.multiple_of(lax.rem(x + j, 4) * 64, 64), 64), :]


def cache_rows(a0, a2, a1, a3, after1, after2, t0, t1, t2, t3):
    x = lax.axis_index("x")
    y = lax.axis_index("y")
    i = lax.broadcasted_iota(jnp.int32, (64, ROW_TOK), 0)
    t = lax.broadcasted_iota(jnp.int32, (64, ROW_TOK), 1)
    want = 16 * lax.rem(i, 16) + 4 * y + lax.rem(x + lax.div(i, 16), 4)
    select = jnp.where(t == want, 1.0, 0.0).astype(jnp.bfloat16)
    for j, a in zip(HOPS, (a0, a2, a1, a3)):
        got = jnp.dot(select, a[...], preferred_element_type=jnp.float32).astype(jnp.bfloat16)
        rows = pl.ds(pl.multiple_of(lax.rem(y + j, 4) * 16, 16), 16)
        for k, out in enumerate((t0, t1, t2, t3)):
            out[rows, :] = got[16 * k : 16 * k + 16]


def cache_heads(t0, t2, t1, t3, out, buf):
    x = lax.axis_index("x")
    for j, t in zip(HOPS, (t0, t2, t1, t3)):
        buf[lax.rem(x + 4 - j, 4)] = t[...]
    for k, src in enumerate((0, 1, 3)):
        out[:, k * HEAD : (k + 1) * HEAD] = buf[src, :, :HEAD]
        out[:, (3 + k) * HEAD : (4 + k) * HEAD] = buf[src, :, HEAD:]


def cache_join(c0, c2, c3, c1, after, out):
    for n, c in enumerate((c0, c1, c2, c3)):
        out[n] = c[...]


def finish(plan, own, other, r0, r2, r1, r3, attended, cache):
    x = lax.axis_index("x")
    for j, r in zip(HOPS, (r0, r2, r1, r3)):
        low = pl.multiple_of(lax.rem(x + 4 - j, 4) * 512, 512)
        attended[:, pl.ds(low, 512)] = r[...]
    z = lax.axis_index("z")
    core = lax.axis_index("core")
    group = 2 * z + core
    for ref, t in ((own, core), (other, 1 - core)):
        for j in range(4):
            e = 2 * lax.rem(z + j, 4) + t
            rows = pl.ds(pl.multiple_of(e * 64, 64), 64)
            v = ref[j]
            cache[0, 0, rows, :] = jnp.where(plan[e, 0] == group, v, jnp.zeros_like(v))


def per_device(tokens, gain, q_weight, key_value_weight, q_bias, kv_bias, plan, home_offsets):
    bf = jnp.bfloat16
    f32 = jnp.float32
    blocks = call(
        cut,
        [((28, COLS), bf)] * 4,
        (q_weight, key_value_weight),
        [ANY] * 2,
        [
            pltpu.VMEM((28, 2048), bf),
            pltpu.VMEM((28, 768), bf),
            pltpu.SemaphoreType.DMA((2,)),
        ],
        grant=60,
    )
    (kept,) = call(keep, [((28, COLS), bf)], (blocks[0],), [ANY], [pltpu.SemaphoreType.DMA])
    got = [kept] + spread(lambda j: send(blocks[j], along_x(j)))
    (w0,) = call(place, [((112, COLS), bf)], got, scratch=[pltpu.VMEM((4, 28, COLS), f32)])
    (n0,) = call(norm, [((64, 3584), bf)], (tokens, gain, w0), [VM, VM, ANY])
    (s0,) = call(
        stage,
        [((4, 112, COLS), bf)],
        (w0, *[send(w0, along_first(-j)) for j in (2, 3, 1)], n0),
        [VM] * 4 + [ANY],
    )
    n1 = send(n0, along_x(-1))
    n3 = send(n0, along_x(1))
    s1 = send(s0, along_second(-1))
    s3 = send(s0, along_second(1))
    own1, r1, r3, low, high = call(
        relay,
        [((12, 112, COLS), bf)] + [((2, 112, COLS), bf)] * 2 + [((32, 3584), bf)] * 2,
        (n1, n3, s0, s1, s3),
    )
    n2a = send(low, along_x(-1))
    n2b = send(high, along_x(1))
    s2a = send(r1, along_second(-1))
    s2b = send(r3, along_second(1))
    other1 = send(own1, other_core)
    (own2,) = call(
        join2, [((4, 112, COLS), bf)], (n2a, n2b, s2a, s2b), [ANY] * 2 + [VM] * 2
    )
    other2 = send(own2, other_core)
    w, x_all, cs, qb, kvb = call(
        gather,
        [
            ((32, 112, COLS), bf),
            ((ROW_TOK, 3584), bf),
            ((ROW_TOK, HEAD), f32),
            ((512,), f32),
            ((2, HEAD), f32),
        ],
        (
            home_offsets, own1, own2, other1, n0, n1, n2a, n2b, n3,
            jnp.asarray(rotary_table()), q_bias, kv_bias,
        ),
        [SM] + [VM] * 8 + [ANY] * 3,
        [pltpu.SemaphoreType.DMA((7,))],
    )
    w, kv = call(
        kv_project,
        [((32, 112, COLS), bf), ((ROW_TOK, 256), bf)],
        (w, other2, x_all, cs, kvb),
        input_output_aliases={0: 0},
    )
    (q,) = call(q_project, [((ROW_TOK, 512), bf)], (w, x_all, cs, qb))

    a2, a1, a3 = spread(lambda j: send(kv, along_y(-j)))
    a = [kv, a1, a2, a3]
    b = [send(v, pair_x) for v in a]
    rows = call(cache_rows, [((64, 256), bf)] * 4, (kv, a2, a1, a3, q, b[0]), [VM] * 4 + [ANY] * 2)
    (mine,) = call(
        cache_heads,
        [((64, 768), bf)],
        (rows[0], *spread(lambda j: send(rows[j], along_x(j)))),
        scratch=[pltpu.VMEM((4, 64, 256), bf)],
    )
    mask, last = call(
        attend_own,
        [((ROW_TOK, 1024), f32), ((ROW_TOK, HEAD), bf)],
        (home_offsets, q, *a, mine),
        [SM] + [VM] * 5 + [ANY],
    )
    outs = call(
        attend,
        [((64, 512), bf)] * 4,
        (mask, last, q, *a, *b),
        scratch=[pltpu.VMEM((ROW_TOK, 512), bf)],
    )
    (cached,) = call(
        cache_join,
        [((4, 64, 768), bf)],
        (mine, *[send(mine, along_z(-j)) for j in (2, 3, 1)], outs[0]),
        [VM] * 4 + [ANY],
    )
    attended, cache = call(
        finish,
        [((64, 2048), bf), ((1, 1, 512, 768), bf)],
        (
            plan,
            cached,
            send(cached, other_core),
            outs[0],
            *spread(lambda j: send(outs[j], along_x(j))),
        ),
        [SM] + [VM] * 6,
    )
    return attended, cache


def solution(mesh):
    fine = Mesh(mesh.devices.reshape(SIZES), EVERY)
    in_specs = (P(EVERY, None), P(), P(EVERY, None), P(EVERY, None), P(), P(), P(), P())
    out_specs = (P(EVERY, None), P(("z", "core"), ("y", "x"), None, None))
    return jax.shard_map(
        per_device, mesh=fine, in_specs=in_specs, out_specs=out_specs, check_vma=False
    )
```
